32 devices in a mesh: wide: 8 (over z, y), narrow: 4 (over x, core).
Axes of the slice: x: 2, y: 2, z: 4, core: 2. Of those that a mesh axis runs over, the one named last changes fastest.
Arguments:
- images: bfloat16 [704, 16, 16, 256], P(('wide', 'narrow')), may hold values from -6 to 6
- time_embed: bfloat16 [704, 512], P(('wide', 'narrow')), may hold values from -6 to 6
- out_cotangent: bfloat16 [704, 16, 16, 256], P(('wide', 'narrow')), may hold values from -6 to 6
- conv_master: float32 [2, 9, 256, 256], P(None, None, ('wide', 'narrow')), may hold values from -0.125 to 0.125
- dense_master: float32 [512, 256], P(('wide', 'narrow')), may hold values from -0.25 to 0.25
- attn_master: float32 [4, 256, 256], P(None, ('wide', 'narrow'))
- vector_master: float32 [12, 256], P(None, ('wide', 'narrow'))
- vector_first: float32 [12, 256], P(None, ('wide', 'narrow'))
- vector_second: float32 [12, 256], P(None, ('wide', 'narrow')), as said below
- owners: int32 [23], replicated, may hold values from 0 to 31, as said below
- slot_first: float32 [32, 512, 256], P(('wide', 'narrow'))
- slot_second: float32 [32, 512, 256], P(('wide', 'narrow')), as said below
- slot_left_basis: float32 [32, 512, 512], P(('wide', 'narrow')), as said below
- slot_right_basis: float32 [32, 256, 256], P(('wide', 'narrow')), as said below
- slot_left_stat: float32 [32, 512, 512], P(('wide', 'narrow')), as said below
- slot_right_stat: float32 [32, 256, 256], P(('wide', 'narrow')), as said below
Outputs:
- activations: bfloat16 [704, 16, 16, 256], P(('wide', 'narrow'))
- image_grad: float32 [704, 16, 16, 256], P(('wide', 'narrow'))
- time_grad: float32 [704, 512], P(('wide', 'narrow'))
- conv_new: float32 [2, 9, 256, 256], P(None, None, ('wide', 'narrow'))
- dense_new: float32 [512, 256], P(('wide', 'narrow'))
- attn_new: float32 [4, 256, 256], P(None, ('wide', 'narrow'))
- vector_new: float32 [12, 256], P(None, ('wide', 'narrow'))
- conv_copy: bfloat16 [2, 9, 256, 256], P(None, None, ('wide', 'narrow'))
- dense_copy: bfloat16 [512, 256], P(('wide', 'narrow'))
- attn_copy: bfloat16 [4, 256, 256], P(None, ('wide', 'narrow'))
- vector_copy: bfloat16 [12, 256], P(None, ('wide', 'narrow'))
- vector_first_new: float32 [12, 256], P(None, ('wide', 'narrow'))
- vector_second_new: float32 [12, 256], P(None, ('wide', 'narrow'))
- slot_first_new: float32 [32, 512, 256], P(('wide', 'narrow'))
- slot_second_new: float32 [32, 512, 256], P(('wide', 'narrow'))
- left_basis_new: float32 [32, 512, 512], P(('wide', 'narrow'))
- right_basis_new: float32 [32, 256, 256], P(('wide', 'narrow'))
- left_stat_new: float32 [32, 512, 512], P(('wide', 'narrow'))
- right_stat_new: float32 [32, 256, 256], P(('wide', 'narrow'))
The draws below stay inside these ranges and needn't reach their ends.
Inputs may be any that keep to these rules, and one draw needn't show every extreme that they name: `owners`: Twenty-three different device numbers, counted over wide and narrow together with wide the slower. `slot_left_basis`: in each slot the leading block is orthogonal, of order 512 in the slot of the time projection's owner and 256 elsewhere; the rest is zero. `slot_right_basis`: each slot is orthogonal. `slot_left_stat`: in each slot the leading block (of the same order as the basis) is symmetric with a positive, strictly dominant diagonal; the rest is zero. `slot_right_stat`: each slot is symmetric with a positive, strictly dominant diagonal. `slot_second`: every entry is positive. `vector_second`: every entry is positive.
All inputs are finite; a program needn't handle non-finite values.
Results may differ from the reference program's by a relative error of at most 0.018.
The reference program's roundings to bfloat16 on the way count: a program that leaves them out, or rounds other values in their place, can miss the bound.
Values may be sent and summed in bfloat16 or wider, within the bound.
A program may use at most 576 MiB of HBM per device.

```python
import math
import jax
import jax.numpy as jnp
from jax import lax

C = 256
TEMB = 512
GROUPS = 32
SIDE = 16
IMG_DEV = 22
STEP = 10
IMAGES = 704
N_WIDE = 8
N_NARROW = 4


def owner_list(key):
    return jax.random.permutation(key, N_WIDE * N_NARROW)[:23].astype(jnp.int32)


def grad_size():
    return 0.3 * math.sqrt(IMAGES * SIDE * SIDE)


def vector_size():
    return 0.7 * math.sqrt(IMAGES * SIDE * SIDE)


def signed_law(key, shape, level):
    sign_key, size_key = jax.random.split(key)
    signs = jnp.where(jax.random.bernoulli(sign_key, 0.5, shape), 1.0, -1.0)
    return level * signs * jnp.exp(jax.random.uniform(size_key, shape, jnp.float32, math.log(0.5), math.log(2.0)))


def positive_law(key, shape, level):
    return level * jnp.exp(jax.random.uniform(key, shape, jnp.float32, 0.0, math.log(4.0)))


def attn_law(key):
    scales = jnp.array([1.5, 1.5, 1.0, 4.0], jnp.float32) * C ** (-0.5)
    return jax.random.normal(key, (4, C, C), jnp.float32) * scales[:, None, None]


def vector_law(key):
    gain_key, shift_key = jax.random.split(key)
    gains = 1.0 + 0.3 * jax.random.uniform(gain_key, (3, C), jnp.float32, -1.0, 1.0)
    shifts = 0.3 * jax.random.normal(shift_key, (9, C), jnp.float32)
    return jnp.concatenate([gains, shifts], axis=0)


def permutations(key, count, width):
    return jax.vmap(lambda part_key: jax.random.permutation(part_key, width))(jax.random.split(key, count))


def basis_law(key, orders, width):
    count = orders.shape[0]
    keys = jax.random.split(key, 5)
    index = jnp.arange(width)
    clipped = jnp.minimum(index, C - 1)
    is_big = (orders == width)[:, None]
    samples = jnp.where(is_big, permutations(keys[0], count, width), permutations(keys[1], count, C)[:, clipped])
    freqs = jnp.where(is_big, permutations(keys[2], count, width), permutations(keys[3], count, C)[:, clipped])
    signs = jnp.where(jax.random.bernoulli(keys[4], 0.5, (count, 1, width)), 1.0, -1.0)
    order_int = orders[:, None, None]
    phase = (2 * samples[:, :, None] + 1) * freqs[:, None, :] % (4 * order_int)
    order_float = order_int.astype(jnp.float32)
    weight = jnp.sqrt(jnp.where(freqs[:, None, :] == 0, 1.0, 2.0) / order_float)
    value = weight * jnp.cos(math.pi * phase.astype(jnp.float32) / (2.0 * order_float)) * signs
    inside = (index[None, :, None] < order_int) & (index[None, None, :] < order_int)
    return jnp.where(inside, value, 0.0)


def stat_law(key, orders, width):
    level = 8.0 * C * grad_size() ** 2
    diag_key, rough_key = jax.random.split(key)
    count = orders.shape[0]
    index = jnp.arange(width)
    diagonal = positive_law(diag_key, (count, width), level)
    rough = jax.random.uniform(rough_key, (count, width, width), jnp.float32, -1.0, 1.0)
    rough = (rough + jnp.swapaxes(rough, 1, 2)) * 0.4 * level / orders.astype(jnp.float32)[:, None, None]
    value = jnp.where((index[:, None] == index[None, :])[None], diagonal[:, :, None], rough)
    order_int = orders[:, None, None]
    inside = (index[None, :, None] < order_int) & (index[None, None, :] < order_int)
    return jnp.where(inside, value, 0.0)


def draw_owners(key, part):
    return owner_list(key)


def draw_attn_master(key, part):
    key = jax.random.fold_in(key, 11)
    return attn_law(key)


def draw_vector_master(key, part):
    key = jax.random.fold_in(key, 13)
    return vector_law(key)


def draw_vector_first(key, part):
    key = jax.random.fold_in(key, 15)
    return signed_law(key, (12, C), grad_size())


def draw_vector_second(key, part):
    key = jax.random.fold_in(key, 16)
    return positive_law(key, (12, C), vector_size() ** 2)


def draw_slot_first(key, part):
    key = jax.random.fold_in(key, 17)
    return signed_law(key, (N_WIDE * N_NARROW, TEMB, C), grad_size())


def draw_slot_second(key, part):
    key = jax.random.fold_in(key, 18)
    return positive_law(key, (N_WIDE * N_NARROW, TEMB, C), grad_size() ** 2)


def draw_slot_left_basis(key, part):
    dense_slot = owner_list(key)[9]
    key = jax.random.fold_in(key, 19)
    orders = jnp.where(jnp.arange(N_WIDE * N_NARROW) == dense_slot, TEMB, C).astype(jnp.int32)
    return basis_law(key, orders, TEMB)


def draw_slot_right_basis(key, part):
    key = jax.random.fold_in(key, 20)
    orders = jnp.full((N_WIDE * N_NARROW,), C, jnp.int32)
    return basis_law(key, orders, C)


def draw_slot_left_stat(key, part):
    dense_slot = owner_list(key)[9]
    key = jax.random.fold_in(key, 21)
    orders = jnp.where(jnp.arange(N_WIDE * N_NARROW) == dense_slot, TEMB, C).astype(jnp.int32)
    return stat_law(key, orders, TEMB)


def draw_slot_right_stat(key, part):
    key = jax.random.fold_in(key, 22)
    orders = jnp.full((N_WIDE * N_NARROW,), C, jnp.int32)
    return stat_law(key, orders, C)


def block_scale(own_key, extent, cuts, low, largest):
    level, own = 1.0, jax.random.fold_in(own_key, 6)
    for dim, shards_of in cuts:
        draws = jnp.exp(jax.random.uniform(jax.random.fold_in(own, dim), (shards_of,), jnp.float32, low / len(cuts), largest / len(cuts)))
        level = level * jnp.repeat(draws, extent[dim] // shards_of).reshape([-1 if axis == dim else 1 for axis in range(len(extent))])
    return level


def centred(stream_key, dims, deviation, reach, cuts=(), held_as=jnp.bfloat16):
    factor_of = block_scale(stream_key, dims, cuts, -0.22, 0.18) if cuts else 1.0
    values = jax.random.normal(stream_key, dims, jnp.float32) * deviation * factor_of
    return jnp.minimum(jnp.maximum(values, -reach), reach).astype(held_as)


def setup_inputs(seed: int = 0) -> dict:
    key_of = jax.random.split(jax.random.key(seed), 17)
    images = centred(key_of[0], (IMAGES, SIDE, SIDE, C), 1.0, 6.0, ((0, 32),))
    time_embed = centred(key_of[1], (IMAGES, TEMB), 1.0, 6.0, ((0, 32),))
    out_cotangent = centred(key_of[2], (IMAGES, SIDE, SIDE, C), 1.0, 6.0, ((0, 32),))
    conv_master = centred(key_of[3], (2, 9, C, C), (9 * C) ** -0.5, 0.125, ((2, 32),), jnp.float32)
    dense_master = centred(key_of[4], (TEMB, C), TEMB ** -0.5, 0.25, ((0, 32),), jnp.float32)
    attn_master = draw_attn_master(jax.random.fold_in(key_of[16], 71), 0)
    vector_master = draw_vector_master(jax.random.fold_in(key_of[16], 71), 0)
    vector_first = draw_vector_first(jax.random.fold_in(key_of[16], 71), 0)
    vector_second = draw_vector_second(jax.random.fold_in(key_of[16], 71), 0)
    owners = draw_owners(jax.random.fold_in(key_of[16], 71), 0)
    slot_first = draw_slot_first(jax.random.fold_in(key_of[16], 71), 0)
    slot_second = draw_slot_second(jax.random.fold_in(key_of[16], 71), 0)
    slot_left_basis = draw_slot_left_basis(jax.random.fold_in(key_of[16], 71), 0)
    slot_right_basis = draw_slot_right_basis(jax.random.fold_in(key_of[16], 71), 0)
    slot_left_stat = draw_slot_left_stat(jax.random.fold_in(key_of[16], 71), 0)
    slot_right_stat = draw_slot_right_stat(jax.random.fold_in(key_of[16], 71), 0)
    return {"images": images, "time_embed": time_embed, "out_cotangent": out_cotangent, "conv_master": conv_master, "dense_master": dense_master, "attn_master": attn_master, "vector_master": vector_master, "vector_first": vector_first, "vector_second": vector_second, "owners": owners, "slot_first": slot_first, "slot_second": slot_second, "slot_left_basis": slot_left_basis, "slot_right_basis": slot_right_basis, "slot_left_stat": slot_left_stat, "slot_right_stat": slot_right_stat}


@jax.custom_vjp
def reduced_precision(v):
    return lax.optimization_barrier(v.astype(jnp.bfloat16)).astype(jnp.float32)

@jax.custom_vjp
def reduced_backward(v):
    return v

def low_keep(v):
    return (reduced_precision(v), None)

def low_pass(kept, grad):
    return (grad,)

def back_keep(v):
    return (v, None)

def back_low(kept, grad):
    return (reduced_precision(grad),)
reduced_precision.defvjp(low_keep, low_pass)
reduced_backward.defvjp(back_keep, back_low)
half_root = 0.5 ** 0.5
norm_eps = 1e-06
adam_eps = 1e-08
highest_precision = lax.Precision.HIGHEST

def swish_act(value):
    return value * jax.nn.sigmoid(value)

def group_norm(feature, gain, shift):
    image_count = feature.shape[0]
    grouped = feature.reshape(image_count, -1, GROUPS, feature.shape[-1] // GROUPS)
    center = lax.optimization_barrier(jnp.mean(grouped, axis=(1, 3), keepdims=True))
    spread = lax.optimization_barrier(jnp.mean(jnp.square(grouped - center), axis=(1, 3), keepdims=True))
    normal_form = ((grouped - center) * lax.rsqrt(spread + norm_eps)).reshape(feature.shape)
    return normal_form * gain + shift

def patches(image):
    side_cells = image.shape[1]
    padded = jnp.pad(image, ((0, 0), (1, 1), (1, 1), (0, 0)))
    return jnp.concatenate([padded[:, offset_y:offset_y + side_cells, offset_x:offset_x + side_cells, :] for offset_y in range(3) for offset_x in range(3)], axis=-1)

def conv_apply(image, kernel):
    flat_kernel = kernel.reshape(-1, kernel.shape[-1])
    return jnp.einsum('bhwk,kc->bhwc', patches(image), flat_kernel, precision=highest_precision)

def forward(params, images, embed):
    conv_all, dense_all, attn_all, vector_all = params
    conv_low = reduced_precision(conv_all)
    dense_low = reduced_precision(dense_all)
    attn_low = reduced_precision(attn_all)
    vectors = reduced_precision(vector_all)
    image_count, side_cells, channel_count = (images.shape[0], images.shape[1], images.shape[3])
    first_act = reduced_precision(swish_act(group_norm(images, vectors[0], vectors[3])))
    embed_act = reduced_precision(swish_act(embed))
    projected = reduced_backward(jnp.dot(embed_act, dense_low, precision=highest_precision) + vectors[7])
    first_conv = reduced_backward(conv_apply(first_act, conv_low[0]) + vectors[6] + projected[:, None, None, :])
    second_act = reduced_precision(swish_act(group_norm(first_conv, vectors[1], vectors[4])))
    second_conv = reduced_backward(conv_apply(second_act, conv_low[1]) + vectors[8])
    middle = (images + second_conv) * half_root
    normed = reduced_precision(group_norm(middle, vectors[2], vectors[5])).reshape(image_count, side_cells * side_cells, channel_count)
    query_rows = reduced_backward(reduced_precision(jnp.einsum('bpc,cd->bpd', normed, attn_low[0], precision=highest_precision) + vectors[9]))
    key_matrix_rows = reduced_backward(reduced_precision(jnp.einsum('bpc,cd->bpd', normed, attn_low[1], precision=highest_precision)))
    value_matrix_rows = reduced_backward(reduced_precision(jnp.einsum('bpc,cd->bpd', normed, attn_low[2], precision=highest_precision) + vectors[10]))
    attention_scores = reduced_backward(jnp.einsum('inf,ilf->inl', query_rows, key_matrix_rows, precision=highest_precision) * channel_count ** (-0.5))
    attention_map = reduced_precision(jax.nn.softmax(attention_scores, axis=-1))
    mixed_values = reduced_backward(reduced_precision(jnp.einsum('mfn,mni->mfi', attention_map, value_matrix_rows, precision=highest_precision)))
    branch = reduced_backward(jnp.einsum('bpc,cd->bpd', mixed_values, attn_low[3], precision=highest_precision) + vectors[11])
    return (middle + branch.reshape(middle.shape)) * half_root

def orthonormal(matrix):
    gram_matrix = jnp.dot(matrix.T, matrix, precision=highest_precision)
    factor = jnp.linalg.cholesky(gram_matrix)
    return jax.scipy.linalg.solve_triangular(factor, matrix.T, lower=True).T

def soap_step(gradient, first, second, left_basis, right_basis, left_stat, right_stat):
    inner = jnp.einsum('ji,tjk->tik', left_basis, gradient, precision=highest_precision)
    turned = jnp.einsum('tik,kl->til', inner, right_basis, precision=highest_precision)
    moment = 0.5 * first + 0.5 * turned
    second_new = 0.5 * second + 0.5 * turned * turned
    correction = 1.0 - 0.5 ** STEP
    direction = moment / correction / (jnp.sqrt(second_new / correction) + adam_eps)
    outer = jnp.einsum('ij,tjk->tik', left_basis, direction, precision=highest_precision)
    update = jnp.einsum('tik,lk->til', outer, right_basis, precision=highest_precision)
    left_stat_new = 0.95 * left_stat + 0.05 * jnp.einsum('tik,tjk->ij', gradient, gradient, precision=highest_precision)
    right_stat_new = 0.95 * right_stat + 0.05 * jnp.einsum('tki,tkj->ij', gradient, gradient, precision=highest_precision)
    left_new = orthonormal(jnp.dot(left_stat_new, left_basis, precision=highest_precision))
    right_new = orthonormal(jnp.dot(right_stat_new, right_basis, precision=highest_precision))
    return (moment, second_new, update, left_new, right_new, left_stat_new, right_stat_new)

def reference(images, time_embed, out_cotangent, conv_master, dense_master, attn_master, vector_master, vector_first, vector_second, owners, slot_first, slot_second, slot_left_basis, slot_right_basis, slot_left_stat, slot_right_stat):
    params = (conv_master, dense_master, attn_master, vector_master)
    group_total = images.shape[0] // IMG_DEV

    def one_group(totals, inputs):
        image_group, embed_group, cot_group = inputs
        output, pull = jax.vjp(forward, params, image_group.astype(jnp.float32), embed_group.astype(jnp.float32))
        grad_params, grad_images, grad_embed = pull(cot_group.astype(jnp.float32))
        totals = jax.tree.map(jnp.add, totals, grad_params)
        return (totals, (output.astype(jnp.bfloat16), grad_images, grad_embed))
    zero_grads = jax.tree.map(jnp.zeros_like, params)
    grouped = (images.reshape((group_total, IMG_DEV) + images.shape[1:]), time_embed.reshape((group_total, IMG_DEV) + time_embed.shape[1:]), out_cotangent.reshape((group_total, IMG_DEV) + out_cotangent.shape[1:]))
    grads, (outputs, image_grads, embed_grads) = lax.scan(one_group, zero_grads, grouped)
    activations = outputs.reshape(images.shape)
    image_grad = image_grads.reshape(images.shape)
    time_grad = embed_grads.reshape(time_embed.shape)
    grad_conv, grad_dense, grad_attn, grad_vector = grads
    matrices = [grad_conv[0, tap] for tap in range(9)] + [grad_dense] + [grad_conv[1, tap] for tap in range(9)] + [grad_attn[index] for index in range(4)]
    first_out = jnp.zeros_like(slot_first)
    second_out = jnp.zeros_like(slot_second)
    left_out = jnp.zeros_like(slot_left_basis)
    right_out = jnp.zeros_like(slot_right_basis)
    left_stat_out = jnp.zeros_like(slot_left_stat)
    right_stat_out = jnp.zeros_like(slot_right_stat)
    updates = []
    for number in range(23):
        gradient = matrices[number][None]
        side_order = gradient.shape[1]
        owner_slot = owners[number]
        results = soap_step(gradient, slot_first[owner_slot, :side_order][None], slot_second[owner_slot, :side_order][None], slot_left_basis[owner_slot, :side_order, :side_order], slot_right_basis[owner_slot], slot_left_stat[owner_slot, :side_order, :side_order], slot_right_stat[owner_slot])
        moment, second_new, update, left_new, right_new, left_stat_new, right_stat_new = results
        first_out = first_out.at[owner_slot, :side_order].set(moment[0])
        second_out = second_out.at[owner_slot, :side_order].set(second_new[0])
        left_out = left_out.at[owner_slot, :side_order, :side_order].set(left_new)
        right_out = right_out.at[owner_slot].set(right_new)
        left_stat_out = left_stat_out.at[owner_slot, :side_order, :side_order].set(left_stat_new)
        right_stat_out = right_stat_out.at[owner_slot].set(right_stat_new)
        updates.append(update[0])
    conv_update = jnp.stack([jnp.stack(updates[0:9]), jnp.stack(updates[10:19])])
    attn_update = jnp.stack(updates[19:23])
    conv_new = conv_master - (9 * C) ** (-0.5) * (conv_update + 0.01 * conv_master)
    dense_new = dense_master - TEMB ** (-0.5) * (updates[9] + 0.01 * dense_master)
    attn_new = attn_master - C ** (-0.5) * (attn_update + 0.01 * attn_master)
    correction = 1.0 - 0.5 ** STEP
    vector_first_new = 0.5 * vector_first + 0.5 * grad_vector
    vector_second_new = 0.5 * vector_second + 0.5 * grad_vector * grad_vector
    vector_new = vector_master - 0.2 * (vector_first_new / correction) / (jnp.sqrt(vector_second_new / correction) + adam_eps)
    return (activations, image_grad, time_grad, conv_new, dense_new, attn_new, vector_new, conv_new.astype(jnp.bfloat16), dense_new.astype(jnp.bfloat16), attn_new.astype(jnp.bfloat16), vector_new.astype(jnp.bfloat16), vector_first_new, vector_second_new, first_out, second_out, left_out, right_out, left_stat_out, right_stat_out)
```

```python
import functools

import jax
import jax.numpy as jnp
from jax import lax
from jax.experimental import pallas as pl
from jax.experimental.pallas import tpu as pltpu
from jax.sharding import PartitionSpec as P

BF = jnp.bfloat16
F32 = jnp.float32
STEP = 10
GROUP = 8
BLK = 128
half_root = 0.5**0.5
norm_eps = 1e-6
adam_eps = 1e-8
HI = lax.Precision.HIGHEST
MESH = pl.DeviceIdType.MESH
AXES = ("wide", "narrow")
MATS = 22
VMEM = pl.BlockSpec(memory_space=pltpu.VMEM)
SMEM = pl.BlockSpec(memory_space=pltpu.SMEM)
ANY = pl.BlockSpec(memory_space=pl.ANY)
LIMIT = 56 << 20

def mm(a,b):
    return lax.dot_general(a,b,(((1,),(0,)),((),())),preferred_element_type=F32)
def mm_nt(a,b):
    return lax.dot_general(a,b,(((1,),(1,)),((),())),preferred_element_type=F32)
def mm_tn(a,b):
    return lax.dot_general(a,b,(((0,),(0,)),((),())),preferred_element_type=F32)

def group_sum(v):
    lane=lax.broadcasted_iota(jnp.int32, v.shape, 1)
    n=v.shape[1]
    for s in (1,2,4):
        v=v+jnp.where((lane & s)==0, pltpu.roll(v,n-s,1), pltpu.roll(v,s,1))
    return v

def col_sum(v):
    return jnp.sum(v,axis=0,keepdims=True)

def pad8(v):
    return jnp.broadcast_to(v,(8,v.shape[1]))

def group_mean(colsum, count):
    return group_sum(pad8(colsum))[0:1]*(1.0/count)

def normal_form(v):
    count=v.shape[0]*GROUP
    m=group_mean(col_sum(v),count)
    c=v-m
    var=group_mean(col_sum(c*c),count)
    r=lax.rsqrt(var+norm_eps)
    return c*r, r

def norm_back(grad, xhat, r, gain):
    count=grad.shape[0]*GROUP
    shift_grad=col_sum(grad)
    gain_grad=col_sum(grad*xhat)
    m1=group_mean(shift_grad*gain,count)
    m2=group_mean(gain_grad*gain,count)
    return (grad*(gain*r)-(m1*r)-xhat*(m2*r)), gain_grad, shift_grad

def sigmoid(y):
    return pl.reciprocal(1.0+jnp.exp(-y),approx=True)

def spread(ref, i, v, side):
    tokens, c = v.shape
    x=lax.broadcasted_iota(jnp.int32,(tokens,1),0) & (side-1)
    before=jnp.where(x==0,0.0,pltpu.roll(v,1,0)).astype(BF)
    after=jnp.where(x==side-1,0.0,pltpu.roll(v,tokens-1,0)).astype(BF)
    ref[i,side:side+tokens,0:c]=before
    ref[i,side:side+tokens,c:2*c]=v.astype(BF)
    ref[i,side:side+tokens,2*c:3*c]=after

def taps(ref, count, dy, tokens, side):
    return jnp.concatenate([ref[i,side*dy:side*dy+tokens,:] for i in range(count)],axis=0)

def train_body(side, owners_ref, img_ref, cot_ref, emb_ref, w_ref,
         act_ref, igrad_ref, tgrad_ref, gw_ref, gvec_ref, inv_ref,
         dense_ref, vec_ref, wt, acc, gvec, proj, pgrad, p1, p2, s2, s1):
    step=pl.program_id(0); steps=pl.num_programs(0)
    ib,tokens,c=img_ref.shape
    batch=emb_ref.shape[0]
    scale=c**-0.5

    @pl.when(step==0)
    def _():
        acc[...]=jnp.zeros_like(acc)
        gvec[...]=jnp.zeros_like(gvec)
        pgrad[...]=jnp.zeros_like(pgrad)
        for ref in (p1,p2,s2,s1):
            for i in range(ib):
                z=jnp.zeros((side,3*c),BF)
                ref[i,0:side,:]=z
                ref[i,side+tokens:2*side+tokens,:]=z
        for k in range(2):
            for t in range(9):
                wt[k, 8-t]=w_ref[9*k+t].T
        chips=c//16
        total=jnp.zeros((16,c),F32)
        for o in range(chips):
            total=total+w_ref[24,16*o:16*o+16].astype(F32)
            for h in range(2):
                dense_ref[32*o+16*h:32*o+16*h+16]=w_ref[22+h,16*o:16*o+16]
        vec_ref[...]=total
        for d in range(inv_ref.shape[0]):
            inv_ref[d]=-1
        for m in range(owners_ref.shape[0]):
            inv_ref[owners_ref[m]]=m if m<9 else MATS if m==9 else m-1
        e=emb_ref[...].astype(F32)
        proj[0:batch]=mm((e*sigmoid(e)).astype(BF),dense_ref[...])+total[7:8]

    vec=vec_ref[...]
    row=lambda k: vec[k:k+1]

    def conv(ref, weight):
        out=None
        for dy in range(3):
            w=weight(dy)
            part=mm(taps(ref,ib,dy,tokens,side), w)
            out=part if out is None else out+part
        return out
    cat=lambda parts: jnp.concatenate(parts,axis=0)

    xs=[img_ref[i].astype(F32) for i in range(ib)]
    n0=[];
    for i in range(ib):
        h,r=normal_form(xs[i]); n0.append((h,r))
        y=h*row(0)+row(3)
        spread(p1,i,y*sigmoid(y),side)
    c1=conv(p1, lambda dy: jnp.concatenate([w_ref[3*dy+dx] for dx in range(3)],axis=0))
    n1=[]
    for i in range(ib):
        v=c1[i*tokens:(i+1)*tokens]+(row(6)+proj[pl.ds(step*ib+i,1),:])
        h,r=normal_form(v); n1.append((h,r))
        y=h*row(1)+row(4)
        spread(p2,i,y*sigmoid(y),side)
    c2=conv(p2, lambda dy: jnp.concatenate([w_ref[9+3*dy+dx] for dx in range(3)],axis=0))
    mids=[(xs[i]+(c2[i*tokens:(i+1)*tokens]+row(8)))*half_root for i in range(ib)]
    n2=[normal_form(m) for m in mids]
    normed=cat([(h*row(2)+row(5)).astype(BF) for h,r in n2])
    q=(mm(normed,w_ref[18])+row(9)).astype(BF)
    k=mm(normed,w_ref[19]).astype(BF)
    v=(mm(normed,w_ref[20])+row(10)).astype(BF)
    att=[]; mixed=[]
    for i in range(ib):
        sl=slice(i*tokens,(i+1)*tokens)
        sc=mm_nt(q[sl],k[sl])*scale
        e=jnp.exp(sc-jnp.max(sc,axis=1,keepdims=True))
        a=e/jnp.sum(e,axis=1,keepdims=True)
        att.append(a)
        mixed.append(mm(a.astype(BF),v[sl]).astype(BF))
    mixed=cat(mixed)
    branch=mm(mixed,w_ref[21])+row(11)
    cots=[cot_ref[i].astype(F32)*half_root for i in range(ib)]
    for i in range(ib):
        act_ref[i]=((mids[i]+branch[i*tokens:(i+1)*tokens])*half_root).astype(BF)
    bg=cat([g.astype(BF) for g in cots])
    acc[21]+=mm_tn(mixed,bg)
    mg=mm_nt(bg,w_ref[21]).astype(BF)
    qg=[];kg=[];vg=[]
    for i in range(ib):
        sl=slice(i*tokens,(i+1)*tokens)
        pg=mm_nt(mg[sl],v[sl])
        a=att[i]
        vg.append(mm_tn(a.astype(BF),mg[sl]).astype(BF))
        sg=(a*(pg-jnp.sum(a*pg,axis=1,keepdims=True))).astype(BF)
        qg.append((mm(sg,k[sl])*scale).astype(BF))
        kg.append((mm_tn(sg,q[sl])*scale).astype(BF))
    qg,kg,vg=cat(qg),cat(kg),cat(vg)
    normed_t=normed.T
    acc[18]+=mm(normed_t,qg)
    acc[19]+=mm(normed_t,kg)
    acc[20]+=mm(normed_t,vg)
    ng=mm_nt(qg,w_ref[18])+mm_nt(kg,w_ref[19])+mm_nt(vg,w_ref[20])
    up=lambda t: t.astype(F32)
    sums={9:col_sum(up(qg)),10:col_sum(up(vg)),11:col_sum(up(bg))}
    def add(kk,val):
        sums[kk]=val if kk not in sums else sums[kk]+val
    midg=[]
    for i in range(ib):
        h,r=n2[i]
        d,gg,gs=norm_back(ng[i*tokens:(i+1)*tokens],h,r,row(2))
        add(2,gg);add(5,gs)
        m=cots[i]+d
        midg.append(m)
        g=(m*half_root).astype(BF).astype(F32)
        add(8,col_sum(g))
        spread(s2,i,g,side)
    def wgrad(base, aref, gref):
        at=cat([aref[i,side:side+tokens,c:2*c] for i in range(ib)]).T
        for dy in range(3):
            g=mm(at,taps(gref,ib,dy,tokens,side))
            for dx in range(3):
                acc[base+8-(3*dy+dx)]+=g[:,dx*c:(dx+1)*c]
    wgrad(9,p2,s2)
    def back_conv(ref,kk):
        return conv(ref, lambda dy: jnp.concatenate([wt[kk,3*dy+dx] for dx in range(3)],axis=0))
    ag=back_conv(s2,1)
    def swish_back(grad,h,gain,shift):
        y=h*gain+shift
        s=sigmoid(y)
        return grad*(s*(1.0+y*(1.0-s)))
    for i in range(ib):
        h,r=n1[i]
        d=swish_back(ag[i*tokens:(i+1)*tokens],h,row(1),row(4))
        d,gg,gs=norm_back(d,h,r,row(1))
        add(1,gg);add(4,gs)
        g=d.astype(BF).astype(F32)
        s=col_sum(g)
        add(6,s)
        pg=s.astype(BF).astype(F32)
        pgrad[pl.ds(step*ib+i,1),:]=pg
        add(7,pg)
        spread(s1,i,g,side)
    wgrad(0,p1,s1)
    ag=back_conv(s1,0)
    for i in range(ib):
        h,r=n0[i]
        d=swish_back(ag[i*tokens:(i+1)*tokens],h,row(0),row(3))
        d,gg,gs=norm_back(d,h,r,row(0))
        add(0,gg);add(3,gs)
        igrad_ref[i]=midg[i]*half_root+d
    gvec[0:12]+=jnp.concatenate([sums[j] for j in range(12)],axis=0)

    @pl.when(step==steps-1)
    def _():
        for m in range(acc.shape[0]):
            gw_ref[m]=acc[m].astype(BF)
        gvec_ref[...]=gvec[...]
        e=emb_ref[...].astype(F32)
        s=sigmoid(e)
        ea=(e*s).astype(BF)
        pg=pgrad[0:batch].astype(BF)
        tgrad_ref[...]=mm_nt(pg,dense_ref[...])*(s*(1.0+e*(1.0-s)))
        gd=mm_tn(ea,pg).astype(BF)
        for o in range(c//16):
            for h in range(2):
                gw_ref[22+h,16*o:16*o+16]=gd[32*o+16*h:32*o+16*h+16]

def train_images(owners,images,cot,embed,w,side,ndev):
    batch,tokens,c=images.shape
    emb=embed.shape[1]
    ib=2 if batch%2==0 else 1
    rows=-(-batch//8)*8
    whole=lambda a: pl.BlockSpec(a.shape,lambda s: (0,)*len(a.shape))
    blk=pl.BlockSpec((ib,tokens,c),lambda s:(s,0,0))
    sd=jax.ShapeDtypeStruct
    outs=[sd((batch,tokens,c),BF),sd((batch,tokens,c),F32),sd((batch,emb),F32),sd((MATS+2,c,c),BF),sd((16,c),F32)]
    return pl.pallas_call(functools.partial(train_body,side),grid=(batch//ib,),
        in_specs=[SMEM,blk,blk,whole(embed),whole(w)],
        out_specs=[blk,blk]+[whole(o) for o in outs[2:]]+[SMEM],
        out_shape=outs+[sd((ndev,),jnp.int32)],
        scratch_shapes=[pltpu.VMEM((emb,c),BF),pltpu.VMEM((16,c),F32),pltpu.VMEM((2,9,c,c),BF),pltpu.VMEM((MATS,c,c),F32),pltpu.VMEM((16,c),F32),pltpu.VMEM((rows,c),F32),pltpu.VMEM((rows,c),F32)]
          +[pltpu.VMEM((ib,tokens+2*side,3*c),BF)]*4,
        compiler_params=pltpu.CompilerParams(vmem_limit_bytes=LIMIT),
        name="train_images")(owners,images,cot,embed,w)

def fdot(a,b,ca,cb):
    return lax.dot_general(a,b,(((ca,),(cb,)),((),())),precision=HI,preferred_element_type=F32)
nn=lambda a,b: fdot(a,b,1,0)
nt=lambda a,b: fdot(a,b,1,1)
tn=lambda a,b: fdot(a,b,0,0)

def inverse_factors(blocks):
    n=BLK
    lane=lax.broadcasted_iota(jnp.int32,(8,n),1)
    sub=lax.broadcasted_iota(jnp.int32,(8,n),0)
    tables=[[b[8*v:8*v+8] for v in range(n//8)] for b in blocks]
    over_lanes=lambda t,j: jnp.broadcast_to(t[:,j:j+1],(8,n))
    over_rows=lambda t,i: jnp.broadcast_to(t[i:i+1],(8,n))
    for J in range(n//8):
        lo=8*J
        in_block=(lane>=lo)&(lane<lo+8)
        for t in tables:
            cur=t[J]
            cols=[over_lanes(cur,lo+j) for j in range(8)]
            m=[[over_rows(cols[j],i) for j in range(i+1)] for i in range(8)]
            R=[jnp.where(in_block,jnp.where(lane==lo+i,1.0,0.0),over_rows(cur,i)) for i in range(8)]
            r=[None]*8
            l=[[None]*8 for _ in range(8)]
            for k in range(8):
                d=m[k][k]
                r[k]=pl.reciprocal(d,approx=True)
                for i in range(k+1,8):
                    l[i][k]=m[i][k]*r[k]
                for i in range(k+1,8):
                    for j in range(k+1,i+1):
                        m[i][j]=m[i][j]-l[i][k]*m[j][k]
                    R[i]=R[i]-l[i][k]*R[k]
            P=[None]*8
            for k in range(7,-1,-1):
                P[k]=R[k]*r[k]
                for i in range(7,k,-1):
                    P[k]=P[k]-l[i][k]*P[i]
            done=R[0]*lax.rsqrt(m[0][0])
            for i in range(1,8):
                done=jnp.where(sub==i,R[i]*lax.rsqrt(m[i][i]),done)
            t[J]=jnp.where(lane<=lo+sub,done,0.0)
            for v in range(J+1,n//8):
                new=jnp.where(in_block,0.0,t[v])
                for k in range(8):
                    new=new-over_lanes(t[v],lo+k)*P[k]
                t[v]=new
    return [jnp.concatenate(t,axis=0) for t in tables]

def at(k,size):
    return pl.ds(pl.multiple_of(k*size,size),size)

def split(x):
    hi=x.astype(BF)
    return hi,(x-hi.astype(F32)).astype(BF)

def bdot(a,b,ca,cb):
    return lax.dot_general(a,b,(((ca,),(cb,)),((),())),preferred_element_type=F32)

def dot3(a,b,ca,cb):
    (ah,al),(bh,bl)=split(a),split(b)
    return bdot(ah,bh,ca,cb)+(bdot(ah,bl,ca,cb)+bdot(al,bh,ca,cb))

def dot2(a,b,ca,cb):
    ah,al=split(a)
    return bdot(ah,b,ca,cb)+bdot(al,b,ca,cb)

def factor_both(a_l, g_l, a_r, g_r):
    for p in range(g_l.shape[0]//BLK):
        lo,hi=p*BLK,(p+1)*BLK
        live=[(a,g) for a,g in ((a_l,g_l),(a_r,g_r)) if g.shape[0]>lo]
        invs=inverse_factors([g[lo:hi,lo:hi] for _,g in live])
        for (a,g),inv in zip(live,invs):
            q=dot3(a[:,lo:hi],inv,1,1)
            if hi<g.shape[0]:
                r=nn(inv,g[lo:hi,hi:])
                g[hi:,hi:]=g[hi:,hi:]-tn(r,r)
                a[:,hi:]=a[:,hi:]-dot3(q,r,1,0)
            a[:,lo:hi]=q

def soap(nb, grad, ins, outs, update, g_l, g_r):
    (first,second,left,right,lstat,rstat)=ins
    first_o,second_o,left_o,right_o,lstat_o,rstat_o=outs
    c=right.shape[0]
    big=left.shape[0]
    g=grad[...]
    L=left[...]; Rb=right[...]
    ls=0.95*lstat[...]+0.05*bdot(g,g,1,1)
    rs=0.95*rstat[...]+0.05*bdot(g,g,0,0)
    lstat_o[...]=ls; rstat_o[...]=rs
    ar=nn(rs,Rb)
    right_o[...]=ar
    g_r[...]=tn(ar,ar)
    al=nn(ls,L)
    left_o[...]=al
    unit=(lax.broadcasted_iota(jnp.int32,(big,big),0)==lax.broadcasted_iota(jnp.int32,(big,big),1))&(lax.broadcasted_iota(jnp.int32,(big,big),0)>=nb*c)
    g_l[...]=tn(al,al)+jnp.where(unit,1.0,0.0)
    corr=1.0-0.5**STEP
    turned=dot3(dot2(L,g,0,0),Rb,1,0)
    inside=lax.broadcasted_iota(jnp.int32,(big,c),0)<nb*c
    moment=jnp.where(inside,0.5*first[...]+0.5*turned,0.0)
    sec=jnp.where(inside,0.5*second[...]+0.5*turned*turned,0.0)
    first_o[...]=moment; second_o[...]=sec
    direction=moment/corr/(jnp.sqrt(sec/corr)+adam_eps)
    update[...]=dot3(dot3(L,direction,1,0),Rb,1,1)
    factor_both(left_o,g_l,right_o,g_r)

def owner_body(inv_ref, q_ref, *refs):
    ins_hbm=refs[0:6]; outs_hbm=refs[6:12]; send_o=refs[12]
    ins=refs[13:19]; outs=refs[19:25]
    grad,update,g_l,g_r,in_sem,out_sem=refs[25:]
    me=lax.axis_index("wide")*lax.axis_size("narrow")+lax.axis_index("narrow")
    held=inv_ref[me]
    kind=jnp.where(held<0,0,jnp.where(held==MATS,2,1))
    c=ins[3].shape[1]; big=ins[2].shape[1]
    copies_in=[pltpu.make_async_copy(h.at[0],v,in_sem.at[i]) for i,(h,v) in enumerate(zip(ins_hbm,ins))]
    copies_out=[pltpu.make_async_copy(v,h.at[0],out_sem.at[i]) for i,(h,v) in enumerate(zip(outs_hbm,outs))]
    for cp in copies_in: cp.start()
    @pl.when(kind==1)
    def _():
        grad[...]=jnp.zeros_like(grad)
        for i in range(big//32):
            grad[16*i:16*i+16]=q_ref[32*i:32*i+16]
    @pl.when(kind==2)
    def _():
        grad[...]=q_ref[...]
    for cp in copies_in: cp.wait()
    ndev=send_o.shape[0]
    @pl.when(kind==0)
    def _():
        for o in outs: o[...]=jnp.zeros_like(o)
        send_o[...]=jnp.zeros_like(send_o)
    @pl.when(kind>0)
    def _():
        soap(kind,grad,ins,outs,update,g_l,g_r)
    for size,number in ((c,1),(big,2)):
        @pl.when(kind==number)
        def _():
            r=size//ndev
            for d in range(ndev):
                u=update[r*d:r*d+r]
                if r<16: u=jnp.concatenate([u,jnp.zeros((16-r,c),F32)],axis=0)
                send_o[d]=u.astype(BF)
    for cp in copies_out: cp.start()
    for cp in copies_out: cp.wait()

def owner_step(inv,q,first,second,left,right,lstat,rstat,ndev):
    c=right.shape[1]; big=left.shape[1]
    slots=(first,second,left,right,lstat,rstat)
    sd=lambda a: jax.ShapeDtypeStruct(a.shape,F32)
    vm=pl.BlockSpec(memory_space=pltpu.VMEM); hb=pl.BlockSpec(memory_space=pl.ANY)
    buf=lambda a: pltpu.VMEM(a.shape[1:],F32)
    return pl.pallas_call(owner_body,
        in_specs=[pl.BlockSpec(memory_space=pltpu.SMEM),vm]+[hb]*6,
        out_specs=[hb]*6+[vm],
        out_shape=[sd(a) for a in slots]+[jax.ShapeDtypeStruct((ndev,16,c),BF)],
        scratch_shapes=[buf(a) for a in slots]*2+[pltpu.VMEM((big,c),BF),pltpu.VMEM((big,c),F32)]+[pltpu.VMEM((big,big),F32),pltpu.VMEM((c,c),F32),
          pltpu.SemaphoreType.DMA((6,)),pltpu.SemaphoreType.DMA((6,))],
        compiler_params=pltpu.CompilerParams(vmem_limit_bytes=LIMIT),
        name="owner_step")(inv,q,*slots)

def place():
    w,n=lax.axis_index("wide"),lax.axis_index("narrow")
    return lax.div(w,2),lax.rem(w,2),lax.div(n,2),lax.rem(n,2)

def device(z,y,x,core):
    return (z*2+y,x*2+core)

def chip_of(z,y,x):
    return (z*2+y)*2+x

def greet(partners):
    barrier=pltpu.get_barrier_semaphore()
    count=0
    for dev,cond in partners:
        if cond is None:
            pl.semaphore_signal(barrier,inc=1,device_id=dev,device_id_type=MESH)
            count=count+1
        else:
            @pl.when(cond)
            def _():
                pl.semaphore_signal(barrier,inc=1,device_id=dev,device_id_type=MESH)
            count=count+jnp.where(cond,1,0)
    pl.semaphore_wait(barrier,count)

def remote(src,dst,send,recv,dev):
    return pltpu.make_async_remote_copy(src_ref=src,dst_ref=dst,send_sem=send,recv_sem=recv,device_id=dev,device_id_type=MESH)

GATHER=MATS+4
SHARE=GATHER//2
CUT=(SHARE+1)//2

def gather_body(depth, conv_ref, dense_ref, attn_ref, vec_ref, w_ref, part, vbuf,
                pair_s, pair_r, own_r, twin_r, up_s, down_s, x_s, y_s, twin_s):
    z,y,x,core=place()
    me=chip_of(z,y,x)
    rank=me*2+core
    twin=device(z,y,x,1-core)
    greet([(twin,None),(device(z,y,1-x,core),None),(device(z,1-y,x,core),None),
           (device(z-1,y,x,core),z>0),(device(z+1,y,x,core),z<depth-1)])
    conv=conv_ref.shape[0]
    part[0,0:conv]=conv_ref[...]
    part[0,conv:MATS]=attn_ref[...]
    part[0,MATS]=dense_ref[0:8]
    part[0,MATS+1]=dense_ref[8:16]
    vbuf[...]=jnp.zeros_like(vbuf)
    vbuf[0:vec_ref.shape[0],0:vec_ref.shape[1]]=vec_ref[...]
    mine=pltpu.roll(vbuf[...],rank*vec_ref.shape[1],1)
    part[0,MATS+2]=mine[0:8]
    part[0,MATS+3]=mine[8:16]
    swap=remote(part.at[0],part.at[1],pair_s,pair_r,twin)
    swap.start()
    rows=lambda o: pl.ds(pl.multiple_of(o*16,16),16)
    swap.wait()
    even,odd=core,1-core
    for m in range(MATS):
        w_ref[m,rows(me)]=jnp.concatenate([part[even,m],part[odd,m]],axis=0).astype(BF)
    for h,src in ((0,even),(1,odd)):
        w_ref[MATS+h,rows(me)]=jnp.concatenate([part[src,MATS],part[src,MATS+1]],axis=0).astype(BF)
    w_ref[MATS+2,rows(me)]=jnp.concatenate([part[0,MATS+2]+part[1,MATS+2],part[0,MATS+3]+part[1,MATS+3]],axis=0).astype(BF)
    w_ref[MATS+3,rows(me)]=jnp.zeros((16,w_ref.shape[2]),BF)

    def block(h,o,whose=core):
        return w_ref.at[pl.ds(SHARE*whose+(0,CUT)[h],(CUT,SHARE-CUT)[h]),rows(o)]
    def copy(h,o,send,recv,dev):
        return remote(block(h,o),block(h,o),send,recv.at[h,o],dev)
    def arrived(h,o):
        copy(h,o,pair_s,own_r,twin).wait_recv()
    side_x,side_y=device(z,y,1-x,core),device(z,1-y,x,core)
    to_x=lambda h,o: copy(h,o,x_s.at[h,o],own_r,side_x)
    to_y=lambda h,o: copy(h,o,y_s.at[h,o],own_r,side_y)
    to_twin=lambda h,o: copy(h,o,twin_s.at[h,o],twin_r,twin)
    to_up=lambda h,o: copy(h,o,up_s.at[h,o],own_r,device(z+1,y,x,core))
    to_down=lambda h,o: copy(h,o,down_s.at[h,o],own_r,device(z-1,y,x,core))

    def line(zz,wait,up,down):
        o=chip_of(zz,y,x)
        for h in range(2):
            if wait: arrived(h,o)
            if up:
                @pl.when(z<depth-1)
                def _(): to_up(h,o).start()
            if down:
                @pl.when(z>0)
                def _(): to_down(h,o).start()
            first,second=((to_x,to_y),(to_y,to_x))[h]
            first(h,o).start()
            second(h,o).start()
            if wait: to_twin(h,o).start()
    def sides(zz):
        o=chip_of(zz,y,1-x)
        arrived(0,o); to_y(0,o).start(); to_twin(0,o).start()
        o=chip_of(zz,1-y,x)
        arrived(1,o); to_x(1,o).start(); to_twin(1,o).start()
    def both(d,run):
        for zz,up in ((z-d,True),(z+d,False)):
            @pl.when((zz>=0)&(zz<depth))
            def _(): run(zz,up)
    line(z,False,True,True)
    for d in range(1,depth+1):
        if d<depth:
            both(d,lambda zz,up: line(zz,True,up,not up))
        if d==1: sides(z)
        else: both(d-1,lambda zz,up: sides(zz))
    @pl.loop(0,depth)
    def _(zz):
        for a in range(2):
            o=chip_of(zz,1-y,a)
            arrived(0,o); to_twin(0,o).start()
            o=chip_of(zz,a,1-x)
            arrived(1,o); to_twin(1,o).start()
    @pl.loop(1,depth*4)
    def _(k):
        o=lax.rem(me+k,depth*4)
        for h in range(2):
            remote(block(h,o,1-core),block(h,o,1-core),pair_s,twin_r.at[h,o],twin).wait_recv()
            to_twin(h,o).wait_send()
    @pl.loop(0,depth)
    def _(zz):
        o=chip_of(zz,y,x)
        for h in range(2):
            to_x(h,o).wait_send(); to_y(h,o).wait_send()
            @pl.when((z<depth-1)&(zz<=z))
            def _(): to_up(h,o).wait_send()
            @pl.when((z>0)&(zz>=z))
            def _(): to_down(h,o).wait_send()
        to_y(0,chip_of(zz,y,1-x)).wait_send()
        to_x(1,chip_of(zz,1-y,x)).wait_send()

def gather_weights(conv,dense,attn,vec,depth):
    c=conv.shape[2]
    chips=depth*4
    dma=pltpu.SemaphoreType.DMA
    return pl.pallas_call(functools.partial(gather_body,depth),
        out_shape=jax.ShapeDtypeStruct((GATHER,c,c),BF),
        in_specs=[VMEM]*4,out_specs=VMEM,
        scratch_shapes=[pltpu.VMEM((2,GATHER,8,c),F32),pltpu.VMEM((16,c),F32),dma,dma]+[dma((2,chips))]*7,
        compiler_params=pltpu.CompilerParams(collective_id=0,has_side_effects=True,vmem_limit_bytes=LIMIT),
        name="gather_weights")(conv,dense,attn,vec)

REDUCE=MATS+2
HALF=REDUCE//2
PARTS=((0,5,"xyz"),(5,4,"yzx"),(9,3,"zxy"))

def reduce_body(depth, inv_ref, g_ref, v_ref, q_ref, vec_o, acc, core_in, bx0, by0, up0, down0, bx1, by1, up1, down1, bx2, by2, up2, down2,
                final, pick, vsend, vrecv, core_s, core_r, ex_s, ex_r, up_s, up_r, down_s, down_r, twin_s, twin_r, out_s, out_r, v_s, v_r):
    z,y,x,core=place()
    me=chip_of(z,y,x)
    chips=depth*4
    twin=device(z,y,x,1-core)
    def of_chip(o):
        return device(lax.div(o,4),lax.rem(lax.div(o,2),2),lax.rem(o,2),core)
    others=[lax.rem(me+k,chips) for k in range(1,chips)]
    greet([(twin,None)]+[(of_chip(o),None) for o in others])
    c=g_ref.shape[2]
    pair=[]
    for i,(m0,n,_) in enumerate(PARTS):
        cp=remote(g_ref.at[pl.ds(HALF*(1-core)+m0,n)],core_in.at[m0:m0+n],core_s.at[i],core_r.at[i],twin)
        cp.start(); pair.append(cp)
    def vec_start(stage,dev):
        cp=remote(vsend.at[stage],vrecv.at[stage],v_s.at[stage],v_r.at[stage],dev)
        cp.start()
        return cp
    def vec_end(stage,cp):
        cp.wait()
        total=vsend[stage]+vrecv[stage]
        if stage<4: vsend[stage+1]=total
        else: vec_o[...]=total
    vsend[0]=v_ref[...]
    vcp=vec_start(0,twin)
    nbr_x,nbr_y=device(z,y,1-x,core),device(z,1-y,x,core)
    bufs=((bx0,by0,up0,down0),(bx1,by1,up1,down1),(bx2,by2,up2,down2))
    started={}
    def where(i,done):
        return ["z" in done and z, "y" in done and y, "x" in done and x]
    def index(m,place):
        return tuple([m]+[slice(None) if p is False else p for p in place])
    def swap_start(i,stage):
        m0,n,order=PARTS[i]
        axis=order[stage]
        at=where(i,order[:stage])
        at["zyx".index(axis)]=1-(x if axis=="x" else y)
        dst=bufs[i][0 if axis=="x" else 1]
        k=0 if axis=="x" else 1
        cp=remote(acc.at[index(slice(m0,m0+n),at)],dst,ex_s.at[i,k],ex_r.at[i,k],nbr_x if axis=="x" else nbr_y)
        cp.start()
        started[i,stage]=cp
    def swap_end(i,stage):
        m0,n,order=PARTS[i]
        axis=order[stage]
        started.pop((i,stage)).wait()
        at=where(i,order[:stage+1])
        src=bufs[i][0 if axis=="x" else 1]
        @pl.loop(0,n)
        def _(m):
            there=index(m0+m,at)
            acc[there]=(acc[there].astype(F32)+src[m].astype(F32)).astype(BF)
    def z_line(i,stage):
        m0,n,order=PARTS[i]
        at=where(i,order[:stage])
        up,down=bufs[i][2:]
        def view(zz):
            a=list(at); a[0]=zz
            return index(slice(m0,m0+n),a)
        def add(buf,zz):
            a=list(at); a[0]=zz
            @pl.loop(0,n)
            def _(m):
                there=index(m0+m,a)
                acc[there]=(acc[there].astype(F32)+buf[zz,m].astype(F32)).astype(BF)
        def to_up(zz): return remote(acc.at[view(zz)],up.at[zz],up_s.at[i,zz],up_r.at[i,zz],device(z+1,y,x,core))
        def to_down(zz): return remote(acc.at[view(zz)],down.at[zz],down_s.at[i,zz],down_r.at[i,zz],device(z-1,y,x,core))
        for k in range(depth-1):
            top,low=depth-1-k,k
            @pl.when(z<top)
            def _():
                @pl.when(z>0)
                def _():
                    to_up(top).wait_recv(); add(up,top)
                to_up(top).start()
            @pl.when(z>low)
            def _():
                @pl.when(z<depth-1)
                def _():
                    to_down(low).wait_recv(); add(down,low)
                to_down(low).start()
        @pl.when(z>0)
        def _():
            to_up(z).wait_recv(); add(up,z)
        @pl.when(z<depth-1)
        def _():
            to_down(z).wait_recv(); add(down,z)
        for k in range(depth-1):
            top,low=depth-1-k,k
            @pl.when(z<top)
            def _(): to_up(top).wait_send()
            @pl.when(z>low)
            def _(): to_down(low).wait_send()

    def add_pair(i):
        m0,n,_=PARTS[i]
        pair[i].wait()
        @pl.loop(0,n)
        def _(m):
            s=(g_ref[HALF*core+m0+m].astype(F32)+core_in[m0+m].astype(F32)).astype(BF)
            acc[m0+m]=s.reshape(acc.shape[1:])
    add_pair(0); swap_start(0,0)
    add_pair(1); swap_start(1,0)
    add_pair(2)
    vec_end(0,vcp); vcp=vec_start(1,nbr_x)
    z_line(2,0)
    vec_end(1,vcp); vcp=vec_start(2,nbr_y)
    swap_end(0,0); swap_start(0,1)
    swap_start(2,1)
    swap_end(1,0)
    z_line(1,1)
    vec_end(2,vcp); vcp=vec_start(3,device(lax.div(z,2)*2+(1-lax.rem(z,2)),y,x,core))
    swap_start(1,2)
    swap_end(2,1); swap_start(2,2)
    swap_end(0,1)
    z_line(0,2)
    vec_end(3,vcp); vcp=vec_start(4,device(lax.rem(z+2,4),y,x,core))
    swap_end(1,2)
    swap_end(2,2)
    there=pl.ds(HALF*core,HALF)
    for m in range(HALF):
        final[HALF*core+m]=acc[m,z,y,x]
    cp=remote(final.at[there],final.at[there],twin_s,twin_r,twin)
    cp.start(); cp.wait()
    for k in range(chips):
        o=me if k==0 else others[k-1]
        m=jnp.maximum(inv_ref[o*2+core],0)
        pick[k,0]=final[m]
        pick[k,1]=final[REDUCE-1]
        if k:
            remote(pick.at[k],q_ref.at[me],out_s.at[k],out_r.at[me],of_chip(o)).start()
    q_ref[me]=pick[0]
    vec_end(4,vcp)
    for k in range(1,chips):
        o=others[k-1]
        remote(pick.at[k],q_ref.at[o],out_s.at[k],out_r.at[o],of_chip(o)).wait()

def reduce_grads(inv,grads,vec,depth):
    c=grads.shape[2]
    chips=depth*4
    dma=pltpu.SemaphoreType.DMA
    vm=lambda *s: pltpu.VMEM(s,BF)
    bufs=[]
    for _,n,order in PARTS:
        left={"z":depth,"y":2,"x":2}
        shapes={}
        for axis in order:
            del left[axis]
            shapes[axis]=tuple(left[k] for k in "zyx" if k in left)
        bufs+=[vm(n,*shapes["x"],16,c),vm(n,*shapes["y"],16,c),vm(depth,n,*shapes["z"],16,c),vm(depth,n,*shapes["z"],16,c)]
    return pl.pallas_call(functools.partial(reduce_body,depth),
        out_shape=[jax.ShapeDtypeStruct((chips,2,16,c),BF),jax.ShapeDtypeStruct(vec.shape,F32)],
        in_specs=[SMEM,VMEM,VMEM],out_specs=[VMEM,VMEM],
        scratch_shapes=[vm(HALF,depth,2,2,16,c),vm(HALF,c,c)]+bufs+[vm(REDUCE,16,c),vm(chips,2,16,c),
          pltpu.VMEM((5,)+vec.shape,F32),pltpu.VMEM((5,)+vec.shape,F32),
          dma((3,)),dma((3,)),dma((3,2)),dma((3,2)),dma((3,depth)),dma((3,depth)),dma((3,depth)),dma((3,depth)),dma,dma,
          dma((chips,)),dma((chips,)),dma((5,)),dma((5,))],
        compiler_params=pltpu.CompilerParams(collective_id=1,has_side_effects=True,vmem_limit_bytes=LIMIT),
        name="reduce_grads")(inv,grads,vec)

def deal_body(ndev, send_ref, out_ref, s_sem, r_sem):
    w,n=lax.axis_index("wide"),lax.axis_index("narrow")
    width=lax.axis_size("narrow")
    me=w*width+n
    dev=lambda d: (lax.div(d,width),lax.rem(d,width))
    others=[lax.rem(me+k,ndev) for k in range(1,ndev)]
    greet([(dev(d),None) for d in others])
    def copy(k):
        d=others[k]
        return remote(send_ref.at[d],out_ref.at[me],s_sem.at[k],r_sem.at[me],dev(d))
    for k in range(ndev-1): copy(k).start()
    out_ref[me]=send_ref[me]
    for k in range(ndev-1):
        d=others[k]
        remote(send_ref.at[d],out_ref.at[d],s_sem.at[k],r_sem.at[d],dev(d)).wait()

def deal_updates(send):
    ndev=send.shape[0]
    dma=pltpu.SemaphoreType.DMA
    return pl.pallas_call(functools.partial(deal_body,ndev),
        out_shape=jax.ShapeDtypeStruct(send.shape,send.dtype),
        in_specs=[VMEM],out_specs=VMEM,
        scratch_shapes=[dma((ndev,)),dma((ndev,))],
        compiler_params=pltpu.CompilerParams(collective_id=2,has_side_effects=True,vmem_limit_bytes=LIMIT),
        name="deal_updates")(send)

def weights_body(owners_ref, upd_ref, conv_ref, dense_ref, attn_ref, vm_ref, v1_ref, v2_ref, gv_ref,
                 conv_o, dense_o, attn_o, vec_o, convc_o, densec_o, attnc_o, vecc_o, v1_o, v2_o):
    me=lax.axis_index("wide")*lax.axis_size("narrow")+lax.axis_index("narrow")
    c=dense_ref.shape[1]
    def new(master,number,fan):
        u=upd_ref[owners_ref[number]].astype(F32)[0:master.shape[0]]
        return master-fan**-0.5*(u+0.01*master)
    for k in range(conv_ref.shape[0]):
        v=new(conv_ref[k],k+(k>=9),9*c)
        conv_o[k]=v; convc_o[k]=v.astype(BF)
    v=new(dense_ref[...],9,dense_ref.shape[0]*lax.axis_size("wide")*lax.axis_size("narrow"))
    dense_o[...]=v; densec_o[...]=v.astype(BF)
    for k in range(4):
        v=new(attn_ref[k],19+k,c)
        attn_o[k]=v; attnc_o[k]=v.astype(BF)
    rows,cols=vm_ref.shape
    g=pltpu.roll(gv_ref[...],lax.rem(c-me*cols,c),1)[0:rows,0:cols]
    corr=1.0-0.5**STEP
    f=0.5*v1_ref[...]+0.5*g
    s=0.5*v2_ref[...]+0.5*g*g
    v=vm_ref[...]-0.2*(f/corr)/(jnp.sqrt(s/corr)+adam_eps)
    vec_o[...]=v; vecc_o[...]=v.astype(BF)
    v1_o[...]=f; v2_o[...]=s

def new_weights(owners,upd,conv,dense,attn,vm,v1,v2,gvec):
    sd=jax.ShapeDtypeStruct
    mains=(conv,dense,attn,vm)
    return pl.pallas_call(weights_body,
        out_shape=[sd(a.shape,F32) for a in mains]+[sd(a.shape,BF) for a in mains]+[sd(v1.shape,F32)]*2,
        in_specs=[SMEM]+[VMEM]*8,out_specs=[VMEM]*10,
        compiler_params=pltpu.CompilerParams(vmem_limit_bytes=LIMIT),
        name="new_weights")(owners,upd,conv,dense,attn,vm,v1,v2,gvec)

def step(depth, images, time_embed, out_cotangent, conv_master, dense_master, attn_master, vector_master, vector_first, vector_second,
         owners, slot_first, slot_second, slot_left_basis, slot_right_basis, slot_left_stat, slot_right_stat):
    batch,side,_,c=images.shape
    ndev=lax.axis_size("wide")*lax.axis_size("narrow")
    flat=lambda a: a.reshape(batch,side*side,c)
    conv=conv_master.reshape((-1,)+conv_master.shape[2:])
    if depth:
        w=gather_weights(conv,dense_master,attn_master,vector_master,depth)
    else:
        gather=lambda a,axis: lax.all_gather(a.astype(BF),AXES,axis=axis,tiled=True)
        dense=jnp.swapaxes(gather(dense_master,0).reshape(c//16,2,16,c),0,1).reshape(2,c,c)
        vec=jnp.pad(gather(vector_master,1),((0,c-vector_master.shape[0]),(0,0)))
        w=jnp.concatenate([gather(conv,1),gather(attn_master,1),dense,vec[None],jnp.zeros((1,c,c),BF)])
    act,igrad,tgrad,grads,gvec,inv=train_images(owners,flat(images),flat(out_cotangent),time_embed,w,side,ndev)
    if depth:
        q,gvec=reduce_grads(inv,grads,gvec,depth)
        q=q.reshape(-1,c)
    else:
        total=lax.optimization_barrier(lax.psum(grads.astype(F32),AXES)).astype(BF)
        gvec=lax.psum(gvec,AXES)
        held=inv[lax.axis_index(AXES)]
        q=jnp.stack([total[jnp.maximum(held,0)].reshape(c//16,16,c),total[MATS+1].reshape(c//16,16,c)],axis=1).reshape(-1,c)
    *slots,send=owner_step(inv,q,slot_first,slot_second,slot_left_basis,slot_right_basis,slot_left_stat,slot_right_stat,ndev)
    if depth:
        upd=deal_updates(send)
        new=new_weights(owners,upd,conv,dense_master,attn_master,vector_master,vector_first,vector_second,gvec)
    else:
        upd=lax.all_to_all(send,AXES,0,0,tiled=True)
        new=new_weights(owners,upd,conv,dense_master,attn_master,vector_master,vector_first,vector_second,gvec)
    conv_new,dense_new,attn_new,vec_new,conv_copy,dense_copy,attn_copy,vec_copy,first_new,second_new=new
    return (act.reshape(images.shape),igrad.reshape(images.shape),tgrad,conv_new.reshape(conv_master.shape),dense_new,attn_new,vec_new,
            conv_copy.reshape(conv_master.shape),dense_copy,attn_copy,vec_copy,first_new,second_new,*slots)

def solution(mesh):
    rows,both=P(AXES),P(None,AXES)
    taps=P(None,None,AXES)
    depth=4 if (mesh.shape["wide"],mesh.shape["narrow"])==(8,4) else 0
    return jax.shard_map(functools.partial(step,depth),mesh=mesh,
        in_specs=(rows,rows,rows,taps,rows,both,both,both,both,P())+(rows,)*6,
        out_specs=(rows,rows,rows,taps,rows,both,both,taps,rows,both,both,both,both)+(rows,)*6,
        check_vma=False)
```

```python
import functools

import jax
import jax.numpy as jnp
from jax import lax
from jax.experimental import pallas as pl
from jax.experimental.pallas import tpu as pltpu
from jax.sharding import PartitionSpec as P

BF = jnp.bfloat16
F32 = jnp.float32
STEP = 10
GROUP = 8
BLK = 128
half_root = 0.5**0.5
norm_eps = 1e-6
adam_eps = 1e-8
HI = lax.Precision.HIGHEST
MESH = pl.DeviceIdType.MESH
AXES = ("wide", "narrow")
MATS = 22
VMEM = pl.BlockSpec(memory_space=pltpu.VMEM)
SMEM = pl.BlockSpec(memory_space=pltpu.SMEM)
ANY = pl.BlockSpec(memory_space=pl.ANY)
LIMIT = 56 << 20
TOGETHER = 6

def mm(a,b):
    return lax.dot_general(a,b,(((1,),(0,)),((),())),preferred_element_type=F32)
def mm_nt(a,b):
    return lax.dot_general(a,b,(((1,),(1,)),((),())),preferred_element_type=F32)
def mm_tn(a,b):
    return lax.dot_general(a,b,(((0,),(0,)),((),())),preferred_element_type=F32)

def group_sum(v):
    lane=lax.broadcasted_iota(jnp.int32, v.shape, 1)
    n=v.shape[1]
    for s in (1,2,4):
        v=v+jnp.where((lane & s)==0, pltpu.roll(v,n-s,1), pltpu.roll(v,s,1))
    return v

def col_sum(v):
    return jnp.sum(v,axis=0,keepdims=True)

def pad8(v):
    return jnp.broadcast_to(v,(8,v.shape[1]))

def group_mean(colsum, count):
    return group_sum(pad8(colsum))[0:1]*(1.0/count)

def normal_form(v):
    count=v.shape[0]*GROUP
    m=group_mean(col_sum(v),count)
    yield
    c=v-m
    var=group_mean(col_sum(c*c),count)
    yield
    r=lax.rsqrt(var+norm_eps)
    return c*r, r

def norm_back(grad, xhat, r, gain):
    count=grad.shape[0]*GROUP
    shift_grad=col_sum(grad)
    gain_grad=col_sum(grad*xhat)
    m1=group_mean(shift_grad*gain,count)
    m2=group_mean(gain_grad*gain,count)
    yield
    return (grad*(gain*r)-(m1*r)-xhat*(m2*r)), gain_grad, shift_grad

def sigmoid(y):
    return pl.reciprocal(1.0+jnp.exp(-y),approx=True)

def spread(ref, i, v, side):
    tokens, c = v.shape
    x=lax.broadcasted_iota(jnp.int32,(tokens,1),0) & (side-1)
    before=jnp.where(x==0,0.0,pltpu.roll(v,1,0)).astype(BF)
    after=jnp.where(x==side-1,0.0,pltpu.roll(v,tokens-1,0)).astype(BF)
    ref[i,side:side+tokens,0:c]=before
    ref[i,side:side+tokens,c:2*c]=v.astype(BF)
    ref[i,side:side+tokens,2*c:3*c]=after

def taps(ref, count, dy, tokens, side):
    return jnp.concatenate([ref[i,side*dy:side*dy+tokens,:] for i in range(count)],axis=0)

def train_body(side, owners_ref, img_ref, cot_ref, emb_ref, w_ref,
         act_ref, igrad_ref, tgrad_ref, gw_ref, gvec_ref, inv_ref,
         dense_ref, vec_ref, wt, acc, gvec, proj, pgrad, p1, p2, s2, s1):
    step=pl.program_id(0); steps=pl.num_programs(0)
    ib,tokens,c=img_ref.shape
    batch=emb_ref.shape[0]
    scale=c**-0.5

    @pl.when(step==0)
    def _():
        acc[...]=jnp.zeros_like(acc)
        gvec[...]=jnp.zeros_like(gvec)
        pgrad[...]=jnp.zeros_like(pgrad)
        for ref in (p1,p2,s2,s1):
            for i in range(ib):
                z=jnp.zeros((side,3*c),BF)
                ref[i,0:side,:]=z
                ref[i,side+tokens:2*side+tokens,:]=z
        for k in range(2):
            for t in range(9):
                wt[k, 8-t]=w_ref[9*k+t].T
        chips=c//16
        total=jnp.zeros((16,c),F32)
        for o in range(chips):
            total=total+w_ref[24,16*o:16*o+16].astype(F32)
            for h in range(2):
                dense_ref[32*o+16*h:32*o+16*h+16]=w_ref[22+h,16*o:16*o+16]
        vec_ref[...]=total
        for d in range(inv_ref.shape[0]):
            inv_ref[d]=-1
        for m in range(owners_ref.shape[0]):
            inv_ref[owners_ref[m]]=m if m<9 else MATS if m==9 else m-1
        e=emb_ref[...].astype(F32)
        proj[0:batch]=mm((e*sigmoid(e)).astype(BF),dense_ref[...])+total[7:8]

    vec=vec_ref[...]
    row=lambda k: vec[k:k+1]

    up=lambda t: t.astype(F32)
    sums={}
    def add(kk,val):
        sums[kk]=val if kk not in sums else sums[kk]+val
    def three(ref,k,dy):
        return jnp.concatenate([ref[k+3*dy+dx] for dx in range(3)],axis=0)
    def conv(ref,i,weight):
        out=None
        for dy in range(3):
            part=mm(ref[i,side*dy:side*dy+tokens,:],weight(dy))
            out=part if out is None else out+part
            yield
        return out
    def wgrad(base,aref,gref,i):
        at=aref[i,side:side+tokens,c:2*c].T
        for dy in range(3):
            g=mm(at,gref[i,side*dy:side*dy+tokens,:])
            for dx in range(3):
                acc[base+8-(3*dy+dx)]+=g[:,dx*c:(dx+1)*c]
            yield
    def swish_back(grad,h,gain,shift):
        y=h*gain+shift
        s=sigmoid(y)
        return grad*(s*(1.0+y*(1.0-s)))

    def image(i):
        x=img_ref[i].astype(F32)
        h0,r0=yield from normal_form(x)
        y=h0*row(0)+row(3)
        spread(p1,i,y*sigmoid(y),side)
        yield
        t=yield from conv(p1,i,lambda dy: three(w_ref,0,dy))
        t=t+(row(6)+proj[pl.ds(step*ib+i,1),:])
        h1,r1=yield from normal_form(t)
        y=h1*row(1)+row(4)
        spread(p2,i,y*sigmoid(y),side)
        yield
        t=yield from conv(p2,i,lambda dy: three(w_ref,9,dy))
        mid=(x+(t+row(8)))*half_root
        h2,r2=yield from normal_form(mid)
        normed=(h2*row(2)+row(5)).astype(BF)
        yield
        q=(mm(normed,w_ref[18])+row(9)).astype(BF)
        k=mm(normed,w_ref[19]).astype(BF)
        yield
        v=(mm(normed,w_ref[20])+row(10)).astype(BF)
        sc=mm_nt(q,k)*scale
        yield
        e=jnp.exp(sc-jnp.max(sc,axis=1,keepdims=True))
        a=e/jnp.sum(e,axis=1,keepdims=True)
        low=a.astype(BF)
        yield
        mixed=mm(low,v).astype(BF)
        cot=cot_ref[i].astype(F32)*half_root
        bg=cot.astype(BF)
        mg=mm_nt(bg,w_ref[21]).astype(BF)
        add(11,col_sum(up(bg)))
        yield
        branch=mm(mixed,w_ref[21])+row(11)
        pg=mm_nt(mg,v)
        act_ref[i]=((mid+branch)*half_root).astype(BF)
        yield
        sg=(a*(pg-jnp.sum(a*pg,axis=1,keepdims=True))).astype(BF)
        acc[21]+=mm_tn(mixed,bg)
        vg=mm_tn(low,mg).astype(BF)
        yield
        qg=(mm(sg,k)*scale).astype(BF)
        kg=(mm_tn(sg,q)*scale).astype(BF)
        yield
        ng=mm_nt(qg,w_ref[18])+mm_nt(kg,w_ref[19])+mm_nt(vg,w_ref[20])
        yield
        normed_t=normed.T
        acc[18]+=mm(normed_t,qg)
        acc[19]+=mm(normed_t,kg)
        acc[20]+=mm(normed_t,vg)
        add(9,col_sum(up(qg)));add(10,col_sum(up(vg)))
        yield
        d,gg,gs=yield from norm_back(ng,h2,r2,row(2))
        add(2,gg);add(5,gs)
        midg=cot+d
        g=up((midg*half_root).astype(BF))
        add(8,col_sum(g))
        spread(s2,i,g,side)
        yield
        ag=yield from conv(s2,i,lambda dy: three(wt.at[1],0,dy))
        d=swish_back(ag,h1,row(1),row(4))
        yield
        yield from wgrad(9,p2,s2,i)
        d,gg,gs=yield from norm_back(d,h1,r1,row(1))
        add(1,gg);add(4,gs)
        g=up(d.astype(BF))
        s=col_sum(g)
        add(6,s)
        pgr=up(s.astype(BF))
        pgrad[pl.ds(step*ib+i,1),:]=pgr
        add(7,pgr)
        spread(s1,i,g,side)
        yield
        ag=yield from conv(s1,i,lambda dy: three(wt.at[0],0,dy))
        d=swish_back(ag,h0,row(0),row(3))
        yield
        yield from wgrad(0,p1,s1,i)
        d,gg,gs=yield from norm_back(d,h0,r0,row(0))
        add(0,gg);add(3,gs)
        igrad_ref[i]=midg*half_root+d

    def run(count):
        sums.clear()
        live=[image(i) for i in range(count)]
        while live:
            for g in list(live):
                try: next(g)
                except StopIteration: live.remove(g)
        gvec[0:12]+=jnp.concatenate([sums[j] for j in range(12)],axis=0)
    rest=batch-ib*(-(-batch//ib)-1)
    if rest==ib: run(ib)
    else:
        @pl.when(step<steps-1)
        def _(): run(ib)
        @pl.when(step==steps-1)
        def _(): run(rest)

    @pl.when(step==steps-1)
    def _():
        for m in range(acc.shape[0]):
            gw_ref[m]=acc[m].astype(BF)
        gvec_ref[...]=gvec[...]
        e=emb_ref[...].astype(F32)
        s=sigmoid(e)
        ea=(e*s).astype(BF)
        pg=pgrad[0:batch].astype(BF)
        tgrad_ref[...]=mm_nt(pg,dense_ref[...])*(s*(1.0+e*(1.0-s)))
        gd=mm_tn(ea,pg).astype(BF)
        for o in range(c//16):
            for h in range(2):
                gw_ref[22+h,16*o:16*o+16]=gd[32*o+16*h:32*o+16*h+16]

def train_images(owners,images,cot,embed,w,side,ndev):
    batch,tokens,c=images.shape
    emb=embed.shape[1]
    ib=min(TOGETHER,batch)
    rows=-(-batch//8)*8
    whole=lambda a: pl.BlockSpec(a.shape,lambda s: (0,)*len(a.shape))
    blk=pl.BlockSpec((ib,tokens,c),lambda s:(s,0,0))
    sd=jax.ShapeDtypeStruct
    outs=[sd((batch,tokens,c),BF),sd((batch,tokens,c),F32),sd((batch,emb),F32),sd((MATS+2,c,c),BF),sd((16,c),F32)]
    return pl.pallas_call(functools.partial(train_body,side),grid=(-(-batch//ib),),
        in_specs=[SMEM,blk,blk,whole(embed),whole(w)],
        out_specs=[blk,blk]+[whole(o) for o in outs[2:]]+[SMEM],
        out_shape=outs+[sd((ndev,),jnp.int32)],
        scratch_shapes=[pltpu.VMEM((emb,c),BF),pltpu.VMEM((16,c),F32),pltpu.VMEM((2,9,c,c),BF),pltpu.VMEM((MATS,c,c),F32),pltpu.VMEM((16,c),F32),pltpu.VMEM((rows,c),F32),pltpu.VMEM((rows,c),F32)]
          +[pltpu.VMEM((ib,tokens+2*side,3*c),BF)]*4,
        compiler_params=pltpu.CompilerParams(vmem_limit_bytes=LIMIT),
        name="train_images")(owners,images,cot,embed,w)

def fdot(a,b,ca,cb):
    return lax.dot_general(a,b,(((ca,),(cb,)),((),())),precision=HI,preferred_element_type=F32)
nn=lambda a,b: fdot(a,b,1,0)
nt=lambda a,b: fdot(a,b,1,1)
tn=lambda a,b: fdot(a,b,0,0)

def inverse_factors(blocks):
    n=BLK
    lane=lax.broadcasted_iota(jnp.int32,(8,n),1)
    sub=lax.broadcasted_iota(jnp.int32,(8,n),0)
    tables=[[b[8*v:8*v+8] for v in range(n//8)] for b in blocks]
    over_lanes=lambda t,j: jnp.broadcast_to(t[:,j:j+1],(8,n))
    over_rows=lambda t,i: jnp.broadcast_to(t[i:i+1],(8,n))
    for J in range(n//8):
        lo=8*J
        in_block=(lane>=lo)&(lane<lo+8)
        for t in tables:
            cur=t[J]
            cols=[over_lanes(cur,lo+j) for j in range(8)]
            m=[[over_rows(cols[j],i) for j in range(i+1)] for i in range(8)]
            R=[jnp.where(in_block,jnp.where(lane==lo+i,1.0,0.0),over_rows(cur,i)) for i in range(8)]
            r=[None]*8
            l=[[None]*8 for _ in range(8)]
            for k in range(8):
                d=m[k][k]
                r[k]=pl.reciprocal(d,approx=True)
                for i in range(k+1,8):
                    l[i][k]=m[i][k]*r[k]
                for i in range(k+1,8):
                    for j in range(k+1,i+1):
                        m[i][j]=m[i][j]-l[i][k]*m[j][k]
                    R[i]=R[i]-l[i][k]*R[k]
            P=[None]*8
            for k in range(7,-1,-1):
                P[k]=R[k]*r[k]
                for i in range(7,k,-1):
                    P[k]=P[k]-l[i][k]*P[i]
            done=R[0]*lax.rsqrt(m[0][0])
            for i in range(1,8):
                done=jnp.where(sub==i,R[i]*lax.rsqrt(m[i][i]),done)
            t[J]=jnp.where(lane<=lo+sub,done,0.0)
            for v in range(J+1,n//8):
                new=jnp.where(in_block,0.0,t[v])
                for k in range(8):
                    new=new-over_lanes(t[v],lo+k)*P[k]
                t[v]=new
    return [jnp.concatenate(t,axis=0) for t in tables]

def at(k,size):
    return pl.ds(pl.multiple_of(k*size,size),size)

def split(x):
    hi=x.astype(BF)
    return hi,(x-hi.astype(F32)).astype(BF)

def bdot(a,b,ca,cb):
    return lax.dot_general(a,b,(((ca,),(cb,)),((),())),preferred_element_type=F32)

def dot3(a,b,ca,cb):
    (ah,al),(bh,bl)=split(a),split(b)
    return bdot(ah,bh,ca,cb)+(bdot(ah,bl,ca,cb)+bdot(al,bh,ca,cb))

def dot2(a,b,ca,cb):
    ah,al=split(a)
    return bdot(ah,b,ca,cb)+bdot(al,b,ca,cb)

def factor_both(a_l, g_l, a_r, g_r):
    for p in range(g_l.shape[0]//BLK):
        lo,hi=p*BLK,(p+1)*BLK
        live=[(a,g) for a,g in ((a_l,g_l),(a_r,g_r)) if g.shape[0]>lo]
        invs=inverse_factors([g[lo:hi,lo:hi] for _,g in live])
        for (a,g),inv in zip(live,invs):
            q=dot3(a[:,lo:hi],inv,1,1)
            if hi<g.shape[0]:
                r=nn(inv,g[lo:hi,hi:])
                g[hi:,hi:]=g[hi:,hi:]-tn(r,r)
                a[:,hi:]=a[:,hi:]-dot3(q,r,1,0)
            a[:,lo:hi]=q

def soap(nb, grad, ins, outs, update, g_l, g_r):
    (first,second,left,right,lstat,rstat)=ins
    first_o,second_o,left_o,right_o,lstat_o,rstat_o=outs
    c=right.shape[0]
    big=left.shape[0]
    g=grad[...]
    L=left[...]; Rb=right[...]
    ls=0.95*lstat[...]+0.05*bdot(g,g,1,1)
    rs=0.95*rstat[...]+0.05*bdot(g,g,0,0)
    lstat_o[...]=ls; rstat_o[...]=rs
    ar=nn(rs,Rb)
    right_o[...]=ar
    g_r[...]=tn(ar,ar)
    al=nn(ls,L)
    left_o[...]=al
    unit=(lax.broadcasted_iota(jnp.int32,(big,big),0)==lax.broadcasted_iota(jnp.int32,(big,big),1))&(lax.broadcasted_iota(jnp.int32,(big,big),0)>=nb*c)
    g_l[...]=tn(al,al)+jnp.where(unit,1.0,0.0)
    corr=1.0-0.5**STEP
    turned=dot3(dot2(L,g,0,0),Rb,1,0)
    inside=lax.broadcasted_iota(jnp.int32,(big,c),0)<nb*c
    moment=jnp.where(inside,0.5*first[...]+0.5*turned,0.0)
    sec=jnp.where(inside,0.5*second[...]+0.5*turned*turned,0.0)
    first_o[...]=moment; second_o[...]=sec
    direction=moment/corr/(jnp.sqrt(sec/corr)+adam_eps)
    update[...]=dot3(dot3(L,direction,1,0),Rb,1,1)
    factor_both(left_o,g_l,right_o,g_r)

def owner_body(inv_ref, q_ref, *refs):
    ins_hbm=refs[0:6]; outs_hbm=refs[6:12]; send_o=refs[12]
    ins=refs[13:19]; outs=refs[19:25]
    grad,update,g_l,g_r,in_sem,out_sem=refs[25:]
    me=lax.axis_index("wide")*lax.axis_size("narrow")+lax.axis_index("narrow")
    held=inv_ref[me]
    kind=jnp.where(held<0,0,jnp.where(held==MATS,2,1))
    c=ins[3].shape[1]; big=ins[2].shape[1]
    copies_in=[pltpu.make_async_copy(h.at[0],v,in_sem.at[i]) for i,(h,v) in enumerate(zip(ins_hbm,ins))]
    copies_out=[pltpu.make_async_copy(v,h.at[0],out_sem.at[i]) for i,(h,v) in enumerate(zip(outs_hbm,outs))]
    for cp in copies_in: cp.start()
    @pl.when(kind==1)
    def _():
        grad[...]=jnp.zeros_like(grad)
        for i in range(big//32):
            grad[16*i:16*i+16]=q_ref[32*i:32*i+16]
    @pl.when(kind==2)
    def _():
        grad[...]=q_ref[...]
    for cp in copies_in: cp.wait()
    ndev=send_o.shape[0]
    @pl.when(kind==0)
    def _():
        for o in outs: o[...]=jnp.zeros_like(o)
        send_o[...]=jnp.zeros_like(send_o)
    @pl.when(kind>0)
    def _():
        soap(kind,grad,ins,outs,update,g_l,g_r)
    for size,number in ((c,1),(big,2)):
        @pl.when(kind==number)
        def _():
            r=size//ndev
            for d in range(ndev):
                u=update[r*d:r*d+r]
                if r<16: u=jnp.concatenate([u,jnp.zeros((16-r,c),F32)],axis=0)
                send_o[d]=u.astype(BF)
    for cp in copies_out: cp.start()
    for cp in copies_out: cp.wait()

def owner_step(inv,q,first,second,left,right,lstat,rstat,ndev):
    c=right.shape[1]; big=left.shape[1]
    slots=(first,second,left,right,lstat,rstat)
    sd=lambda a: jax.ShapeDtypeStruct(a.shape,F32)
    vm=pl.BlockSpec(memory_space=pltpu.VMEM); hb=pl.BlockSpec(memory_space=pl.ANY)
    buf=lambda a: pltpu.VMEM(a.shape[1:],F32)
    return pl.pallas_call(owner_body,
        in_specs=[pl.BlockSpec(memory_space=pltpu.SMEM),vm]+[hb]*6,
        out_specs=[hb]*6+[vm],
        out_shape=[sd(a) for a in slots]+[jax.ShapeDtypeStruct((ndev,16,c),BF)],
        scratch_shapes=[buf(a) for a in slots]*2+[pltpu.VMEM((big,c),BF),pltpu.VMEM((big,c),F32)]+[pltpu.VMEM((big,big),F32),pltpu.VMEM((c,c),F32),
          pltpu.SemaphoreType.DMA((6,)),pltpu.SemaphoreType.DMA((6,))],
        compiler_params=pltpu.CompilerParams(vmem_limit_bytes=LIMIT),
        name="owner_step")(inv,q,*slots)

def place():
    w,n=lax.axis_index("wide"),lax.axis_index("narrow")
    return lax.div(w,2),lax.rem(w,2),lax.div(n,2),lax.rem(n,2)

def device(z,y,x,core):
    return (z*2+y,x*2+core)

def chip_of(z,y,x):
    return (z*2+y)*2+x

def greet(partners):
    barrier=pltpu.get_barrier_semaphore()
    count=0
    for dev,cond in partners:
        if cond is None:
            pl.semaphore_signal(barrier,inc=1,device_id=dev,device_id_type=MESH)
            count=count+1
        else:
            @pl.when(cond)
            def _():
                pl.semaphore_signal(barrier,inc=1,device_id=dev,device_id_type=MESH)
            count=count+jnp.where(cond,1,0)
    pl.semaphore_wait(barrier,count)

def remote(src,dst,send,recv,dev):
    return pltpu.make_async_remote_copy(src_ref=src,dst_ref=dst,send_sem=send,recv_sem=recv,device_id=dev,device_id_type=MESH)

GATHER=MATS+4
SHARE=GATHER//2
CUT=(SHARE+1)//2

def gather_body(depth, conv_ref, dense_ref, attn_ref, vec_ref, w_ref, part, vbuf,
                pair_s, pair_r, own_r, twin_r, up_s, down_s, x_s, y_s, twin_s):
    z,y,x,core=place()
    me=chip_of(z,y,x)
    rank=me*2+core
    twin=device(z,y,x,1-core)
    greet([(twin,None),(device(z,y,1-x,core),None),(device(z,1-y,x,core),None),
           (device(z-1,y,x,core),z>0),(device(z+1,y,x,core),z<depth-1)])
    conv=conv_ref.shape[0]
    part[0,0:conv]=conv_ref[...]
    part[0,conv:MATS]=attn_ref[...]
    part[0,MATS]=dense_ref[0:8]
    part[0,MATS+1]=dense_ref[8:16]
    cols,rows_v=vec_ref.shape
    vbuf[...]=jnp.zeros_like(vbuf)
    vbuf[0:cols,0:rows_v]=vec_ref[...]
    turned=vbuf[0:8,0:128].T[0:16]
    vbuf[...]=jnp.zeros_like(vbuf)
    vbuf[:,0:8]=turned
    mine=pltpu.roll(vbuf[...],rank*cols,1)
    part[0,MATS+2]=mine[0:8]
    part[0,MATS+3]=mine[8:16]
    swap=remote(part.at[0],part.at[1],pair_s,pair_r,twin)
    swap.start()
    rows=lambda o: pl.ds(pl.multiple_of(o*16,16),16)
    swap.wait()
    even,odd=core,1-core
    for m in range(MATS):
        w_ref[m,rows(me)]=jnp.concatenate([part[even,m],part[odd,m]],axis=0).astype(BF)
    for h,src in ((0,even),(1,odd)):
        w_ref[MATS+h,rows(me)]=jnp.concatenate([part[src,MATS],part[src,MATS+1]],axis=0).astype(BF)
    w_ref[MATS+2,rows(me)]=jnp.concatenate([part[0,MATS+2]+part[1,MATS+2],part[0,MATS+3]+part[1,MATS+3]],axis=0).astype(BF)
    w_ref[MATS+3,rows(me)]=jnp.zeros((16,w_ref.shape[2]),BF)

    def block(h,o,whose=core):
        return w_ref.at[pl.ds(SHARE*whose+(0,CUT)[h],(CUT,SHARE-CUT)[h]),rows(o)]
    def copy(h,o,send,recv,dev):
        return remote(block(h,o),block(h,o),send,recv.at[h,o],dev)
    def arrived(h,o):
        copy(h,o,pair_s,own_r,twin).wait_recv()
    side_x,side_y=device(z,y,1-x,core),device(z,1-y,x,core)
    to_x=lambda h,o: copy(h,o,x_s.at[h,o],own_r,side_x)
    to_y=lambda h,o: copy(h,o,y_s.at[h,o],own_r,side_y)
    to_twin=lambda h,o: copy(h,o,twin_s.at[h,o],twin_r,twin)
    to_up=lambda h,o: copy(h,o,up_s.at[h,o],own_r,device(z+1,y,x,core))
    to_down=lambda h,o: copy(h,o,down_s.at[h,o],own_r,device(z-1,y,x,core))

    def line(zz,wait,up,down):
        o=chip_of(zz,y,x)
        for h in range(2):
            if wait: arrived(h,o)
            if up:
                @pl.when(z<depth-1)
                def _(): to_up(h,o).start()
            if down:
                @pl.when(z>0)
                def _(): to_down(h,o).start()
            first,second=((to_x,to_y),(to_y,to_x))[h]
            first(h,o).start()
            second(h,o).start()
            if wait: to_twin(h,o).start()
    def sides(zz):
        o=chip_of(zz,y,1-x)
        arrived(0,o); to_y(0,o).start(); to_twin(0,o).start()
        o=chip_of(zz,1-y,x)
        arrived(1,o); to_x(1,o).start(); to_twin(1,o).start()
    def both(d,run):
        for zz,up in ((z-d,True),(z+d,False)):
            @pl.when((zz>=0)&(zz<depth))
            def _(): run(zz,up)
    line(z,False,True,True)
    for d in range(1,depth+1):
        if d<depth:
            both(d,lambda zz,up: line(zz,True,up,not up))
        if d==1: sides(z)
        else: both(d-1,lambda zz,up: sides(zz))
    @pl.loop(0,depth)
    def _(zz):
        for a in range(2):
            o=chip_of(zz,1-y,a)
            arrived(0,o); to_twin(0,o).start()
            o=chip_of(zz,a,1-x)
            arrived(1,o); to_twin(1,o).start()
    @pl.loop(1,depth*4)
    def _(k):
        o=lax.rem(me+k,depth*4)
        for h in range(2):
            remote(block(h,o,1-core),block(h,o,1-core),pair_s,twin_r.at[h,o],twin).wait_recv()
            to_twin(h,o).wait_send()
    @pl.loop(0,depth)
    def _(zz):
        o=chip_of(zz,y,x)
        for h in range(2):
            to_x(h,o).wait_send(); to_y(h,o).wait_send()
            @pl.when((z<depth-1)&(zz<=z))
            def _(): to_up(h,o).wait_send()
            @pl.when((z>0)&(zz>=z))
            def _(): to_down(h,o).wait_send()
        to_y(0,chip_of(zz,y,1-x)).wait_send()
        to_x(1,chip_of(zz,1-y,x)).wait_send()

def gather_weights(conv,dense,attn,vec,depth):
    c=conv.shape[2]
    chips=depth*4
    dma=pltpu.SemaphoreType.DMA
    return pl.pallas_call(functools.partial(gather_body,depth),
        out_shape=jax.ShapeDtypeStruct((GATHER,c,c),BF),
        in_specs=[VMEM]*4,out_specs=VMEM,
        scratch_shapes=[pltpu.VMEM((2,GATHER,8,c),F32),pltpu.VMEM((16,c),F32),dma,dma]+[dma((2,chips))]*7,
        compiler_params=pltpu.CompilerParams(collective_id=0,has_side_effects=True,vmem_limit_bytes=LIMIT),
        name="gather_weights")(conv,dense,attn,vec)

REDUCE=MATS+2
HALF=REDUCE//2
PARTS=((0,5,"xyz"),(5,4,"yzx"),(9,3,"zxy"))

def reduce_body(depth, inv_ref, g_ref, v_ref, q_ref, vec_o, acc, core_in, bx0, by0, up0, down0, bx1, by1, up1, down1, bx2, by2, up2, down2,
                final, pick, vsend, vrecv, core_s, core_r, ex_s, ex_r, up_s, up_r, down_s, down_r, twin_s, twin_r, out_s, out_r, v_s, v_r):
    z,y,x,core=place()
    me=chip_of(z,y,x)
    chips=depth*4
    twin=device(z,y,x,1-core)
    def of_chip(o):
        return device(lax.div(o,4),lax.rem(lax.div(o,2),2),lax.rem(o,2),core)
    others=[lax.rem(me+k,chips) for k in range(1,chips)]
    greet([(twin,None)]+[(of_chip(o),None) for o in others])
    c=g_ref.shape[2]
    pair=[]
    for i,(m0,n,_) in enumerate(PARTS):
        cp=remote(g_ref.at[pl.ds(HALF*(1-core)+m0,n)],core_in.at[m0:m0+n],core_s.at[i],core_r.at[i],twin)
        cp.start(); pair.append(cp)
    def vec_start(stage,dev):
        cp=remote(vsend.at[stage],vrecv.at[stage],v_s.at[stage],v_r.at[stage],dev)
        cp.start()
        return cp
    def vec_end(stage,cp):
        cp.wait()
        total=vsend[stage]+vrecv[stage]
        if stage<4: vsend[stage+1]=total
        else: vec_o[...]=total
    vsend[0]=v_ref[...]
    vcp=vec_start(0,twin)
    nbr_x,nbr_y=device(z,y,1-x,core),device(z,1-y,x,core)
    bufs=((bx0,by0,up0,down0),(bx1,by1,up1,down1),(bx2,by2,up2,down2))
    started={}
    def where(i,done):
        return ["z" in done and z, "y" in done and y, "x" in done and x]
    def index(m,place):
        return tuple([m]+[slice(None) if p is False else p for p in place])
    def swap_start(i,stage):
        m0,n,order=PARTS[i]
        axis=order[stage]
        at=where(i,order[:stage])
        at["zyx".index(axis)]=1-(x if axis=="x" else y)
        dst=bufs[i][0 if axis=="x" else 1]
        k=0 if axis=="x" else 1
        cp=remote(acc.at[index(slice(m0,m0+n),at)],dst,ex_s.at[i,k],ex_r.at[i,k],nbr_x if axis=="x" else nbr_y)
        cp.start()
        started[i,stage]=cp
    def swap_end(i,stage):
        m0,n,order=PARTS[i]
        axis=order[stage]
        started.pop((i,stage)).wait()
        at=where(i,order[:stage+1])
        src=bufs[i][0 if axis=="x" else 1]
        @pl.loop(0,n)
        def _(m):
            there=index(m0+m,at)
            acc[there]=(acc[there].astype(F32)+src[m].astype(F32)).astype(BF)
    def z_line(i,stage):
        m0,n,order=PARTS[i]
        at=where(i,order[:stage])
        up,down=bufs[i][2:]
        def view(zz):
            a=list(at); a[0]=zz
            return index(slice(m0,m0+n),a)
        def add(buf,zz):
            a=list(at); a[0]=zz
            @pl.loop(0,n)
            def _(m):
                there=index(m0+m,a)
                acc[there]=(acc[there].astype(F32)+buf[zz,m].astype(F32)).astype(BF)
        def to_up(zz): return remote(acc.at[view(zz)],up.at[zz],up_s.at[i,zz],up_r.at[i,zz],device(z+1,y,x,core))
        def to_down(zz): return remote(acc.at[view(zz)],down.at[zz],down_s.at[i,zz],down_r.at[i,zz],device(z-1,y,x,core))
        for k in range(depth-1):
            top,low=depth-1-k,k
            @pl.when(z<top)
            def _():
                @pl.when(z>0)
                def _():
                    to_up(top).wait_recv(); add(up,top)
                to_up(top).start()
            @pl.when(z>low)
            def _():
                @pl.when(z<depth-1)
                def _():
                    to_down(low).wait_recv(); add(down,low)
                to_down(low).start()
        @pl.when(z>0)
        def _():
            to_up(z).wait_recv(); add(up,z)
        @pl.when(z<depth-1)
        def _():
            to_down(z).wait_recv(); add(down,z)
        for k in range(depth-1):
            top,low=depth-1-k,k
            @pl.when(z<top)
            def _(): to_up(top).wait_send()
            @pl.when(z>low)
            def _(): to_down(low).wait_send()

    def add_pair(i):
        m0,n,_=PARTS[i]
        pair[i].wait()
        @pl.loop(0,n)
        def _(m):
            s=(g_ref[HALF*core+m0+m].astype(F32)+core_in[m0+m].astype(F32)).astype(BF)
            acc[m0+m]=s.reshape(acc.shape[1:])
    add_pair(0); swap_start(0,0)
    add_pair(1); swap_start(1,0)
    add_pair(2)
    vec_end(0,vcp); vcp=vec_start(1,nbr_x)
    z_line(2,0)
    vec_end(1,vcp); vcp=vec_start(2,nbr_y)
    swap_end(0,0); swap_start(0,1)
    swap_start(2,1)
    swap_end(1,0)
    z_line(1,1)
    vec_end(2,vcp); vcp=vec_start(3,device(lax.div(z,2)*2+(1-lax.rem(z,2)),y,x,core))
    swap_start(1,2)
    swap_end(2,1); swap_start(2,2)
    swap_end(0,1)
    z_line(0,2)
    vec_end(3,vcp); vcp=vec_start(4,device(lax.rem(z+2,4),y,x,core))
    swap_end(1,2)
    swap_end(2,2)
    there=pl.ds(HALF*core,HALF)
    for m in range(HALF):
        final[HALF*core+m]=acc[m,z,y,x]
    cp=remote(final.at[there],final.at[there],twin_s,twin_r,twin)
    cp.start(); cp.wait()
    for k in range(chips):
        o=me if k==0 else others[k-1]
        m=jnp.maximum(inv_ref[o*2+core],0)
        pick[k,0]=final[m]
        pick[k,1]=final[REDUCE-1]
        if k:
            remote(pick.at[k],q_ref.at[me],out_s.at[k],out_r.at[me],of_chip(o)).start()
    q_ref[me]=pick[0]
    vec_end(4,vcp)
    for k in range(1,chips):
        o=others[k-1]
        remote(pick.at[k],q_ref.at[o],out_s.at[k],out_r.at[o],of_chip(o)).wait()

def reduce_grads(inv,grads,vec,depth):
    c=grads.shape[2]
    chips=depth*4
    dma=pltpu.SemaphoreType.DMA
    vm=lambda *s: pltpu.VMEM(s,BF)
    bufs=[]
    for _,n,order in PARTS:
        left={"z":depth,"y":2,"x":2}
        shapes={}
        for axis in order:
            del left[axis]
            shapes[axis]=tuple(left[k] for k in "zyx" if k in left)
        bufs+=[vm(n,*shapes["x"],16,c),vm(n,*shapes["y"],16,c),vm(depth,n,*shapes["z"],16,c),vm(depth,n,*shapes["z"],16,c)]
    return pl.pallas_call(functools.partial(reduce_body,depth),
        out_shape=[jax.ShapeDtypeStruct((chips,2,16,c),BF),jax.ShapeDtypeStruct(vec.shape,F32)],
        in_specs=[SMEM,VMEM,VMEM],out_specs=[VMEM,VMEM],
        scratch_shapes=[vm(HALF,depth,2,2,16,c),vm(HALF,c,c)]+bufs+[vm(REDUCE,16,c),vm(chips,2,16,c),
          pltpu.VMEM((5,)+vec.shape,F32),pltpu.VMEM((5,)+vec.shape,F32),
          dma((3,)),dma((3,)),dma((3,2)),dma((3,2)),dma((3,depth)),dma((3,depth)),dma((3,depth)),dma((3,depth)),dma,dma,
          dma((chips,)),dma((chips,)),dma((5,)),dma((5,))],
        compiler_params=pltpu.CompilerParams(collective_id=1,has_side_effects=True,vmem_limit_bytes=LIMIT),
        name="reduce_grads")(inv,grads,vec)

def deal_body(ndev, send_ref, out_ref, s_sem, r_sem):
    w,n=lax.axis_index("wide"),lax.axis_index("narrow")
    width=lax.axis_size("narrow")
    me=w*width+n
    dev=lambda d: (lax.div(d,width),lax.rem(d,width))
    others=[lax.rem(me+k,ndev) for k in range(1,ndev)]
    greet([(dev(d),None) for d in others])
    def copy(k):
        d=others[k]
        return remote(send_ref.at[d],out_ref.at[me],s_sem.at[k],r_sem.at[me],dev(d))
    for k in range(ndev-1): copy(k).start()
    out_ref[me]=send_ref[me]
    for k in range(ndev-1):
        d=others[k]
        remote(send_ref.at[d],out_ref.at[d],s_sem.at[k],r_sem.at[d],dev(d)).wait()

def deal_updates(send):
    ndev=send.shape[0]
    dma=pltpu.SemaphoreType.DMA
    return pl.pallas_call(functools.partial(deal_body,ndev),
        out_shape=jax.ShapeDtypeStruct(send.shape,send.dtype),
        in_specs=[VMEM],out_specs=VMEM,
        scratch_shapes=[dma((ndev,)),dma((ndev,))],
        compiler_params=pltpu.CompilerParams(collective_id=2,has_side_effects=True,vmem_limit_bytes=LIMIT),
        name="deal_updates")(send)

def weights_body(owners_ref, upd_ref, conv_ref, dense_ref, attn_ref, vm_ref, v1_ref, v2_ref, gv_ref,
                 conv_o, dense_o, attn_o, vec_o, convc_o, densec_o, attnc_o, vecc_o, v1_o, v2_o):
    me=lax.axis_index("wide")*lax.axis_size("narrow")+lax.axis_index("narrow")
    c=dense_ref.shape[1]
    def new(master,number,fan):
        u=upd_ref[owners_ref[number]].astype(F32)[0:master.shape[0]]
        return master-fan**-0.5*(u+0.01*master)
    for k in range(conv_ref.shape[0]):
        v=new(conv_ref[k],k+(k>=9),9*c)
        conv_o[k]=v; convc_o[k]=v.astype(BF)
    v=new(dense_ref[...],9,dense_ref.shape[0]*lax.axis_size("wide")*lax.axis_size("narrow"))
    dense_o[...]=v; densec_o[...]=v.astype(BF)
    for k in range(4):
        v=new(attn_ref[k],19+k,c)
        attn_o[k]=v; attnc_o[k]=v.astype(BF)
    cols,rows=vm_ref.shape
    g=pltpu.roll(gv_ref[...],lax.rem(c-me*cols,c),1)[:,0:128].T[0:cols,0:rows]
    corr=1.0-0.5**STEP
    f=0.5*v1_ref[...]+0.5*g
    s=0.5*v2_ref[...]+0.5*g*g
    v=vm_ref[...]-0.2*(f/corr)/(jnp.sqrt(s/corr)+adam_eps)
    vec_o[...]=v; vecc_o[...]=v.astype(BF)
    v1_o[...]=f; v2_o[...]=s

def new_weights(owners,upd,conv,dense,attn,vm,v1,v2,gvec):
    sd=jax.ShapeDtypeStruct
    mains=(conv,dense,attn,vm)
    return pl.pallas_call(weights_body,
        out_shape=[sd(a.shape,F32) for a in mains]+[sd(a.shape,BF) for a in mains]+[sd(v1.shape,F32)]*2,
        in_specs=[SMEM]+[VMEM]*8,out_specs=[VMEM]*10,
        compiler_params=pltpu.CompilerParams(vmem_limit_bytes=LIMIT),
        name="new_weights")(owners,upd,conv,dense,attn,vm,v1,v2,gvec)

def step(depth, images, time_embed, out_cotangent, conv_master, dense_master, attn_master, vector_master, vector_first, vector_second,
         owners, slot_first, slot_second, slot_left_basis, slot_right_basis, slot_left_stat, slot_right_stat):
    batch,side,_,c=images.shape
    ndev=lax.axis_size("wide")*lax.axis_size("narrow")
    flat=lambda a: a.reshape(batch,side*side,c)
    conv=conv_master.reshape((-1,)+conv_master.shape[2:])
    vector,vector_first,vector_second=vector_master.T,vector_first.T,vector_second.T
    if depth:
        w=gather_weights(conv,dense_master,attn_master,vector,depth)
    else:
        gather=lambda a,axis: lax.all_gather(a.astype(BF),AXES,axis=axis,tiled=True)
        dense=jnp.swapaxes(gather(dense_master,0).reshape(c//16,2,16,c),0,1).reshape(2,c,c)
        vec=jnp.pad(gather(vector_master,1),((0,c-vector_master.shape[0]),(0,0)))
        w=jnp.concatenate([gather(conv,1),gather(attn_master,1),dense,vec[None],jnp.zeros((1,c,c),BF)])
    act,igrad,tgrad,grads,gvec,inv=train_images(owners,flat(images),flat(out_cotangent),time_embed,w,side,ndev)
    if depth:
        q,gvec=reduce_grads(inv,grads,gvec,depth)
        q=q.reshape(-1,c)
    else:
        total=lax.optimization_barrier(lax.psum(grads.astype(F32),AXES)).astype(BF)
        gvec=lax.psum(gvec,AXES)
        held=inv[lax.axis_index(AXES)]
        q=jnp.stack([total[jnp.maximum(held,0)].reshape(c//16,16,c),total[MATS+1].reshape(c//16,16,c)],axis=1).reshape(-1,c)
    *slots,send=owner_step(inv,q,slot_first,slot_second,slot_left_basis,slot_right_basis,slot_left_stat,slot_right_stat,ndev)
    if depth:
        upd=deal_updates(send)
        new=new_weights(owners,upd,conv,dense_master,attn_master,vector,vector_first,vector_second,gvec)
    else:
        upd=lax.all_to_all(send,AXES,0,0,tiled=True)
        new=new_weights(owners,upd,conv,dense_master,attn_master,vector,vector_first,vector_second,gvec)
    conv_new,dense_new,attn_new,vec_new,conv_copy,dense_copy,attn_copy,vec_copy,first_new,second_new=new
    return (act.reshape(images.shape),igrad.reshape(images.shape),tgrad,conv_new.reshape(conv_master.shape),dense_new,attn_new,vec_new.T,
            conv_copy.reshape(conv_master.shape),dense_copy,attn_copy,vec_copy.T,first_new.T,second_new.T,*slots)

def solution(mesh):
    rows,both=P(AXES),P(None,AXES)
    taps=P(None,None,AXES)
    depth=4 if (mesh.shape["wide"],mesh.shape["narrow"])==(8,4) else 0
    return jax.shard_map(functools.partial(step,depth),mesh=mesh,
        in_specs=(rows,rows,rows,taps,rows,both,both,both,both,P())+(rows,)*6,
        out_specs=(rows,rows,rows,taps,rows,both,both,taps,rows,both,both,both,both)+(rows,)*6,
        check_vma=False)
```

```python
import functools

import jax
import jax.numpy as jnp
from jax import lax
from jax.experimental import pallas as pl
from jax.experimental.pallas import tpu as pltpu
from jax.sharding import PartitionSpec as P

BF = jnp.bfloat16
F32 = jnp.float32
STEP = 10
GROUP = 8
BLK = 128
half_root = 0.5**0.5
norm_eps = 1e-6
adam_eps = 1e-8
HI = lax.Precision.HIGHEST
MESH = pl.DeviceIdType.MESH
AXES = ("wide", "narrow")
MATS = 22
VMEM = pl.BlockSpec(memory_space=pltpu.VMEM)
SMEM = pl.BlockSpec(memory_space=pltpu.SMEM)
ANY = pl.BlockSpec(memory_space=pl.ANY)
LIMIT = 56 << 20
TOGETHER = 6
DEAL = False

def mm(a,b):
    return lax.dot_general(a,b,(((1,),(0,)),((),())),preferred_element_type=F32)
def mm_nt(a,b):
    return lax.dot_general(a,b,(((1,),(1,)),((),())),preferred_element_type=F32)
def mm_tn(a,b):
    return lax.dot_general(a,b,(((0,),(0,)),((),())),preferred_element_type=F32)

def group_sum(v):
    lane=lax.broadcasted_iota(jnp.int32, v.shape, 1)
    n=v.shape[1]
    for s in (1,2,4):
        v=v+jnp.where((lane & s)==0, pltpu.roll(v,n-s,1), pltpu.roll(v,s,1))
    return v

def col_sum(v):
    return jnp.sum(v,axis=0,keepdims=True)

def pad8(v):
    return jnp.broadcast_to(v,(8,v.shape[1]))

def group_mean(colsum, count):
    return group_sum(pad8(colsum))[0:1]*(1.0/count)

def normal_form(v):
    count=v.shape[0]*GROUP
    m=group_mean(col_sum(v),count)
    yield
    c=v-m
    var=group_mean(col_sum(c*c),count)
    yield
    r=lax.rsqrt(var+norm_eps)
    return c*r, r

def norm_back(grad, xhat, r, gain):
    count=grad.shape[0]*GROUP
    shift_grad=col_sum(grad)
    gain_grad=col_sum(grad*xhat)
    m1=group_mean(shift_grad*gain,count)
    m2=group_mean(gain_grad*gain,count)
    yield
    return (grad*(gain*r)-(m1*r)-xhat*(m2*r)), gain_grad, shift_grad

def sigmoid(y):
    return pl.reciprocal(1.0+jnp.exp(-y),approx=True)

def spread(ref, i, v, side):
    tokens, c = v.shape
    x=lax.broadcasted_iota(jnp.int32,(tokens,1),0) & (side-1)
    before=jnp.where(x==0,0.0,pltpu.roll(v,1,0)).astype(BF)
    after=jnp.where(x==side-1,0.0,pltpu.roll(v,tokens-1,0)).astype(BF)
    ref[i,side:side+tokens,0:c]=before
    ref[i,side:side+tokens,c:2*c]=v.astype(BF)
    ref[i,side:side+tokens,2*c:3*c]=after

def taps(ref, count, dy, tokens, side):
    return jnp.concatenate([ref[i,side*dy:side*dy+tokens,:] for i in range(count)],axis=0)

def train_body(side, owners_ref, img_ref, cot_ref, emb_ref, w_ref,
         act_ref, igrad_ref, tgrad_ref, gw_ref, gvec_ref, inv_ref,
         dense_ref, vec_ref, wt, acc, gvec, proj, pgrad, p1, p2, s2, s1):
    step=pl.program_id(0); steps=pl.num_programs(0)
    ib,tokens,c=img_ref.shape
    batch=emb_ref.shape[0]
    scale=c**-0.5

    @pl.when(step==0)
    def _():
        acc[...]=jnp.zeros_like(acc)
        gvec[...]=jnp.zeros_like(gvec)
        pgrad[...]=jnp.zeros_like(pgrad)
        for ref in (p1,p2,s2,s1):
            for i in range(ib):
                z=jnp.zeros((side,3*c),BF)
                ref[i,0:side,:]=z
                ref[i,side+tokens:2*side+tokens,:]=z
        for k in range(2):
            for t in range(9):
                wt[k, 8-t]=w_ref[9*k+t].T
        chips=c//16
        total=jnp.zeros((16,c),F32)
        for o in range(chips):
            total=total+w_ref[24,16*o:16*o+16].astype(F32)
            for h in range(2):
                dense_ref[32*o+16*h:32*o+16*h+16]=w_ref[22+h,16*o:16*o+16]
        vec_ref[...]=total
        for d in range(inv_ref.shape[0]):
            inv_ref[d]=-1
        for m in range(owners_ref.shape[0]):
            inv_ref[owners_ref[m]]=m if m<9 else MATS if m==9 else m-1
        e=emb_ref[...].astype(F32)
        proj[0:batch]=mm((e*sigmoid(e)).astype(BF),dense_ref[...])+total[7:8]

    vec=vec_ref[...]
    row=lambda k: vec[k:k+1]

    up=lambda t: t.astype(F32)
    sums={}
    def add(kk,val):
        sums[kk]=val if kk not in sums else sums[kk]+val
    def three(ref,k,dy):
        return jnp.concatenate([ref[k+3*dy+dx] for dx in range(3)],axis=0)
    def conv(ref,i,weight):
        out=None
        for dy in range(3):
            part=mm(ref[i,side*dy:side*dy+tokens,:],weight(dy))
            out=part if out is None else out+part
            yield
        return out
    def wgrad(base,aref,gref,i):
        at=aref[i,side:side+tokens,c:2*c].T
        for dy in range(3):
            g=mm(at,gref[i,side*dy:side*dy+tokens,:])
            for dx in range(3):
                acc[base+8-(3*dy+dx)]+=g[:,dx*c:(dx+1)*c]
            yield
    def swish_back(grad,h,gain,shift):
        y=h*gain+shift
        s=sigmoid(y)
        return grad*(s*(1.0+y*(1.0-s)))

    def image(i):
        x=img_ref[i].astype(F32)
        h0,r0=yield from normal_form(x)
        y=h0*row(0)+row(3)
        spread(p1,i,y*sigmoid(y),side)
        yield
        t=yield from conv(p1,i,lambda dy: three(w_ref,0,dy))
        t=t+(row(6)+proj[pl.ds(step*ib+i,1),:])
        h1,r1=yield from normal_form(t)
        y=h1*row(1)+row(4)
        spread(p2,i,y*sigmoid(y),side)
        yield
        t=yield from conv(p2,i,lambda dy: three(w_ref,9,dy))
        mid=(x+(t+row(8)))*half_root
        h2,r2=yield from normal_form(mid)
        normed=(h2*row(2)+row(5)).astype(BF)
        yield
        q=(mm(normed,w_ref[18])+row(9)).astype(BF)
        k=mm(normed,w_ref[19]).astype(BF)
        yield
        v=(mm(normed,w_ref[20])+row(10)).astype(BF)
        sc=mm_nt(q,k)*scale
        yield
        e=jnp.exp(sc-jnp.max(sc,axis=1,keepdims=True))
        a=e/jnp.sum(e,axis=1,keepdims=True)
        low=a.astype(BF)
        yield
        mixed=mm(low,v).astype(BF)
        cot=cot_ref[i].astype(F32)*half_root
        bg=cot.astype(BF)
        mg=mm_nt(bg,w_ref[21]).astype(BF)
        add(11,col_sum(up(bg)))
        yield
        branch=mm(mixed,w_ref[21])+row(11)
        pg=mm_nt(mg,v)
        act_ref[i]=((mid+branch)*half_root).astype(BF)
        yield
        sg=(a*(pg-jnp.sum(a*pg,axis=1,keepdims=True))).astype(BF)
        acc[21]+=mm_tn(mixed,bg)
        vg=mm_tn(low,mg).astype(BF)
        yield
        qg=(mm(sg,k)*scale).astype(BF)
        kg=(mm_tn(sg,q)*scale).astype(BF)
        yield
        ng=mm_nt(qg,w_ref[18])+mm_nt(kg,w_ref[19])+mm_nt(vg,w_ref[20])
        yield
        normed_t=normed.T
        acc[18]+=mm(normed_t,qg)
        acc[19]+=mm(normed_t,kg)
        acc[20]+=mm(normed_t,vg)
        add(9,col_sum(up(qg)));add(10,col_sum(up(vg)))
        yield
        d,gg,gs=yield from norm_back(ng,h2,r2,row(2))
        add(2,gg);add(5,gs)
        midg=cot+d
        g=up((midg*half_root).astype(BF))
        add(8,col_sum(g))
        spread(s2,i,g,side)
        yield
        ag=yield from conv(s2,i,lambda dy: three(wt.at[1],0,dy))
        d=swish_back(ag,h1,row(1),row(4))
        yield
        yield from wgrad(9,p2,s2,i)
        d,gg,gs=yield from norm_back(d,h1,r1,row(1))
        add(1,gg);add(4,gs)
        g=up(d.astype(BF))
        s=col_sum(g)
        add(6,s)
        pgr=up(s.astype(BF))
        pgrad[pl.ds(step*ib+i,1),:]=pgr
        add(7,pgr)
        spread(s1,i,g,side)
        yield
        ag=yield from conv(s1,i,lambda dy: three(wt.at[0],0,dy))
        d=swish_back(ag,h0,row(0),row(3))
        yield
        yield from wgrad(0,p1,s1,i)
        d,gg,gs=yield from norm_back(d,h0,r0,row(0))
        add(0,gg);add(3,gs)
        igrad_ref[i]=midg*half_root+d

    def run(count):
        sums.clear()
        live=[image(i) for i in range(count)]
        while live:
            for g in list(live):
                try: next(g)
                except StopIteration: live.remove(g)
        gvec[0:12]+=jnp.concatenate([sums[j] for j in range(12)],axis=0)
    rest=batch-ib*(-(-batch//ib)-1)
    if rest==ib: run(ib)
    else:
        @pl.when(step<steps-1)
        def _(): run(ib)
        @pl.when(step==steps-1)
        def _(): run(rest)

    @pl.when(step==steps-1)
    def _():
        for m in range(acc.shape[0]):
            gw_ref[m]=acc[m].astype(BF)
        gvec_ref[...]=gvec[...]
        e=emb_ref[...].astype(F32)
        s=sigmoid(e)
        ea=(e*s).astype(BF)
        pg=pgrad[0:batch].astype(BF)
        tgrad_ref[...]=mm_nt(pg,dense_ref[...])*(s*(1.0+e*(1.0-s)))
        gd=mm_tn(ea,pg).astype(BF)
        for o in range(c//16):
            for h in range(2):
                gw_ref[22+h,16*o:16*o+16]=gd[32*o+16*h:32*o+16*h+16]

def train_images(owners,images,cot,embed,w,side,ndev):
    batch,tokens,c=images.shape
    emb=embed.shape[1]
    ib=min(TOGETHER,batch)
    rows=-(-batch//8)*8
    whole=lambda a: pl.BlockSpec(a.shape,lambda s: (0,)*len(a.shape))
    blk=pl.BlockSpec((ib,tokens,c),lambda s:(s,0,0))
    sd=jax.ShapeDtypeStruct
    outs=[sd((batch,tokens,c),BF),sd((batch,tokens,c),F32),sd((batch,emb),F32),sd((MATS+2,c,c),BF),sd((16,c),F32)]
    return pl.pallas_call(functools.partial(train_body,side),grid=(-(-batch//ib),),
        in_specs=[SMEM,blk,blk,whole(embed),whole(w)],
        out_specs=[blk,blk]+[whole(o) for o in outs[2:]]+[SMEM],
        out_shape=outs+[sd((ndev,),jnp.int32)],
        scratch_shapes=[pltpu.VMEM((emb,c),BF),pltpu.VMEM((16,c),F32),pltpu.VMEM((2,9,c,c),BF),pltpu.VMEM((MATS,c,c),F32),pltpu.VMEM((16,c),F32),pltpu.VMEM((rows,c),F32),pltpu.VMEM((rows,c),F32)]
          +[pltpu.VMEM((ib,tokens+2*side,3*c),BF)]*4,
        compiler_params=pltpu.CompilerParams(vmem_limit_bytes=LIMIT),
        name="train_images")(owners,images,cot,embed,w)

def fdot(a,b,ca,cb):
    return lax.dot_general(a,b,(((ca,),(cb,)),((),())),precision=HI,preferred_element_type=F32)
nn=lambda a,b: fdot(a,b,1,0)
nt=lambda a,b: fdot(a,b,1,1)
tn=lambda a,b: fdot(a,b,0,0)

def inverse_factors(blocks):
    n=BLK
    lane=lax.broadcasted_iota(jnp.int32,(8,n),1)
    sub=lax.broadcasted_iota(jnp.int32,(8,n),0)
    tables=[[b[8*v:8*v+8] for v in range(n//8)] for b in blocks]
    over_lanes=lambda t,j: jnp.broadcast_to(t[:,j:j+1],(8,n))
    over_rows=lambda t,i: jnp.broadcast_to(t[i:i+1],(8,n))
    for J in range(n//8):
        lo=8*J
        in_block=(lane>=lo)&(lane<lo+8)
        for t in tables:
            cur=t[J]
            cols=[over_lanes(cur,lo+j) for j in range(8)]
            m=[[over_rows(cols[j],i) for j in range(i+1)] for i in range(8)]
            R=[jnp.where(in_block,jnp.where(lane==lo+i,1.0,0.0),over_rows(cur,i)) for i in range(8)]
            r=[None]*8
            l=[[None]*8 for _ in range(8)]
            for k in range(8):
                d=m[k][k]
                r[k]=pl.reciprocal(d,approx=True)
                for i in range(k+1,8):
                    l[i][k]=m[i][k]*r[k]
                for i in range(k+1,8):
                    for j in range(k+1,i+1):
                        m[i][j]=m[i][j]-l[i][k]*m[j][k]
                    R[i]=R[i]-l[i][k]*R[k]
            P=[None]*8
            for k in range(7,-1,-1):
                P[k]=R[k]*r[k]
                for i in range(7,k,-1):
                    P[k]=P[k]-l[i][k]*P[i]
            done=R[0]*lax.rsqrt(m[0][0])
            for i in range(1,8):
                done=jnp.where(sub==i,R[i]*lax.rsqrt(m[i][i]),done)
            t[J]=jnp.where(lane<=lo+sub,done,0.0)
            for v in range(J+1,n//8):
                new=jnp.where(in_block,0.0,t[v])
                for k in range(8):
                    new=new-over_lanes(t[v],lo+k)*P[k]
                t[v]=new
    return [jnp.concatenate(t,axis=0) for t in tables]

def at(k,size):
    return pl.ds(pl.multiple_of(k*size,size),size)

def split(x):
    hi=x.astype(BF)
    return hi,(x-hi.astype(F32)).astype(BF)

def bdot(a,b,ca,cb):
    return lax.dot_general(a,b,(((ca,),(cb,)),((),())),preferred_element_type=F32)

def dot3(a,b,ca,cb):
    (ah,al),(bh,bl)=split(a),split(b)
    return bdot(ah,bh,ca,cb)+(bdot(ah,bl,ca,cb)+bdot(al,bh,ca,cb))

def dot2(a,b,ca,cb):
    ah,al=split(a)
    return bdot(ah,b,ca,cb)+bdot(al,b,ca,cb)

def factor_both(a_l, g_l, a_r, g_r):
    for p in range(g_l.shape[0]//BLK):
        lo,hi=p*BLK,(p+1)*BLK
        live=[(a,g) for a,g in ((a_l,g_l),(a_r,g_r)) if g.shape[0]>lo]
        invs=inverse_factors([g[lo:hi,lo:hi] for _,g in live])
        for (a,g),inv in zip(live,invs):
            q=dot3(a[:,lo:hi],inv,1,1)
            if hi<g.shape[0]:
                r=nn(inv,g[lo:hi,hi:])
                g[hi:,hi:]=g[hi:,hi:]-tn(r,r)
                a[:,hi:]=a[:,hi:]-dot3(q,r,1,0)
            a[:,lo:hi]=q

def owned(inv_ref):
    held=inv_ref[lax.axis_index("wide")*lax.axis_size("narrow")+lax.axis_index("narrow")]
    return jnp.where(held<0,0,jnp.where(held==MATS,2,1))

def fetch_grad(kind, q_ref, grad):
    big=grad.shape[0]
    @pl.when(kind==1)
    def _():
        grad[...]=jnp.zeros_like(grad)
        for i in range(big//32):
            grad[16*i:16*i+16]=q_ref[32*i:32*i+16]
    @pl.when(kind==2)
    def _():
        grad[...]=q_ref[...]

def copies(srcs,dsts,sems):
    return [pltpu.make_async_copy(a,b,sems.at[i]) for i,(a,b) in enumerate(zip(srcs,dsts))]

def update_body(inv_ref, q_ref, *refs):
    ins_hbm=refs[0:4]; outs_hbm=refs[4:6]; send_o=refs[6]
    ins=refs[7:11]; outs=refs[11:13]
    grad,update,in_sem,out_sem=refs[13:]
    first,second,left,right=ins
    kind=owned(inv_ref)
    c=right.shape[1]; big=left.shape[1]
    ndev=send_o.shape[0]
    copies_in=copies([h.at[0] for h in ins_hbm],ins,in_sem)
    copies_out=copies(outs,[h.at[0] for h in outs_hbm],out_sem)
    for cp in copies_in: cp.start()
    fetch_grad(kind,q_ref,grad)
    for cp in copies_in: cp.wait()
    @pl.when(kind==0)
    def _():
        for o in outs: o[...]=jnp.zeros_like(o)
        send_o[...]=jnp.zeros_like(send_o)
    @pl.when(kind>0)
    def _():
        L=left[...]; Rb=right[...]
        corr=1.0-0.5**STEP
        turned=dot3(dot2(L,grad[...],0,0),Rb,1,0)
        inside=lax.broadcasted_iota(jnp.int32,(big,c),0)<kind*c
        moment=jnp.where(inside,0.5*first[...]+0.5*turned,0.0)
        sec=jnp.where(inside,0.5*second[...]+0.5*turned*turned,0.0)
        outs[0][...]=moment; outs[1][...]=sec
        direction=moment/corr/(jnp.sqrt(sec/corr)+adam_eps)
        update[...]=dot3(dot3(L,direction,1,0),Rb,1,1)
    for cp in copies_out: cp.start()
    for size,number in ((c,1),(big,2)):
        @pl.when(kind==number)
        def _():
            r=size//ndev
            for d in range(ndev):
                u=update[r*d:r*d+r]
                if r<16: u=jnp.concatenate([u,jnp.zeros((16-r,c),F32)],axis=0)
                send_o[d]=u.astype(BF)
    for cp in copies_out: cp.wait()

def basis_body(inv_ref, q_ref, *refs):
    ins_hbm=refs[0:4]; outs_hbm=refs[4:8]
    ins=refs[8:12]; outs=refs[12:16]
    grad,g_l,g_r,in_sem,out_sem=refs[16:]
    left,right,lstat,rstat=ins
    left_o,right_o,lstat_o,rstat_o=outs
    kind=owned(inv_ref)
    c=right.shape[1]; big=left.shape[1]
    copies_in=copies([h.at[0] for h in ins_hbm],ins,in_sem)
    copies_out=copies(outs,[h.at[0] for h in outs_hbm],out_sem)
    for cp in copies_in: cp.start()
    fetch_grad(kind,q_ref,grad)
    for cp in copies_in: cp.wait()
    @pl.when(kind==0)
    def _():
        for o in outs: o[...]=jnp.zeros_like(o)
        for cp in copies_out: cp.start()
    @pl.when(kind>0)
    def _():
        g=grad[...]
        ls=0.95*lstat[...]+0.05*bdot(g,g,1,1)
        rs=0.95*rstat[...]+0.05*bdot(g,g,0,0)
        lstat_o[...]=ls; rstat_o[...]=rs
        for cp in copies_out[2:]: cp.start()
        ar=nn(rs,right[...])
        right_o[...]=ar
        g_r[...]=tn(ar,ar)
        al=nn(ls,left[...])
        left_o[...]=al
        row=lax.broadcasted_iota(jnp.int32,(big,big),0)
        unit=(row==lax.broadcasted_iota(jnp.int32,(big,big),1))&(row>=kind*c)
        g_l[...]=tn(al,al)+jnp.where(unit,1.0,0.0)
        factor_both(left_o,g_l,right_o,g_r)
        for cp in copies_out[:2]: cp.start()
    for cp in copies_out: cp.wait()

def owner_call(body,name,inv,q,ins,outs,extra_out,scratch,cost):
    sd=lambda a: jax.ShapeDtypeStruct(a.shape,F32)
    buf=lambda a: pltpu.VMEM(a.shape[1:],F32)
    dma=pltpu.SemaphoreType.DMA
    return pl.pallas_call(body,
        in_specs=[SMEM,VMEM]+[ANY]*len(ins),
        out_specs=[ANY]*len(outs)+[VMEM]*len(extra_out),
        out_shape=[sd(a) for a in outs]+extra_out,
        scratch_shapes=[buf(a) for a in ins]+[buf(a) for a in outs]+scratch+[dma((len(ins),)),dma((len(outs),))],
        compiler_params=pltpu.CompilerParams(vmem_limit_bytes=LIMIT),
        cost_estimate=pl.CostEstimate(flops=cost,bytes_accessed=4<<20,transcendentals=0),
        name=name)(inv,q,*ins)

def owner_update(inv,q,first,second,left,right,ndev):
    c=right.shape[1]; big=left.shape[1]
    return owner_call(update_body,"owner_update",inv,q,(first,second,left,right),(first,second),
        [jax.ShapeDtypeStruct((ndev,16,c),BF)],[pltpu.VMEM((big,c),BF),pltpu.VMEM((big,c),F32)],4*10**9)

def owner_basis(inv,q,left,right,lstat,rstat):
    c=right.shape[1]; big=left.shape[1]
    slots=(left,right,lstat,rstat)
    return owner_call(basis_body,"owner_basis",inv,q,slots,slots,[],
        [pltpu.VMEM((big,c),BF),pltpu.VMEM((big,big),F32),pltpu.VMEM((c,c),F32)],3*10**10)

def place():
    w,n=lax.axis_index("wide"),lax.axis_index("narrow")
    return lax.div(w,2),lax.rem(w,2),lax.div(n,2),lax.rem(n,2)

def device(z,y,x,core):
    return (z*2+y,x*2+core)

def chip_of(z,y,x):
    return (z*2+y)*2+x

def greet(partners):
    barrier=pltpu.get_barrier_semaphore()
    count=0
    for dev,cond in partners:
        if cond is None:
            pl.semaphore_signal(barrier,inc=1,device_id=dev,device_id_type=MESH)
            count=count+1
        else:
            @pl.when(cond)
            def _():
                pl.semaphore_signal(barrier,inc=1,device_id=dev,device_id_type=MESH)
            count=count+jnp.where(cond,1,0)
    pl.semaphore_wait(barrier,count)

def remote(src,dst,send,recv,dev):
    return pltpu.make_async_remote_copy(src_ref=src,dst_ref=dst,send_sem=send,recv_sem=recv,device_id=dev,device_id_type=MESH)

GATHER=MATS+4
SHARE=GATHER//2
CUT=(SHARE+1)//2

def gather_body(depth, conv_ref, dense_ref, attn_ref, vec_ref, w_ref, part, vbuf,
                pair_s, pair_r, line_r, own_r, twin_r, up_s, down_s, x_s, y_s, twin_s):
    z,y,x,core=place()
    me=chip_of(z,y,x)
    rank=me*2+core
    c=w_ref.shape[-1]
    twin=device(z,y,x,1-core)
    side_x,side_y=device(z,y,1-x,core),device(z,1-y,x,core)
    above,below=device(z+1,y,x,core),device(z-1,y,x,core)
    greet([(twin,None),(side_x,None),(side_y,None),(below,z>0),(above,z<depth-1)])
    conv=conv_ref.shape[0]
    part[0,0:conv]=conv_ref[...]
    part[0,conv:MATS]=attn_ref[...]
    part[0,MATS]=dense_ref[0:8]
    part[0,MATS+1]=dense_ref[8:16]
    cols,rows_v=vec_ref.shape
    vbuf[...]=jnp.zeros_like(vbuf)
    vbuf[0:cols,0:rows_v]=vec_ref[...]
    turned=vbuf[0:8,0:128].T[0:16]
    vbuf[...]=jnp.zeros_like(vbuf)
    vbuf[:,0:8]=turned
    mine=pltpu.roll(vbuf[...],rank*cols,1)
    part[0,MATS+2]=mine[0:8]
    part[0,MATS+3]=mine[8:16]
    swap=remote(part.at[0],part.at[1],pair_s,pair_r,twin)
    swap.start()
    swap.wait()
    even,odd=core,1-core
    join=lambda a,b: jnp.concatenate([a,b],axis=0).astype(BF)
    def fill(m,value):
        @pl.when(core==m//SHARE)
        def _(): w_ref[m,z,y,x]=value()
    for k in range(2):
        @pl.when(core==k)
        def _():
            for m in range(k*SHARE,min((k+1)*SHARE,MATS)):
                w_ref[m,z,y,x]=join(part[even,m],part[odd,m])
    for h,src in ((0,even),(1,odd)):
        fill(MATS+h,lambda: join(part[src,MATS],part[src,MATS+1]))
    fill(MATS+2,lambda: join(part[0,MATS+2]+part[1,MATS+2],part[0,MATS+3]+part[1,MATS+3]))
    fill(MATS+3,lambda: jnp.zeros((16,c),BF))

    def mats(h,whose=core):
        return pl.ds(SHARE*whose+(0,CUT)[h],(CUT,SHARE-CUT)[h])
    every=pl.ds(SHARE*core,SHARE)
    def same(at,send,recv,dev):
        return remote(w_ref.at[at],w_ref.at[at],send,recv,dev)
    def to_up(zz): return same((every,zz,y,x),up_s.at[zz],line_r.at[zz],above)
    def to_down(zz): return same((every,zz,y,x),down_s.at[zz],line_r.at[zz],below)
    def first(h,zz):
        at=(mats(h),zz,y,x)
        return (same(at,x_s.at[0,zz],own_r.at[0,0,zz],side_x),same(at,y_s.at[0,zz],own_r.at[1,0,zz],side_y))[h]
    def second(h,zz):
        return (same((mats(0),zz,y),y_s.at[1,zz],own_r.at[0,1,zz],side_y),
                same((mats(1),zz,slice(None),x),x_s.at[1,zz],own_r.at[1,1,zz],side_x))[h]
    def line(zz,up,down):
        if up or down:
            same((every,zz,y,x),up_s.at[zz],line_r.at[zz],twin).wait_recv()
        if up is not False:
            @pl.when(z<depth-1)
            def _(): to_up(zz).start()
        if down is not False:
            @pl.when(z>0)
            def _(): to_down(zz).start()
        for h in range(2): first(h,zz).start()
    def sides(zz):
        same((mats(0),zz,y,1-x),x_s.at[0,zz],own_r.at[0,0,zz],side_x).wait_recv()
        second(0,zz).start()
        same((mats(1),zz,1-y,x),y_s.at[0,zz],own_r.at[1,0,zz],side_y).wait_recv()
        second(1,zz).start()
    def both(d,run):
        for zz,up in ((z-d,True),(z+d,False)):
            @pl.when((zz>=0)&(zz<depth))
            def _(): run(zz,up)
    line(z,None,None)
    for d in range(1,depth+1):
        if d<depth:
            both(d,lambda zz,up: line(zz,up,not up))
        if d==1: sides(z)
        else: both(d-1,lambda zz,up: sides(zz))
    for h in range(2):
        for zz in range(depth):
            at=((mats(0),zz,1-y),(mats(1),zz,slice(None),1-x))[h]
            same(at,twin_s.at[h],own_r.at[h,1,zz],twin).wait_recv()
        same((mats(h),),twin_s.at[h],twin_r.at[h],twin).start()
    for h in range(2):
        same((mats(h,1-core),),twin_s.at[h],twin_r.at[h],twin).wait_recv()
    for h in range(2):
        same((mats(h),),twin_s.at[h],twin_r.at[h],twin).wait_send()
        for zz in range(depth):
            first(h,zz).wait_send(); second(h,zz).wait_send()
    for zz in range(depth):
        @pl.when((z<depth-1)&(zz<=z))
        def _(): to_up(zz).wait_send()
        @pl.when((z>0)&(zz>=z))
        def _(): to_down(zz).wait_send()

def gather_weights(conv,dense,attn,vec,depth):
    c=conv.shape[2]
    dma=pltpu.SemaphoreType.DMA
    line=dma((depth,))
    return pl.pallas_call(functools.partial(gather_body,depth),
        out_shape=jax.ShapeDtypeStruct((GATHER,depth,2,2,16,c),BF),
        in_specs=[VMEM]*4,out_specs=VMEM,
        scratch_shapes=[pltpu.VMEM((2,GATHER,8,c),F32),pltpu.VMEM((16,c),F32),dma,dma,line,dma((2,2,depth)),dma((2,)),line,line,
          dma((2,depth)),dma((2,depth)),dma((2,))],
        compiler_params=pltpu.CompilerParams(collective_id=0,has_side_effects=True,vmem_limit_bytes=LIMIT),
        name="gather_weights")(conv,dense,attn,vec).reshape(GATHER,c,c)

REDUCE=MATS+2
HALF=REDUCE//2
PARTS=((0,3,"xyz"),(3,2,"yzx"),(5,1,"zxy"),(6,2,"xyz"),(8,2,"yzx"),(10,2,"zxy"))

def reduce_body(depth, inv_ref, g_ref, v_ref, q_ref, vec_o, acc, core_in, *rest):
    bufs=tuple(zip(*[iter(rest[:3*len(PARTS)])]*3))
    (final, pick, vsend, vrecv, core_s, core_r, ex_s, ex_r, z_s, z_r, twin_s, twin_r, out_s, out_r, v_s, v_r)=rest[3*len(PARTS):]
    z,y,x,core=place()
    me=chip_of(z,y,x)
    chips=depth*4
    twin=device(z,y,x,1-core)
    def of_chip(o):
        return device(lax.div(o,4),lax.rem(lax.div(o,2),2),lax.rem(o,2),core)
    others=[lax.rem(me+k,chips) for k in range(1,chips)]
    greet([(twin,None)]+[(of_chip(o),None) for o in others])
    c=g_ref.shape[2]
    pair=[]
    for i,(m0,n,_) in enumerate(PARTS):
        cp=remote(g_ref.at[pl.ds(HALF*(1-core)+m0,n)],core_in.at[m0:m0+n],core_s.at[i],core_r.at[i],twin)
        cp.start(); pair.append(cp)
    def vec_start(stage,dev):
        cp=remote(vsend.at[stage],vrecv.at[stage],v_s.at[stage],v_r.at[stage],dev)
        cp.start()
        return cp
    def vec_end(stage,cp):
        cp.wait()
        total=vsend[stage]+vrecv[stage]
        if stage<4: vsend[stage+1]=total
        else: vec_o[...]=total
    vsend[0]=v_ref[...]
    vcp=vec_start(0,twin)
    nbr_x,nbr_y=device(z,y,1-x,core),device(z,1-y,x,core)
    started={}
    def where(i,done):
        return ["z" in done and z, "y" in done and y, "x" in done and x]
    def index(m,place):
        return tuple([m]+[slice(None) if p is False else p for p in place])
    def swap_start(i,stage):
        m0,n,order=PARTS[i]
        axis=order[stage]
        at=where(i,order[:stage])
        at["zyx".index(axis)]=1-(x if axis=="x" else y)
        dst=bufs[i][0 if axis=="x" else 1]
        k=0 if axis=="x" else 1
        cp=remote(acc.at[index(slice(m0,m0+n),at)],dst,ex_s.at[i,k],ex_r.at[i,k],nbr_x if axis=="x" else nbr_y)
        cp.start()
        started[i,stage]=cp
    def swap_end(i,stage):
        m0,n,order=PARTS[i]
        axis=order[stage]
        started.pop((i,stage)).wait()
        at=where(i,order[:stage+1])
        src=bufs[i][0 if axis=="x" else 1]
        @pl.loop(0,n)
        def _(m):
            there=index(m0+m,at)
            acc[there]=(acc[there].astype(F32)+src[m].astype(F32)).astype(BF)
    def z_copy(i,stage,k):
        m0,n,order=PARTS[i]
        zz=lax.rem(z+k,depth)
        at=where(i,order[:stage])
        at[0]=zz
        return remote(acc.at[index(slice(m0,m0+n),at)],bufs[i][2].at[z],z_s.at[i,k],z_r.at[i,z],device(zz,y,x,core))
    def z_start(i,stage):
        for k in range(1,depth):
            z_copy(i,stage,k).start()
    def z_end(i,stage):
        m0,n,order=PARTS[i]
        src=bufs[i][2]
        at=where(i,order[:stage+1])
        for k in range(1,depth):
            zz=lax.rem(z+k,depth)
            remote(src.at[zz],src.at[zz],z_s.at[i,k],z_r.at[i,zz],twin).wait_recv()
        @pl.loop(0,n)
        def _(m):
            there=index(m0+m,at)
            total=acc[there].astype(F32)
            for k in range(1,depth):
                total=total+src[lax.rem(z+k,depth),m].astype(F32)
            acc[there]=total.astype(BF)
        for k in range(1,depth):
            z_copy(i,stage,k).wait_send()

    def add_pair(i):
        m0,n,_=PARTS[i]
        pair[i].wait()
        @pl.loop(0,n)
        def _(m):
            s=(g_ref[HALF*core+m0+m].astype(F32)+core_in[m0+m].astype(F32)).astype(BF)
            acc[m0+m]=s.reshape(acc.shape[1:])
    groups=range(0,len(PARTS),3)
    for i in groups:
        add_pair(i+2); z_start(i+2,0)
        add_pair(i); swap_start(i,0)
        add_pair(i+1); swap_start(i+1,0)
    vec_end(0,vcp); vcp=vec_start(1,nbr_x)
    for i in groups:
        swap_end(i,0); swap_start(i,1)
        swap_end(i+1,0); z_start(i+1,1)
        z_end(i+2,0); swap_start(i+2,1)
    vec_end(1,vcp); vcp=vec_start(2,nbr_y)
    for i in groups:
        swap_end(i,1); z_start(i,2)
        swap_end(i+2,1); swap_start(i+2,2)
        z_end(i+1,1); swap_start(i+1,2)
    vec_end(2,vcp); vcp=vec_start(3,device(lax.div(z,2)*2+(1-lax.rem(z,2)),y,x,core))
    for i in groups:
        swap_end(i+2,2)
        swap_end(i+1,2)
        z_end(i,2)
    vec_end(3,vcp); vcp=vec_start(4,device(lax.rem(z+2,4),y,x,core))
    there=pl.ds(HALF*core,HALF)
    for m in range(HALF):
        final[HALF*core+m]=acc[m,z,y,x]
    cp=remote(final.at[there],final.at[there],twin_s,twin_r,twin)
    cp.start(); cp.wait()
    for k in range(chips):
        o=me if k==0 else others[k-1]
        m=jnp.maximum(inv_ref[o*2+core],0)
        pick[k,0]=final[m]
        pick[k,1]=final[REDUCE-1]
        if k:
            remote(pick.at[k],q_ref.at[me],out_s.at[k],out_r.at[me],of_chip(o)).start()
    q_ref[me]=pick[0]
    vec_end(4,vcp)
    for k in range(1,chips):
        o=others[k-1]
        remote(pick.at[k],q_ref.at[o],out_s.at[k],out_r.at[o],of_chip(o)).wait()

def reduce_grads(inv,grads,vec,depth):
    c=grads.shape[2]
    chips=depth*4
    dma=pltpu.SemaphoreType.DMA
    vm=lambda *s: pltpu.VMEM(s,BF)
    bufs=[]
    for _,n,order in PARTS:
        left={"z":depth,"y":2,"x":2}
        shapes={}
        for axis in order:
            del left[axis]
            shapes[axis]=tuple(left[k] for k in "zyx" if k in left)
        bufs+=[vm(n,*shapes["x"],16,c),vm(n,*shapes["y"],16,c),vm(depth,n,*shapes["z"],16,c)]
    return pl.pallas_call(functools.partial(reduce_body,depth),
        out_shape=[jax.ShapeDtypeStruct((chips,2,16,c),BF),jax.ShapeDtypeStruct(vec.shape,F32)],
        in_specs=[SMEM,VMEM,VMEM],out_specs=[VMEM,VMEM],
        scratch_shapes=[vm(HALF,depth,2,2,16,c),vm(HALF,c,c)]+bufs+[vm(REDUCE,16,c),vm(chips,2,16,c),
          pltpu.VMEM((5,)+vec.shape,F32),pltpu.VMEM((5,)+vec.shape,F32),
          dma((len(PARTS),)),dma((len(PARTS),)),dma((len(PARTS),2)),dma((len(PARTS),2)),dma((len(PARTS),depth)),dma((len(PARTS),depth)),dma,dma,
          dma((chips,)),dma((chips,)),dma((5,)),dma((5,))],
        compiler_params=pltpu.CompilerParams(collective_id=1,has_side_effects=True,vmem_limit_bytes=LIMIT),
        name="reduce_grads")(inv,grads,vec)

def deal_body(ndev, send_ref, out_ref, s_sem, r_sem):
    w,n=lax.axis_index("wide"),lax.axis_index("narrow")
    width=lax.axis_size("narrow")
    me=w*width+n
    dev=lambda d: (lax.div(d,width),lax.rem(d,width))
    others=[lax.rem(me+k,ndev) for k in range(1,ndev)]
    greet([(dev(d),None) for d in others])
    def copy(k):
        d=others[k]
        return remote(send_ref.at[d],out_ref.at[me],s_sem.at[k],r_sem.at[me],dev(d))
    for k in range(ndev-1): copy(k).start()
    out_ref[me]=send_ref[me]
    for k in range(ndev-1):
        d=others[k]
        remote(send_ref.at[d],out_ref.at[d],s_sem.at[k],r_sem.at[d],dev(d)).wait()

def deal_updates(send):
    ndev=send.shape[0]
    dma=pltpu.SemaphoreType.DMA
    return pl.pallas_call(functools.partial(deal_body,ndev),
        out_shape=jax.ShapeDtypeStruct(send.shape,send.dtype),
        in_specs=[VMEM],out_specs=VMEM,
        scratch_shapes=[dma((ndev,)),dma((ndev,))],
        compiler_params=pltpu.CompilerParams(collective_id=2,has_side_effects=True,vmem_limit_bytes=LIMIT),
        name="deal_updates")(send)

def weights_body(owners_ref, upd_ref, conv_ref, dense_ref, attn_ref, vm_ref, v1_ref, v2_ref, gv_ref,
                 conv_o, dense_o, attn_o, vec_o, convc_o, densec_o, attnc_o, vecc_o, v1_o, v2_o):
    me=lax.axis_index("wide")*lax.axis_size("narrow")+lax.axis_index("narrow")
    c=dense_ref.shape[1]
    def new(master,number,fan):
        u=upd_ref[owners_ref[number]].astype(F32)[0:master.shape[0]]
        return master-fan**-0.5*(u+0.01*master)
    for k in range(conv_ref.shape[0]):
        v=new(conv_ref[k],k+(k>=9),9*c)
        conv_o[k]=v; convc_o[k]=v.astype(BF)
    v=new(dense_ref[...],9,dense_ref.shape[0]*lax.axis_size("wide")*lax.axis_size("narrow"))
    dense_o[...]=v; densec_o[...]=v.astype(BF)
    for k in range(4):
        v=new(attn_ref[k],19+k,c)
        attn_o[k]=v; attnc_o[k]=v.astype(BF)
    cols,rows=vm_ref.shape
    g=pltpu.roll(gv_ref[...],lax.rem(c-me*cols,c),1)[:,0:128].T[0:cols,0:rows]
    corr=1.0-0.5**STEP
    f=0.5*v1_ref[...]+0.5*g
    s=0.5*v2_ref[...]+0.5*g*g
    v=vm_ref[...]-0.2*(f/corr)/(jnp.sqrt(s/corr)+adam_eps)
    vec_o[...]=v; vecc_o[...]=v.astype(BF)
    v1_o[...]=f; v2_o[...]=s

def new_weights(owners,upd,conv,dense,attn,vm,v1,v2,gvec):
    sd=jax.ShapeDtypeStruct
    mains=(conv,dense,attn,vm)
    return pl.pallas_call(weights_body,
        out_shape=[sd(a.shape,F32) for a in mains]+[sd(a.shape,BF) for a in mains]+[sd(v1.shape,F32)]*2,
        in_specs=[SMEM]+[VMEM]*8,out_specs=[VMEM]*10,
        compiler_params=pltpu.CompilerParams(vmem_limit_bytes=LIMIT),
        name="new_weights")(owners,upd,conv,dense,attn,vm,v1,v2,gvec)

def step(depth, images, time_embed, out_cotangent, conv_master, dense_master, attn_master, vector_master, vector_first, vector_second,
         owners, slot_first, slot_second, slot_left_basis, slot_right_basis, slot_left_stat, slot_right_stat):
    batch,side,_,c=images.shape
    ndev=lax.axis_size("wide")*lax.axis_size("narrow")
    flat=lambda a: a.reshape(batch,side*side,c)
    conv=conv_master.reshape((-1,)+conv_master.shape[2:])
    vector,vector_first,vector_second=vector_master.T,vector_first.T,vector_second.T
    if depth:
        w=gather_weights(conv,dense_master,attn_master,vector,depth)
    else:
        gather=lambda a,axis: lax.all_gather(a.astype(BF),AXES,axis=axis,tiled=True)
        dense=jnp.swapaxes(gather(dense_master,0).reshape(c//16,2,16,c),0,1).reshape(2,c,c)
        vec=jnp.pad(gather(vector_master,1),((0,c-vector_master.shape[0]),(0,0)))
        w=jnp.concatenate([gather(conv,1),gather(attn_master,1),dense,vec[None],jnp.zeros((1,c,c),BF)])
    act,igrad,tgrad,grads,gvec,inv=train_images(owners,flat(images),flat(out_cotangent),time_embed,w,side,ndev)
    if depth:
        q,gvec=reduce_grads(inv,grads,gvec,depth)
        q=q.reshape(-1,c)
    else:
        total=lax.optimization_barrier(lax.psum(grads.astype(F32),AXES)).astype(BF)
        gvec=lax.psum(gvec,AXES)
        held=inv[lax.axis_index(AXES)]
        q=jnp.stack([total[jnp.maximum(held,0)].reshape(c//16,16,c),total[MATS+1].reshape(c//16,16,c)],axis=1).reshape(-1,c)
    first_slot,second_slot,send=owner_update(inv,q,slot_first,slot_second,slot_left_basis,slot_right_basis,ndev)
    upd=deal_updates(send) if depth and DEAL else lax.all_to_all(send,AXES,0,0,tiled=True)
    slots=[first_slot,second_slot]+list(owner_basis(inv,q,slot_left_basis,slot_right_basis,slot_left_stat,slot_right_stat))
    new=new_weights(owners,upd,conv,dense_master,attn_master,vector,vector_first,vector_second,gvec)
    conv_new,dense_new,attn_new,vec_new,conv_copy,dense_copy,attn_copy,vec_copy,first_new,second_new=new
    return (act.reshape(images.shape),igrad.reshape(images.shape),tgrad,conv_new.reshape(conv_master.shape),dense_new,attn_new,vec_new.T,
            conv_copy.reshape(conv_master.shape),dense_copy,attn_copy,vec_copy.T,first_new.T,second_new.T,*slots)

def solution(mesh):
    rows,both=P(AXES),P(None,AXES)
    taps=P(None,None,AXES)
    depth=4 if (mesh.shape["wide"],mesh.shape["narrow"])==(8,4) else 0
    return jax.shard_map(functools.partial(step,depth),mesh=mesh,
        in_specs=(rows,rows,rows,taps,rows,both,both,both,both,P())+(rows,)*6,
        out_specs=(rows,rows,rows,taps,rows,both,both,taps,rows,both,both,both,both)+(rows,)*6,
        check_vma=False)
```

```python
import functools

import jax
import jax.numpy as jnp
from jax import lax
from jax.experimental import pallas as pl
from jax.experimental.pallas import tpu as pltpu
from jax.sharding import PartitionSpec as P

BF = jnp.bfloat16
F32 = jnp.float32
STEP = 10
GROUP = 8
BLK = 128
ROWS = 256
half_root = 0.5**0.5
norm_eps = 1e-6
adam_eps = 1e-8
HI = lax.Precision.HIGHEST
MESH = pl.DeviceIdType.MESH
AXES = ("wide", "narrow")
MATS = 22
VMEM = pl.BlockSpec(memory_space=pltpu.VMEM)
SMEM = pl.BlockSpec(memory_space=pltpu.SMEM)
ANY = pl.BlockSpec(memory_space=pl.ANY)
LIMIT = 56 << 20
TOGETHER = 6
DEAL = False

def mm(a,b):
    return lax.dot_general(a,b,(((1,),(0,)),((),())),preferred_element_type=F32)
def mm_nt(a,b):
    return lax.dot_general(a,b,(((1,),(1,)),((),())),preferred_element_type=F32)
def mm_tn(a,b):
    return lax.dot_general(a,b,(((0,),(0,)),((),())),preferred_element_type=F32)

def group_sum(v):
    lane=lax.broadcasted_iota(jnp.int32, v.shape, 1)
    n=v.shape[1]
    for s in (1,2,4):
        v=v+jnp.where((lane & s)==0, pltpu.roll(v,n-s,1), pltpu.roll(v,s,1))
    return v

def col_sum(v):
    return jnp.sum(v,axis=0,keepdims=True)

def pad8(v):
    return jnp.broadcast_to(v,(8,v.shape[1]))

def group_mean(colsum, count):
    return group_sum(pad8(colsum))[0:1]*(1.0/count)

def normal_form(v):
    count=v.shape[0]*GROUP
    m=group_mean(col_sum(v),count)
    yield
    c=v-m
    var=group_mean(col_sum(c*c),count)
    yield
    r=lax.rsqrt(var+norm_eps)
    return c*r, r

def norm_back(grad, xhat, r, gain):
    count=grad.shape[0]*GROUP
    shift_grad=col_sum(grad)
    gain_grad=col_sum(grad*xhat)
    m1=group_mean(shift_grad*gain,count)
    m2=group_mean(gain_grad*gain,count)
    yield
    return (grad*(gain*r)-(m1*r)-xhat*(m2*r)), gain_grad, shift_grad

def sigmoid(y):
    return pl.reciprocal(1.0+jnp.exp(-y),approx=True)

def spread(ref, i, v, side):
    tokens, c = v.shape
    parts=v.reshape(tokens//16,2,8,c)
    low,high=parts[:,0],parts[:,1]
    at=lax.broadcasted_iota(jnp.int32,low.shape,1)
    whole=lambda a,b: jnp.stack([a,b],axis=1).reshape(tokens,c).astype(BF)
    l,h=pltpu.roll(low,1,1),pltpu.roll(high,1,1)
    ref[i,side:side+tokens,0:c]=whole(jnp.where(at==0,0.0,l),jnp.where(at==0,l,h))
    ref[i,side:side+tokens,c:2*c]=v.astype(BF)
    l,h=pltpu.roll(low,7,1),pltpu.roll(high,7,1)
    ref[i,side:side+tokens,2*c:3*c]=whole(jnp.where(at==7,h,l),jnp.where(at==7,0.0,h))

def taps(ref, count, dy, tokens, side):
    return jnp.concatenate([ref[i,side*dy:side*dy+tokens,:] for i in range(count)],axis=0)

def train_body(side, owners_ref, img_ref, cot_ref, emb_ref, w_ref,
         act_ref, igrad_ref, tgrad_ref, gw_ref, gvec_ref, inv_ref,
         dense_ref, vec_ref, wt, acc, gvec, proj, pgrad, p1, p2, s2, s1):
    step=pl.program_id(0); steps=pl.num_programs(0)
    ib,tokens,c=img_ref.shape
    batch=emb_ref.shape[0]
    scale=c**-0.5

    @pl.when(step==0)
    def _():
        acc[...]=jnp.zeros_like(acc)
        gvec[...]=jnp.zeros_like(gvec)
        pgrad[...]=jnp.zeros_like(pgrad)
        for ref in (p1,p2,s2,s1):
            for i in range(ib):
                z=jnp.zeros((side,3*c),BF)
                ref[i,0:side,:]=z
                ref[i,side+tokens:2*side+tokens,:]=z
        for k in range(2):
            for t in range(9):
                wt[k, 8-t]=w_ref[9*k+t].T
        chips=c//16
        total=jnp.zeros((16,c),F32)
        for o in range(chips):
            total=total+w_ref[24,16*o:16*o+16].astype(F32)
            for h in range(2):
                dense_ref[32*o+16*h:32*o+16*h+16]=w_ref[22+h,16*o:16*o+16]
        vec_ref[...]=total
        for d in range(inv_ref.shape[0]):
            inv_ref[d]=-1
        for m in range(owners_ref.shape[0]):
            inv_ref[owners_ref[m]]=m if m<9 else MATS if m==9 else m-1
        e=emb_ref[...].astype(F32)
        proj[0:batch]=mm((e*sigmoid(e)).astype(BF),dense_ref[...])+total[7:8]

    vec=vec_ref[...]
    row=lambda k: vec[k:k+1]

    up=lambda t: t.astype(F32)
    sums={}
    def add(kk,val):
        sums[kk]=val if kk not in sums else sums[kk]+val
    def three(ref,k,dy):
        return jnp.concatenate([ref[k+3*dy+dx] for dx in range(3)],axis=0)
    def conv(ref,i,weight):
        out=mm(jnp.concatenate([ref[i,side*dy:side*dy+tokens,:] for dy in range(3)],axis=1),jnp.concatenate([weight(dy) for dy in range(3)],axis=0))
        yield
        return out
    def wgrad(base,aref,gref,i):
        at=aref[i,side:side+tokens,c:2*c].T
        for dy in range(3):
            g=mm(at,gref[i,side*dy:side*dy+tokens,:])
            for dx in range(3):
                acc[base+8-(3*dy+dx)]+=g[:,dx*c:(dx+1)*c]
            yield
    def swish_back(grad,h,gain,shift):
        y=h*gain+shift
        s=sigmoid(y)
        return grad*(s*(1.0+y*(1.0-s)))

    def image(i):
        x=img_ref[i].astype(F32)
        h0,r0=yield from normal_form(x)
        y=h0*row(0)+row(3)
        spread(p1,i,y*sigmoid(y),side)
        yield
        t=yield from conv(p1,i,lambda dy: three(w_ref,0,dy))
        t=t+(row(6)+proj[pl.ds(step*ib+i,1),:])
        h1,r1=yield from normal_form(t)
        y=h1*row(1)+row(4)
        spread(p2,i,y*sigmoid(y),side)
        yield
        t=yield from conv(p2,i,lambda dy: three(w_ref,9,dy))
        mid=(x+(t+row(8)))*half_root
        h2,r2=yield from normal_form(mid)
        normed=(h2*row(2)+row(5)).astype(BF)
        yield
        q=(mm(normed,w_ref[18])+row(9)).astype(BF)
        k=mm(normed,w_ref[19]).astype(BF)
        yield
        v=(mm(normed,w_ref[20])+row(10)).astype(BF)
        sc=mm_nt(q,k)*scale
        yield
        e=jnp.exp(sc-jnp.max(sc,axis=1,keepdims=True))
        a=e*pl.reciprocal(jnp.sum(e,axis=1,keepdims=True),approx=True)
        low=a.astype(BF)
        yield
        mixed=mm(low,v).astype(BF)
        cot=cot_ref[i].astype(F32)*half_root
        bg=cot.astype(BF)
        mg=mm_nt(bg,w_ref[21]).astype(BF)
        add(11,col_sum(up(bg)))
        yield
        branch=mm(mixed,w_ref[21])+row(11)
        pg=mm_nt(mg,v)
        act_ref[i]=((mid+branch)*half_root).astype(BF)
        yield
        sg=(a*(pg-jnp.sum(a*pg,axis=1,keepdims=True))).astype(BF)
        acc[21]+=mm_tn(mixed,bg)
        vg=mm_tn(low,mg).astype(BF)
        yield
        qg=(mm(sg,k)*scale).astype(BF)
        kg=(mm_tn(sg,q)*scale).astype(BF)
        yield
        ng=mm_nt(qg,w_ref[18])+mm_nt(kg,w_ref[19])+mm_nt(vg,w_ref[20])
        yield
        normed_t=normed.T
        acc[18]+=mm(normed_t,qg)
        acc[19]+=mm(normed_t,kg)
        acc[20]+=mm(normed_t,vg)
        add(9,col_sum(up(qg)));add(10,col_sum(up(vg)))
        yield
        d,gg,gs=yield from norm_back(ng,h2,r2,row(2))
        add(2,gg);add(5,gs)
        midg=cot+d
        g=up((midg*half_root).astype(BF))
        add(8,col_sum(g))
        spread(s2,i,g,side)
        yield
        ag=yield from conv(s2,i,lambda dy: three(wt.at[1],0,dy))
        d=swish_back(ag,h1,row(1),row(4))
        yield
        yield from wgrad(9,p2,s2,i)
        d,gg,gs=yield from norm_back(d,h1,r1,row(1))
        add(1,gg);add(4,gs)
        g=up(d.astype(BF))
        s=col_sum(g)
        add(6,s)
        pgr=up(s.astype(BF))
        pgrad[pl.ds(step*ib+i,1),:]=pgr
        add(7,pgr)
        spread(s1,i,g,side)
        yield
        ag=yield from conv(s1,i,lambda dy: three(wt.at[0],0,dy))
        d=swish_back(ag,h0,row(0),row(3))
        yield
        yield from wgrad(0,p1,s1,i)
        d,gg,gs=yield from norm_back(d,h0,r0,row(0))
        add(0,gg);add(3,gs)
        igrad_ref[i]=midg*half_root+d

    def run(count):
        sums.clear()
        live=[image(i) for i in range(count)]
        while live:
            for g in list(live):
                try: next(g)
                except StopIteration: live.remove(g)
        gvec[0:12]+=jnp.concatenate([sums[j] for j in range(12)],axis=0)
    rest=batch-ib*(-(-batch//ib)-1)
    if rest==ib: run(ib)
    else:
        @pl.when(step<steps-1)
        def _(): run(ib)
        @pl.when(step==steps-1)
        def _(): run(rest)

    @pl.when(step==steps-1)
    def _():
        for m in range(acc.shape[0]):
            gw_ref[m]=acc[m].astype(BF)
        gvec_ref[...]=gvec[...]
        e=emb_ref[...].astype(F32)
        s=sigmoid(e)
        ea=(e*s).astype(BF)
        pg=pgrad[0:batch].astype(BF)
        tgrad_ref[...]=mm_nt(pg,dense_ref[...])*(s*(1.0+e*(1.0-s)))
        gd=mm_tn(ea,pg).astype(BF)
        for o in range(c//16):
            for h in range(2):
                gw_ref[22+h,16*o:16*o+16]=gd[32*o+16*h:32*o+16*h+16]

def train_images(owners,images,cot,embed,w,side,ndev):
    batch,tokens,c=images.shape
    emb=embed.shape[1]
    ib=min(TOGETHER,batch)
    rows=-(-batch//8)*8
    whole=lambda a: pl.BlockSpec(a.shape,lambda s: (0,)*len(a.shape))
    blk=pl.BlockSpec((ib,tokens,c),lambda s:(s,0,0))
    sd=jax.ShapeDtypeStruct
    outs=[sd((batch,tokens,c),BF),sd((batch,tokens,c),F32),sd((batch,emb),F32),sd((MATS+2,c,c),BF),sd((16,c),F32)]
    return pl.pallas_call(functools.partial(train_body,side),grid=(-(-batch//ib),),
        in_specs=[SMEM,blk,blk,whole(embed),whole(w)],
        out_specs=[blk,blk]+[whole(o) for o in outs[2:]]+[SMEM],
        out_shape=outs+[sd((ndev,),jnp.int32)],
        scratch_shapes=[pltpu.VMEM((emb,c),BF),pltpu.VMEM((16,c),F32),pltpu.VMEM((2,9,c,c),BF),pltpu.VMEM((MATS,c,c),F32),pltpu.VMEM((16,c),F32),pltpu.VMEM((rows,c),F32),pltpu.VMEM((rows,c),F32)]
          +[pltpu.VMEM((ib,tokens+2*side,3*c),BF)]*4,
        compiler_params=pltpu.CompilerParams(vmem_limit_bytes=LIMIT),
        name="train_images")(owners,images,cot,embed,w)

def fdot(a,b,ca,cb):
    return lax.dot_general(a,b,(((ca,),(cb,)),((),())),precision=HI,preferred_element_type=F32)
nn=lambda a,b: fdot(a,b,1,0)
nt=lambda a,b: fdot(a,b,1,1)
tn=lambda a,b: fdot(a,b,0,0)

def inverse_factors(blocks, tasks):
    tasks=list(tasks)
    share=-(-len(tasks)//14)
    n=BLK
    lane=lax.broadcasted_iota(jnp.int32,(8,n),1)
    sub=lax.broadcasted_iota(jnp.int32,(8,n),0)
    tables=[[b[8*v:8*v+8] for v in range(n//8)] for b in blocks]
    over_lanes=lambda t,j: jnp.broadcast_to(t[:,j:j+1],(8,n))
    over_rows=lambda t,i: jnp.broadcast_to(t[i:i+1],(8,n))
    for J in range(n//8):
        lo=8*J
        in_block=(lane>=lo)&(lane<lo+8)
        for t in tables:
            cur=t[J]
            cols=[over_lanes(cur,lo+j) for j in range(8)]
            m=[[over_rows(cols[j],i) for j in range(i+1)] for i in range(8)]
            R=[jnp.where(in_block,jnp.where(lane==lo+i,1.0,0.0),over_rows(cur,i)) for i in range(8)]
            r=[None]*8
            l=[[None]*8 for _ in range(8)]
            for k in range(8):
                d=m[k][k]
                r[k]=pl.reciprocal(d,approx=True)
                for i in range(k+1,8):
                    l[i][k]=m[i][k]*r[k]
                for i in range(k+1,8):
                    for j in range(k+1,i+1):
                        m[i][j]=m[i][j]-l[i][k]*m[j][k]
                    R[i]=R[i]-l[i][k]*R[k]
            P=[None]*8
            for k in range(7,-1,-1):
                P[k]=R[k]*r[k]
                for i in range(7,k,-1):
                    P[k]=P[k]-l[i][k]*P[i]
            done=R[0]*lax.rsqrt(m[0][0])
            for i in range(1,8):
                done=jnp.where(sub==i,R[i]*lax.rsqrt(m[i][i]),done)
            t[J]=jnp.where(lane<=lo+sub,done,0.0)
            for v in range(J+1,n//8):
                new=jnp.where(in_block,0.0,t[v])
                for k in range(8):
                    new=new-over_lanes(t[v],lo+k)*P[k]
                t[v]=new
        for _ in range(min(share,len(tasks))): tasks.pop(0)()
    return [jnp.concatenate(t,axis=0) for t in tables]

def at(k,size):
    return pl.ds(pl.multiple_of(k*size,size),size)

def split(x):
    hi=x.astype(BF)
    return hi,(x-hi.astype(F32)).astype(BF)

def bdot(a,b,ca,cb):
    return lax.dot_general(a,b,(((ca,),(cb,)),((),())),preferred_element_type=F32)

def dot3(a,b,ca,cb):
    (ah,al),(bh,bl)=split(a),split(b)
    return bdot(ah,bh,ca,cb)+(bdot(ah,bl,ca,cb)+bdot(al,bh,ca,cb))

def dot2(a,b,ca,cb):
    ah,al=split(a)
    return bdot(ah,b,ca,cb)+bdot(al,b,ca,cb)

def factor_both(a_l, g_l, a_r, g_r):
    tasks=[]
    def renew(a,lo,inv,r,rows):
        def task():
            q=dot3(a[rows,lo:lo+BLK],inv,1,1)
            a[rows,lo:lo+BLK]=q
            if r is not None: a[rows,lo+BLK:]=a[rows,lo+BLK:]-dot3(q,r,1,0)
        return task
    def lower(g,r,start,b):
        def task():
            g[b:b+BLK,b:]=g[b:b+BLK,b:]-tn(r[:,b-start:b-start+BLK],r[:,b-start:])
        return task
    for p in range(g_l.shape[0]//BLK):
        lo,hi=p*BLK,(p+1)*BLK
        live=[(a,g) for a,g in ((a_l,g_l),(a_r,g_r)) if g.shape[0]>lo]
        invs=inverse_factors([g[lo:hi,lo:hi] for _,g in live],tasks)
        tasks=[]
        for (a,g),inv in zip(live,invs):
            n=g.shape[0]
            r=None
            if hi<n:
                r=nn(inv,g[lo:hi,hi:])
                lower(g,r,hi,hi)()
                tasks+=[lower(g,r,hi,b) for b in range(hi+BLK,n,BLK)]
            tasks+=[renew(a,lo,inv,r,slice(k,k+ROWS)) for k in range(0,n,ROWS)]
    for task in tasks: task()

def owned(inv_ref):
    held=inv_ref[lax.axis_index("wide")*lax.axis_size("narrow")+lax.axis_index("narrow")]
    return jnp.where(held<0,0,jnp.where(held==MATS,2,1))

def fetch_grad(kind, q_ref, grad):
    big=grad.shape[0]
    @pl.when(kind==1)
    def _():
        grad[...]=jnp.zeros_like(grad)
        for i in range(big//32):
            grad[16*i:16*i+16]=q_ref[32*i:32*i+16]
    @pl.when(kind==2)
    def _():
        grad[...]=q_ref[...]

def copies(srcs,dsts,sems):
    return [pltpu.make_async_copy(a,b,sems.at[i]) for i,(a,b) in enumerate(zip(srcs,dsts))]

def update_body(inv_ref, q_ref, *refs):
    ins_hbm=refs[0:4]; outs_hbm=refs[4:6]; send_o=refs[6]
    ins=refs[7:11]; outs=refs[11:13]
    grad,update,in_sem,out_sem=refs[13:]
    first,second,left,right=ins
    kind=owned(inv_ref)
    c=right.shape[1]; big=left.shape[1]
    ndev=send_o.shape[0]
    copies_in=copies([h.at[0] for h in ins_hbm],ins,in_sem)
    copies_out=copies(outs,[h.at[0] for h in outs_hbm],out_sem)
    for cp in copies_in: cp.start()
    fetch_grad(kind,q_ref,grad)
    for cp in copies_in: cp.wait()
    @pl.when(kind==0)
    def _():
        for o in outs: o[...]=jnp.zeros_like(o)
        send_o[...]=jnp.zeros_like(send_o)
    @pl.when(kind>0)
    def _():
        L=left[...]; Rb=right[...]
        corr=1.0-0.5**STEP
        turned=dot3(dot2(L,grad[...],0,0),Rb,1,0)
        inside=lax.broadcasted_iota(jnp.int32,(big,c),0)<kind*c
        moment=jnp.where(inside,0.5*first[...]+0.5*turned,0.0)
        sec=jnp.where(inside,0.5*second[...]+0.5*turned*turned,0.0)
        outs[0][...]=moment; outs[1][...]=sec
        direction=moment/corr/(jnp.sqrt(sec/corr)+adam_eps)
        update[...]=dot3(dot3(L,direction,1,0),Rb,1,1)
    for cp in copies_out: cp.start()
    for size,number in ((c,1),(big,2)):
        @pl.when(kind==number)
        def _():
            r=size//ndev
            for d in range(ndev):
                u=update[r*d:r*d+r]
                if r<16: u=jnp.concatenate([u,jnp.zeros((16-r,c),F32)],axis=0)
                send_o[d]=u.astype(BF)
    for cp in copies_out: cp.wait()

def basis_body(inv_ref, q_ref, *refs):
    ins_hbm=refs[0:4]; outs_hbm=refs[4:8]
    ins=refs[8:12]; outs=refs[12:16]
    grad,g_l,g_r,in_sem,out_sem=refs[16:]
    left,right,lstat,rstat=ins
    left_o,right_o,lstat_o,rstat_o=outs
    kind=owned(inv_ref)
    c=right.shape[1]; big=left.shape[1]
    copies_in=copies([h.at[0] for h in ins_hbm],ins,in_sem)
    copies_out=copies(outs,[h.at[0] for h in outs_hbm],out_sem)
    for cp in copies_in: cp.start()
    fetch_grad(kind,q_ref,grad)
    for cp in copies_in: cp.wait()
    @pl.when(kind==0)
    def _():
        for o in outs: o[...]=jnp.zeros_like(o)
        for cp in copies_out: cp.start()
    @pl.when(kind>0)
    def _():
        g=grad[...]
        ls=0.95*lstat[...]+0.05*bdot(g,g,1,1)
        rs=0.95*rstat[...]+0.05*bdot(g,g,0,0)
        lstat_o[...]=ls; rstat_o[...]=rs
        for cp in copies_out[2:]: cp.start()
        ar=dot3(rs,right[...],1,0)
        right_o[...]=ar
        for k in range(0,c,BLK): g_r[k:k+BLK,k:]=tn(ar[:,k:k+BLK],ar[:,k:])
        al=dot3(ls,left[...],1,0)
        left_o[...]=al
        row=lax.broadcasted_iota(jnp.int32,(big,big),0)
        unit=jnp.where((row==lax.broadcasted_iota(jnp.int32,(big,big),1))&(row>=kind*c),1.0,0.0)
        for k in range(0,big,BLK): g_l[k:k+BLK,k:]=tn(al[:,k:k+BLK],al[:,k:])+unit[k:k+BLK,k:]
        factor_both(left_o,g_l,right_o,g_r)
        for cp in copies_out[:2]: cp.start()
    for cp in copies_out: cp.wait()

def owner_call(body,name,inv,q,ins,outs,extra_out,scratch,cost):
    sd=lambda a: jax.ShapeDtypeStruct(a.shape,F32)
    buf=lambda a: pltpu.VMEM(a.shape[1:],F32)
    dma=pltpu.SemaphoreType.DMA
    return pl.pallas_call(body,
        in_specs=[SMEM,VMEM]+[ANY]*len(ins),
        out_specs=[ANY]*len(outs)+[VMEM]*len(extra_out),
        out_shape=[sd(a) for a in outs]+extra_out,
        scratch_shapes=[buf(a) for a in ins]+[buf(a) for a in outs]+scratch+[dma((len(ins),)),dma((len(outs),))],
        compiler_params=pltpu.CompilerParams(vmem_limit_bytes=LIMIT),
        cost_estimate=pl.CostEstimate(flops=cost,bytes_accessed=4<<20,transcendentals=0),
        name=name)(inv,q,*ins)

def owner_update(inv,q,first,second,left,right,ndev):
    c=right.shape[1]; big=left.shape[1]
    return owner_call(update_body,"owner_update",inv,q,(first,second,left,right),(first,second),
        [jax.ShapeDtypeStruct((ndev,16,c),BF)],[pltpu.VMEM((big,c),BF),pltpu.VMEM((big,c),F32)],4*10**9)

def owner_basis(inv,q,left,right,lstat,rstat):
    c=right.shape[1]; big=left.shape[1]
    slots=(left,right,lstat,rstat)
    return owner_call(basis_body,"owner_basis",inv,q,slots,slots,[],
        [pltpu.VMEM((big,c),BF),pltpu.VMEM((big,big),F32),pltpu.VMEM((c,c),F32)],3*10**10)

def place():
    w,n=lax.axis_index("wide"),lax.axis_index("narrow")
    return lax.div(w,2),lax.rem(w,2),lax.div(n,2),lax.rem(n,2)

def device(z,y,x,core):
    return (z*2+y,x*2+core)

def chip_of(z,y,x):
    return (z*2+y)*2+x

def greet(partners):
    barrier=pltpu.get_barrier_semaphore()
    count=0
    for dev,cond in partners:
        if cond is None:
            pl.semaphore_signal(barrier,inc=1,device_id=dev,device_id_type=MESH)
            count=count+1
        else:
            @pl.when(cond)
            def _():
                pl.semaphore_signal(barrier,inc=1,device_id=dev,device_id_type=MESH)
            count=count+jnp.where(cond,1,0)
    pl.semaphore_wait(barrier,count)

def remote(src,dst,send,recv,dev):
    return pltpu.make_async_remote_copy(src_ref=src,dst_ref=dst,send_sem=send,recv_sem=recv,device_id=dev,device_id_type=MESH)

GATHER=MATS+4
SHARE=GATHER//2
CUT=(SHARE+1)//2

def gather_body(depth, conv_ref, dense_ref, attn_ref, vec_ref, w_ref, part, vbuf,
                pair_s, pair_r, line_r, own_r, twin_r, up_s, down_s, x_s, y_s, twin_s):
    z,y,x,core=place()
    me=chip_of(z,y,x)
    rank=me*2+core
    c=w_ref.shape[-1]
    twin=device(z,y,x,1-core)
    side_x,side_y=device(z,y,1-x,core),device(z,1-y,x,core)
    above,below=device(z+1,y,x,core),device(z-1,y,x,core)
    greet([(twin,None),(side_x,None),(side_y,None),(below,z>0),(above,z<depth-1)])
    conv=conv_ref.shape[0]
    part[0,0:conv]=conv_ref[...]
    part[0,conv:MATS]=attn_ref[...]
    part[0,MATS]=dense_ref[0:8]
    part[0,MATS+1]=dense_ref[8:16]
    cols,rows_v=vec_ref.shape
    vbuf[...]=jnp.zeros_like(vbuf)
    vbuf[0:cols,0:rows_v]=vec_ref[...]
    turned=vbuf[0:8,0:128].T[0:16]
    vbuf[...]=jnp.zeros_like(vbuf)
    vbuf[:,0:8]=turned
    mine=pltpu.roll(vbuf[...],rank*cols,1)
    part[0,MATS+2]=mine[0:8]
    part[0,MATS+3]=mine[8:16]
    swap=remote(part.at[0],part.at[1],pair_s,pair_r,twin)
    swap.start()
    swap.wait()
    even,odd=core,1-core
    join=lambda a,b: jnp.concatenate([a,b],axis=0).astype(BF)
    def fill(m,value):
        @pl.when(core==m//SHARE)
        def _(): w_ref[m,z,y,x]=value()
    for k in range(2):
        @pl.when(core==k)
        def _():
            for m in range(k*SHARE,min((k+1)*SHARE,MATS)):
                w_ref[m,z,y,x]=join(part[even,m],part[odd,m])
    for h,src in ((0,even),(1,odd)):
        fill(MATS+h,lambda: join(part[src,MATS],part[src,MATS+1]))
    fill(MATS+2,lambda: join(part[0,MATS+2]+part[1,MATS+2],part[0,MATS+3]+part[1,MATS+3]))
    fill(MATS+3,lambda: jnp.zeros((16,c),BF))

    def mats(h,whose=core):
        return pl.ds(SHARE*whose+(0,CUT)[h],(CUT,SHARE-CUT)[h])
    every=pl.ds(SHARE*core,SHARE)
    def same(at,send,recv,dev):
        return remote(w_ref.at[at],w_ref.at[at],send,recv,dev)
    def to_up(zz): return same((every,zz,y,x),up_s.at[zz],line_r.at[zz],above)
    def to_down(zz): return same((every,zz,y,x),down_s.at[zz],line_r.at[zz],below)
    def first(h,zz):
        at=(mats(h),zz,y,x)
        return (same(at,x_s.at[0,zz],own_r.at[0,0,zz],side_x),same(at,y_s.at[0,zz],own_r.at[1,0,zz],side_y))[h]
    def second(h,zz):
        return (same((mats(0),zz,y),y_s.at[1,zz],own_r.at[0,1,zz],side_y),
                same((mats(1),zz,slice(None),x),x_s.at[1,zz],own_r.at[1,1,zz],side_x))[h]
    def line(zz,up,down):
        if up or down:
            same((every,zz,y,x),up_s.at[zz],line_r.at[zz],twin).wait_recv()
        if up is not False:
            @pl.when(z<depth-1)
            def _(): to_up(zz).start()
        if down is not False:
            @pl.when(z>0)
            def _(): to_down(zz).start()
        for h in range(2): first(h,zz).start()
    def sides(zz):
        same((mats(0),zz,y,1-x),x_s.at[0,zz],own_r.at[0,0,zz],side_x).wait_recv()
        second(0,zz).start()
        same((mats(1),zz,1-y,x),y_s.at[0,zz],own_r.at[1,0,zz],side_y).wait_recv()
        second(1,zz).start()
    def both(d,run):
        for zz,up in ((z-d,True),(z+d,False)):
            @pl.when((zz>=0)&(zz<depth))
            def _(): run(zz,up)
    line(z,None,None)
    for d in range(1,depth+1):
        if d<depth:
            both(d,lambda zz,up: line(zz,up,not up))
        if d==1: sides(z)
        else: both(d-1,lambda zz,up: sides(zz))
    for h in range(2):
        for zz in range(depth):
            at=((mats(0),zz,1-y),(mats(1),zz,slice(None),1-x))[h]
            same(at,twin_s.at[h],own_r.at[h,1,zz],twin).wait_recv()
        same((mats(h),),twin_s.at[h],twin_r.at[h],twin).start()
    for h in range(2):
        same((mats(h,1-core),),twin_s.at[h],twin_r.at[h],twin).wait_recv()
    for h in range(2):
        same((mats(h),),twin_s.at[h],twin_r.at[h],twin).wait_send()
        for zz in range(depth):
            first(h,zz).wait_send(); second(h,zz).wait_send()
    for zz in range(depth):
        @pl.when((z<depth-1)&(zz<=z))
        def _(): to_up(zz).wait_send()
        @pl.when((z>0)&(zz>=z))
        def _(): to_down(zz).wait_send()

def gather_weights(conv,dense,attn,vec,depth):
    c=conv.shape[2]
    dma=pltpu.SemaphoreType.DMA
    line=dma((depth,))
    return pl.pallas_call(functools.partial(gather_body,depth),
        out_shape=jax.ShapeDtypeStruct((GATHER,depth,2,2,16,c),BF),
        in_specs=[VMEM]*4,out_specs=VMEM,
        scratch_shapes=[pltpu.VMEM((2,GATHER,8,c),F32),pltpu.VMEM((16,c),F32),dma,dma,line,dma((2,2,depth)),dma((2,)),line,line,
          dma((2,depth)),dma((2,depth)),dma((2,))],
        compiler_params=pltpu.CompilerParams(collective_id=0,has_side_effects=True,vmem_limit_bytes=LIMIT),
        name="gather_weights")(conv,dense,attn,vec).reshape(GATHER,c,c)

REDUCE=MATS+2
HALF=REDUCE//2
PARTS=((0,3,"xyz"),(3,2,"yzx"),(5,1,"zxy"),(6,2,"xyz"),(8,2,"yzx"),(10,2,"zxy"))

def reduce_body(depth, inv_ref, g_ref, v_ref, q_ref, vec_o, acc, core_in, *rest):
    bufs=tuple(zip(*[iter(rest[:3*len(PARTS)])]*3))
    (final, pick, vsend, vrecv, core_s, core_r, ex_s, ex_r, z_s, z_r, twin_s, twin_r, out_s, out_r, v_s, v_r)=rest[3*len(PARTS):]
    z,y,x,core=place()
    me=chip_of(z,y,x)
    chips=depth*4
    twin=device(z,y,x,1-core)
    def of_chip(o):
        return device(lax.div(o,4),lax.rem(lax.div(o,2),2),lax.rem(o,2),core)
    others=[lax.rem(me+k,chips) for k in range(1,chips)]
    greet([(twin,None)]+[(of_chip(o),None) for o in others])
    c=g_ref.shape[2]
    pair=[]
    for i,(m0,n,_) in enumerate(PARTS):
        cp=remote(g_ref.at[pl.ds(HALF*(1-core)+m0,n)],core_in.at[m0:m0+n],core_s.at[i],core_r.at[i],twin)
        cp.start(); pair.append(cp)
    def vec_start(stage,dev):
        cp=remote(vsend.at[stage],vrecv.at[stage],v_s.at[stage],v_r.at[stage],dev)
        cp.start()
        return cp
    def vec_end(stage,cp):
        cp.wait()
        total=vsend[stage]+vrecv[stage]
        if stage<4: vsend[stage+1]=total
        else: vec_o[...]=total
    vsend[0]=v_ref[...]
    vcp=vec_start(0,twin)
    nbr_x,nbr_y=device(z,y,1-x,core),device(z,1-y,x,core)
    started={}
    def where(i,done):
        return ["z" in done and z, "y" in done and y, "x" in done and x]
    def index(m,place):
        return tuple([m]+[slice(None) if p is False else p for p in place])
    def swap_start(i,stage):
        m0,n,order=PARTS[i]
        axis=order[stage]
        at=where(i,order[:stage])
        at["zyx".index(axis)]=1-(x if axis=="x" else y)
        dst=bufs[i][0 if axis=="x" else 1]
        k=0 if axis=="x" else 1
        cp=remote(acc.at[index(slice(m0,m0+n),at)],dst,ex_s.at[i,k],ex_r.at[i,k],nbr_x if axis=="x" else nbr_y)
        cp.start()
        started[i,stage]=cp
    def swap_end(i,stage):
        m0,n,order=PARTS[i]
        axis=order[stage]
        started.pop((i,stage)).wait()
        at=where(i,order[:stage+1])
        src=bufs[i][0 if axis=="x" else 1]
        @pl.loop(0,n)
        def _(m):
            there=index(m0+m,at)
            acc[there]=(acc[there].astype(F32)+src[m].astype(F32)).astype(BF)
    def z_copy(i,stage,k):
        m0,n,order=PARTS[i]
        zz=lax.rem(z+k,depth)
        at=where(i,order[:stage])
        at[0]=zz
        return remote(acc.at[index(slice(m0,m0+n),at)],bufs[i][2].at[z],z_s.at[i,k],z_r.at[i,z],device(zz,y,x,core))
    def z_start(i,stage):
        for k in range(1,depth):
            z_copy(i,stage,k).start()
    def z_end(i,stage):
        m0,n,order=PARTS[i]
        src=bufs[i][2]
        at=where(i,order[:stage+1])
        for k in range(1,depth):
            zz=lax.rem(z+k,depth)
            remote(src.at[zz],src.at[zz],z_s.at[i,k],z_r.at[i,zz],twin).wait_recv()
        @pl.loop(0,n)
        def _(m):
            there=index(m0+m,at)
            total=acc[there].astype(F32)
            for k in range(1,depth):
                total=total+src[lax.rem(z+k,depth),m].astype(F32)
            acc[there]=total.astype(BF)
        for k in range(1,depth):
            z_copy(i,stage,k).wait_send()

    def add_pair(i):
        m0,n,_=PARTS[i]
        pair[i].wait()
        @pl.loop(0,n)
        def _(m):
            s=(g_ref[HALF*core+m0+m].astype(F32)+core_in[m0+m].astype(F32)).astype(BF)
            acc[m0+m]=s.reshape(acc.shape[1:])
    groups=range(0,len(PARTS),3)
    for i in groups:
        add_pair(i+2); z_start(i+2,0)
        add_pair(i); swap_start(i,0)
        add_pair(i+1); swap_start(i+1,0)
    vec_end(0,vcp); vcp=vec_start(1,nbr_x)
    for i in groups:
        swap_end(i,0); swap_start(i,1)
        swap_end(i+1,0); z_start(i+1,1)
        z_end(i+2,0); swap_start(i+2,1)
    vec_end(1,vcp); vcp=vec_start(2,nbr_y)
    for i in groups:
        swap_end(i,1); z_start(i,2)
        swap_end(i+2,1); swap_start(i+2,2)
        z_end(i+1,1); swap_start(i+1,2)
    vec_end(2,vcp); vcp=vec_start(3,device(lax.div(z,2)*2+(1-lax.rem(z,2)),y,x,core))
    for i in groups:
        swap_end(i+2,2)
        swap_end(i+1,2)
        z_end(i,2)
    vec_end(3,vcp); vcp=vec_start(4,device(lax.rem(z+2,4),y,x,core))
    there=pl.ds(HALF*core,HALF)
    for m in range(HALF):
        final[HALF*core+m]=acc[m,z,y,x]
    cp=remote(final.at[there],final.at[there],twin_s,twin_r,twin)
    cp.start(); cp.wait()
    for k in range(chips):
        o=me if k==0 else others[k-1]
        m=jnp.maximum(inv_ref[o*2+core],0)
        pick[k,0]=final[m]
        pick[k,1]=final[REDUCE-1]
        if k:
            remote(pick.at[k],q_ref.at[me],out_s.at[k],out_r.at[me],of_chip(o)).start()
    q_ref[me]=pick[0]
    vec_end(4,vcp)
    for k in range(1,chips):
        o=others[k-1]
        remote(pick.at[k],q_ref.at[o],out_s.at[k],out_r.at[o],of_chip(o)).wait()

def reduce_grads(inv,grads,vec,depth):
    c=grads.shape[2]
    chips=depth*4
    dma=pltpu.SemaphoreType.DMA
    vm=lambda *s: pltpu.VMEM(s,BF)
    bufs=[]
    for _,n,order in PARTS:
        left={"z":depth,"y":2,"x":2}
        shapes={}
        for axis in order:
            del left[axis]
            shapes[axis]=tuple(left[k] for k in "zyx" if k in left)
        bufs+=[vm(n,*shapes["x"],16,c),vm(n,*shapes["y"],16,c),vm(depth,n,*shapes["z"],16,c)]
    return pl.pallas_call(functools.partial(reduce_body,depth),
        out_shape=[jax.ShapeDtypeStruct((chips,2,16,c),BF),jax.ShapeDtypeStruct(vec.shape,F32)],
        in_specs=[SMEM,VMEM,VMEM],out_specs=[VMEM,VMEM],
        scratch_shapes=[vm(HALF,depth,2,2,16,c),vm(HALF,c,c)]+bufs+[vm(REDUCE,16,c),vm(chips,2,16,c),
          pltpu.VMEM((5,)+vec.shape,F32),pltpu.VMEM((5,)+vec.shape,F32),
          dma((len(PARTS),)),dma((len(PARTS),)),dma((len(PARTS),2)),dma((len(PARTS),2)),dma((len(PARTS),depth)),dma((len(PARTS),depth)),dma,dma,
          dma((chips,)),dma((chips,)),dma((5,)),dma((5,))],
        compiler_params=pltpu.CompilerParams(collective_id=1,has_side_effects=True,vmem_limit_bytes=LIMIT),
        name="reduce_grads")(inv,grads,vec)

def deal_body(ndev, send_ref, out_ref, s_sem, r_sem):
    w,n=lax.axis_index("wide"),lax.axis_index("narrow")
    width=lax.axis_size("narrow")
    me=w*width+n
    dev=lambda d: (lax.div(d,width),lax.rem(d,width))
    others=[lax.rem(me+k,ndev) for k in range(1,ndev)]
    greet([(dev(d),None) for d in others])
    def copy(k):
        d=others[k]
        return remote(send_ref.at[d],out_ref.at[me],s_sem.at[k],r_sem.at[me],dev(d))
    for k in range(ndev-1): copy(k).start()
    out_ref[me]=send_ref[me]
    for k in range(ndev-1):
        d=others[k]
        remote(send_ref.at[d],out_ref.at[d],s_sem.at[k],r_sem.at[d],dev(d)).wait()

def deal_updates(send):
    ndev=send.shape[0]
    dma=pltpu.SemaphoreType.DMA
    return pl.pallas_call(functools.partial(deal_body,ndev),
        out_shape=jax.ShapeDtypeStruct(send.shape,send.dtype),
        in_specs=[VMEM],out_specs=VMEM,
        scratch_shapes=[dma((ndev,)),dma((ndev,))],
        compiler_params=pltpu.CompilerParams(collective_id=2,has_side_effects=True,vmem_limit_bytes=LIMIT),
        name="deal_updates")(send)

def weights_body(owners_ref, upd_ref, conv_ref, dense_ref, attn_ref, vm_ref, v1_ref, v2_ref, gv_ref,
                 conv_o, dense_o, attn_o, vec_o, convc_o, densec_o, attnc_o, vecc_o, v1_o, v2_o):
    me=lax.axis_index("wide")*lax.axis_size("narrow")+lax.axis_index("narrow")
    c=dense_ref.shape[1]
    def new(master,number,fan):
        u=upd_ref[owners_ref[number]].astype(F32)[0:master.shape[0]]
        return master-fan**-0.5*(u+0.01*master)
    for k in range(conv_ref.shape[0]):
        v=new(conv_ref[k],k+(k>=9),9*c)
        conv_o[k]=v; convc_o[k]=v.astype(BF)
    v=new(dense_ref[...],9,dense_ref.shape[0]*lax.axis_size("wide")*lax.axis_size("narrow"))
    dense_o[...]=v; densec_o[...]=v.astype(BF)
    for k in range(4):
        v=new(attn_ref[k],19+k,c)
        attn_o[k]=v; attnc_o[k]=v.astype(BF)
    cols,rows=vm_ref.shape
    g=pltpu.roll(gv_ref[...],lax.rem(c-me*cols,c),1)[:,0:128].T[0:cols,0:rows]
    corr=1.0-0.5**STEP
    f=0.5*v1_ref[...]+0.5*g
    s=0.5*v2_ref[...]+0.5*g*g
    v=vm_ref[...]-0.2*(f/corr)/(jnp.sqrt(s/corr)+adam_eps)
    vec_o[...]=v; vecc_o[...]=v.astype(BF)
    v1_o[...]=f; v2_o[...]=s

def new_weights(owners,upd,conv,dense,attn,vm,v1,v2,gvec):
    sd=jax.ShapeDtypeStruct
    mains=(conv,dense,attn,vm)
    return pl.pallas_call(weights_body,
        out_shape=[sd(a.shape,F32) for a in mains]+[sd(a.shape,BF) for a in mains]+[sd(v1.shape,F32)]*2,
        in_specs=[SMEM]+[VMEM]*8,out_specs=[VMEM]*10,
        compiler_params=pltpu.CompilerParams(vmem_limit_bytes=LIMIT),
        name="new_weights")(owners,upd,conv,dense,attn,vm,v1,v2,gvec)

def step(depth, images, time_embed, out_cotangent, conv_master, dense_master, attn_master, vector_master, vector_first, vector_second,
         owners, slot_first, slot_second, slot_left_basis, slot_right_basis, slot_left_stat, slot_right_stat):
    batch,side,_,c=images.shape
    ndev=lax.axis_size("wide")*lax.axis_size("narrow")
    flat=lambda a: a.reshape(batch,side*side,c)
    conv=conv_master.reshape((-1,)+conv_master.shape[2:])
    vector,vector_first,vector_second=vector_master.T,vector_first.T,vector_second.T
    if depth:
        w=gather_weights(conv,dense_master,attn_master,vector,depth)
    else:
        gather=lambda a,axis: lax.all_gather(a.astype(BF),AXES,axis=axis,tiled=True)
        dense=jnp.swapaxes(gather(dense_master,0).reshape(c//16,2,16,c),0,1).reshape(2,c,c)
        vec=jnp.pad(gather(vector_master,1),((0,c-vector_master.shape[0]),(0,0)))
        w=jnp.concatenate([gather(conv,1),gather(attn_master,1),dense,vec[None],jnp.zeros((1,c,c),BF)])
    act,igrad,tgrad,grads,gvec,inv=train_images(owners,flat(images),flat(out_cotangent),time_embed,w,side,ndev)
    if depth:
        q,gvec=reduce_grads(inv,grads,gvec,depth)
        q=q.reshape(-1,c)
    else:
        total=lax.optimization_barrier(lax.psum(grads.astype(F32),AXES)).astype(BF)
        gvec=lax.psum(gvec,AXES)
        held=inv[lax.axis_index(AXES)]
        q=jnp.stack([total[jnp.maximum(held,0)].reshape(c//16,16,c),total[MATS+1].reshape(c//16,16,c)],axis=1).reshape(-1,c)
    first_slot,second_slot,send=owner_update(inv,q,slot_first,slot_second,slot_left_basis,slot_right_basis,ndev)
    upd=deal_updates(send) if depth and DEAL else lax.all_to_all(send,AXES,0,0,tiled=True)
    slots=[first_slot,second_slot]+list(owner_basis(inv,q,slot_left_basis,slot_right_basis,slot_left_stat,slot_right_stat))
    new=new_weights(owners,upd,conv,dense_master,attn_master,vector,vector_first,vector_second,gvec)
    conv_new,dense_new,attn_new,vec_new,conv_copy,dense_copy,attn_copy,vec_copy,first_new,second_new=new
    return (act.reshape(images.shape),igrad.reshape(images.shape),tgrad,conv_new.reshape(conv_master.shape),dense_new,attn_new,vec_new.T,
            conv_copy.reshape(conv_master.shape),dense_copy,attn_copy,vec_copy.T,first_new.T,second_new.T,*slots)

def solution(mesh):
    rows,both=P(AXES),P(None,AXES)
    taps=P(None,None,AXES)
    depth=4 if (mesh.shape["wide"],mesh.shape["narrow"])==(8,4) else 0
    return jax.shard_map(functools.partial(step,depth),mesh=mesh,
        in_specs=(rows,rows,rows,taps,rows,both,both,both,both,P())+(rows,)*6,
        out_specs=(rows,rows,rows,taps,rows,both,both,taps,rows,both,both,both,both)+(rows,)*6,
        check_vma=False)
```

```python
import functools

import jax
import jax.numpy as jnp
from jax import lax
from jax.experimental import pallas as pl
from jax.experimental.pallas import tpu as pltpu
from jax.sharding import PartitionSpec as P

BF = jnp.bfloat16
F32 = jnp.float32
STEP = 10
GROUP = 8
BLK = 128
ROWS = 256
half_root = 0.5**0.5
norm_eps = 1e-6
adam_eps = 1e-8
HI = lax.Precision.HIGHEST
MESH = pl.DeviceIdType.MESH
AXES = ("wide", "narrow")
MATS = 22
VMEM = pl.BlockSpec(memory_space=pltpu.VMEM)
SMEM = pl.BlockSpec(memory_space=pltpu.SMEM)
ANY = pl.BlockSpec(memory_space=pl.ANY)
LIMIT = 56 << 20
TOGETHER = 6
DEAL = False

def mm(a,b):
    return lax.dot_general(a,b,(((1,),(0,)),((),())),preferred_element_type=F32)
def mm_nt(a,b):
    return lax.dot_general(a,b,(((1,),(1,)),((),())),preferred_element_type=F32)
def mm_tn(a,b):
    return lax.dot_general(a,b,(((0,),(0,)),((),())),preferred_element_type=F32)

def group_sum(v):
    lane=lax.broadcasted_iota(jnp.int32, v.shape, 1)
    n=v.shape[1]
    for s in (1,2,4):
        v=v+jnp.where((lane & s)==0, pltpu.roll(v,n-s,1), pltpu.roll(v,s,1))
    return v

def col_sum(v):
    return jnp.sum(v,axis=0,keepdims=True)

def pad8(v):
    return jnp.broadcast_to(v,(8,v.shape[1]))

def group_mean(colsum, count):
    return group_sum(pad8(colsum))[0:1]*(1.0/count)

def normal_form(v):
    count=v.shape[0]*GROUP
    m=group_mean(col_sum(v),count)
    yield
    c=v-m
    var=group_mean(col_sum(c*c),count)
    yield
    r=lax.rsqrt(var+norm_eps)
    return c*r, r

def norm_back(grad, xhat, r, gain):
    count=grad.shape[0]*GROUP
    shift_grad=col_sum(grad)
    gain_grad=col_sum(grad*xhat)
    m1=group_mean(shift_grad*gain,count)
    m2=group_mean(gain_grad*gain,count)
    yield
    return (grad*(gain*r)-(m1*r)-xhat*(m2*r)), gain_grad, shift_grad

def sigmoid(y):
    return pl.reciprocal(1.0+jnp.exp(-y),approx=True)

def spread(ref, i, v, side):
    tokens, c = v.shape
    parts=v.reshape(tokens//16,2,8,c)
    low,high=parts[:,0],parts[:,1]
    at=lax.broadcasted_iota(jnp.int32,low.shape,1)
    whole=lambda a,b: jnp.stack([a,b],axis=1).reshape(tokens,c).astype(BF)
    l,h=pltpu.roll(low,1,1),pltpu.roll(high,1,1)
    ref[i,side:side+tokens,0:c]=whole(jnp.where(at==0,0.0,l),jnp.where(at==0,l,h))
    ref[i,side:side+tokens,c:2*c]=v.astype(BF)
    l,h=pltpu.roll(low,7,1),pltpu.roll(high,7,1)
    ref[i,side:side+tokens,2*c:3*c]=whole(jnp.where(at==7,h,l),jnp.where(at==7,0.0,h))

def taps(ref, count, dy, tokens, side):
    return jnp.concatenate([ref[i,side*dy:side*dy+tokens,:] for i in range(count)],axis=0)

def train_body(side, owners_ref, img_ref, cot_ref, emb_ref, w_ref,
         act_ref, igrad_ref, tgrad_ref, gw_ref, gvec_ref, inv_ref,
         dense_ref, vec_ref, wt, acc, gvec, proj, pgrad, p1, p2, s2, s1):
    step=pl.program_id(0); steps=pl.num_programs(0)
    ib,tokens,c=img_ref.shape
    batch=emb_ref.shape[0]
    scale=c**-0.5

    @pl.when(step==0)
    def _():
        acc[...]=jnp.zeros_like(acc)
        gvec[...]=jnp.zeros_like(gvec)
        pgrad[...]=jnp.zeros_like(pgrad)
        for ref in (p1,p2,s2,s1):
            for i in range(ib):
                z=jnp.zeros((side,3*c),BF)
                ref[i,0:side,:]=z
                ref[i,side+tokens:2*side+tokens,:]=z
        for k in range(2):
            for t in range(9):
                wt[k, 8-t]=w_ref[9*k+t].T
        chips=c//16
        total=jnp.zeros((16,c),F32)
        for o in range(chips):
            total=total+w_ref[24,16*o:16*o+16].astype(F32)
            for h in range(2):
                dense_ref[32*o+16*h:32*o+16*h+16]=w_ref[22+h,16*o:16*o+16]
        vec_ref[...]=total
        for d in range(inv_ref.shape[0]):
            inv_ref[d]=-1
        for m in range(owners_ref.shape[0]):
            inv_ref[owners_ref[m]]=m if m<9 else MATS if m==9 else m-1
        e=emb_ref[...].astype(F32)
        proj[0:batch]=mm((e*sigmoid(e)).astype(BF),dense_ref[...])+total[7:8]

    vec=vec_ref[...]
    row=lambda k: vec[k:k+1]

    up=lambda t: t.astype(F32)
    sums={}
    def add(kk,val):
        sums[kk]=val if kk not in sums else sums[kk]+val
    def three(ref,k,dy):
        return jnp.concatenate([ref[k+3*dy+dx] for dx in range(3)],axis=0)
    def conv(ref,i,weight):
        out=mm(jnp.concatenate([ref[i,side*dy:side*dy+tokens,:] for dy in range(3)],axis=1),jnp.concatenate([weight(dy) for dy in range(3)],axis=0))
        yield
        return out
    def wgrad(base,aref,gref,i):
        at=aref[i,side:side+tokens,c:2*c].T
        for dy in range(3):
            g=mm(at,gref[i,side*dy:side*dy+tokens,:])
            for dx in range(3):
                acc[base+8-(3*dy+dx)]+=g[:,dx*c:(dx+1)*c]
            yield
    def swish_back(grad,h,gain,shift):
        y=h*gain+shift
        s=sigmoid(y)
        return grad*(s*(1.0+y*(1.0-s)))

    def image(i):
        x=img_ref[i].astype(F32)
        h0,r0=yield from normal_form(x)
        y=h0*row(0)+row(3)
        spread(p1,i,y*sigmoid(y),side)
        yield
        t=yield from conv(p1,i,lambda dy: three(w_ref,0,dy))
        t=t+(row(6)+proj[pl.ds(step*ib+i,1),:])
        h1,r1=yield from normal_form(t)
        y=h1*row(1)+row(4)
        spread(p2,i,y*sigmoid(y),side)
        yield
        t=yield from conv(p2,i,lambda dy: three(w_ref,9,dy))
        mid=(x+(t+row(8)))*half_root
        h2,r2=yield from normal_form(mid)
        normed=(h2*row(2)+row(5)).astype(BF)
        yield
        q=(mm(normed,w_ref[18])+row(9)).astype(BF)
        k=mm(normed,w_ref[19]).astype(BF)
        yield
        v=(mm(normed,w_ref[20])+row(10)).astype(BF)
        sc=mm_nt(q,k)*scale
        yield
        e=jnp.exp(sc-jnp.max(sc,axis=1,keepdims=True))
        a=e*pl.reciprocal(jnp.sum(e,axis=1,keepdims=True),approx=True)
        low=a.astype(BF)
        yield
        mixed=mm(low,v).astype(BF)
        cot=cot_ref[i].astype(F32)*half_root
        bg=cot.astype(BF)
        mg=mm_nt(bg,w_ref[21]).astype(BF)
        add(11,col_sum(up(bg)))
        yield
        branch=mm(mixed,w_ref[21])+row(11)
        pg=mm_nt(mg,v)
        act_ref[i]=((mid+branch)*half_root).astype(BF)
        yield
        sg=(a*(pg-jnp.sum(a*pg,axis=1,keepdims=True))).astype(BF)
        acc[21]+=mm_tn(mixed,bg)
        vg=mm_tn(low,mg).astype(BF)
        yield
        qg=(mm(sg,k)*scale).astype(BF)
        kg=(mm_tn(sg,q)*scale).astype(BF)
        yield
        ng=mm_nt(qg,w_ref[18])+mm_nt(kg,w_ref[19])+mm_nt(vg,w_ref[20])
        yield
        normed_t=normed.T
        acc[18]+=mm(normed_t,qg)
        acc[19]+=mm(normed_t,kg)
        acc[20]+=mm(normed_t,vg)
        add(9,col_sum(up(qg)));add(10,col_sum(up(vg)))
        yield
        d,gg,gs=yield from norm_back(ng,h2,r2,row(2))
        add(2,gg);add(5,gs)
        midg=cot+d
        g=up((midg*half_root).astype(BF))
        add(8,col_sum(g))
        spread(s2,i,g,side)
        yield
        ag=yield from conv(s2,i,lambda dy: three(wt.at[1],0,dy))
        d=swish_back(ag,h1,row(1),row(4))
        yield
        yield from wgrad(9,p2,s2,i)
        d,gg,gs=yield from norm_back(d,h1,r1,row(1))
        add(1,gg);add(4,gs)
        g=up(d.astype(BF))
        s=col_sum(g)
        add(6,s)
        pgr=up(s.astype(BF))
        pgrad[pl.ds(step*ib+i,1),:]=pgr
        add(7,pgr)
        spread(s1,i,g,side)
        yield
        ag=yield from conv(s1,i,lambda dy: three(wt.at[0],0,dy))
        d=swish_back(ag,h0,row(0),row(3))
        yield
        yield from wgrad(0,p1,s1,i)
        d,gg,gs=yield from norm_back(d,h0,r0,row(0))
        add(0,gg);add(3,gs)
        igrad_ref[i]=midg*half_root+d

    def run(count):
        sums.clear()
        live=[image(i) for i in range(count)]
        while live:
            for g in list(live):
                try: next(g)
                except StopIteration: live.remove(g)
        gvec[0:12]+=jnp.concatenate([sums[j] for j in range(12)],axis=0)
    rest=batch-ib*(-(-batch//ib)-1)
    if rest==ib: run(ib)
    else:
        @pl.when(step<steps-1)
        def _(): run(ib)
        @pl.when(step==steps-1)
        def _(): run(rest)

    @pl.when(step==steps-1)
    def _():
        for m in range(acc.shape[0]):
            gw_ref[m]=acc[m].astype(BF)
        gvec_ref[...]=gvec[...]
        e=emb_ref[...].astype(F32)
        s=sigmoid(e)
        ea=(e*s).astype(BF)
        pg=pgrad[0:batch].astype(BF)
        tgrad_ref[...]=mm_nt(pg,dense_ref[...])*(s*(1.0+e*(1.0-s)))
        gd=mm_tn(ea,pg).astype(BF)
        for o in range(c//16):
            for h in range(2):
                gw_ref[22+h,16*o:16*o+16]=gd[32*o+16*h:32*o+16*h+16]

def train_images(owners,images,cot,embed,w,side,ndev):
    batch,tokens,c=images.shape
    emb=embed.shape[1]
    ib=min(TOGETHER,batch)
    rows=-(-batch//8)*8
    whole=lambda a: pl.BlockSpec(a.shape,lambda s: (0,)*len(a.shape))
    blk=pl.BlockSpec((ib,tokens,c),lambda s:(s,0,0))
    sd=jax.ShapeDtypeStruct
    outs=[sd((batch,tokens,c),BF),sd((batch,tokens,c),F32),sd((batch,emb),F32),sd((MATS+2,c,c),BF),sd((16,c),F32)]
    return pl.pallas_call(functools.partial(train_body,side),grid=(-(-batch//ib),),
        in_specs=[SMEM,blk,blk,whole(embed),whole(w)],
        out_specs=[blk,blk]+[whole(o) for o in outs[2:]]+[SMEM],
        out_shape=outs+[sd((ndev,),jnp.int32)],
        scratch_shapes=[pltpu.VMEM((emb,c),BF),pltpu.VMEM((16,c),F32),pltpu.VMEM((2,9,c,c),BF),pltpu.VMEM((MATS,c,c),F32),pltpu.VMEM((16,c),F32),pltpu.VMEM((rows,c),F32),pltpu.VMEM((rows,c),F32)]
          +[pltpu.VMEM((ib,tokens+2*side,3*c),BF)]*4,
        compiler_params=pltpu.CompilerParams(vmem_limit_bytes=LIMIT),
        name="train_images")(owners,images,cot,embed,w)

def fdot(a,b,ca,cb):
    return lax.dot_general(a,b,(((ca,),(cb,)),((),())),precision=HI,preferred_element_type=F32)
nn=lambda a,b: fdot(a,b,1,0)
nt=lambda a,b: fdot(a,b,1,1)
tn=lambda a,b: fdot(a,b,0,0)

def inverse_factors(blocks, tasks):
    tasks=list(tasks)
    share=-(-len(tasks)//14)
    n=BLK
    lane=lax.broadcasted_iota(jnp.int32,(8,n),1)
    sub=lax.broadcasted_iota(jnp.int32,(8,n),0)
    tables=[[b[8*v:8*v+8] for v in range(n//8)] for b in blocks]
    over_lanes=lambda t,j: jnp.broadcast_to(t[:,j:j+1],(8,n))
    over_rows=lambda t,i: jnp.broadcast_to(t[i:i+1],(8,n))
    for J in range(n//8):
        lo=8*J
        in_block=(lane>=lo)&(lane<lo+8)
        for t in tables:
            cur=t[J]
            cols=[over_lanes(cur,lo+j) for j in range(8)]
            m=[[over_rows(cols[j],i) for j in range(i+1)] for i in range(8)]
            R=[jnp.where(in_block,jnp.where(lane==lo+i,1.0,0.0),over_rows(cur,i)) for i in range(8)]
            r=[None]*8
            l=[[None]*8 for _ in range(8)]
            for k in range(8):
                d=m[k][k]
                r[k]=pl.reciprocal(d,approx=True)
                for i in range(k+1,8):
                    l[i][k]=m[i][k]*r[k]
                for i in range(k+1,8):
                    for j in range(k+1,i+1):
                        m[i][j]=m[i][j]-l[i][k]*m[j][k]
                    R[i]=R[i]-l[i][k]*R[k]
            P=[None]*8
            for k in range(7,-1,-1):
                P[k]=R[k]*r[k]
                for i in range(7,k,-1):
                    P[k]=P[k]-l[i][k]*P[i]
            done=R[0]*lax.rsqrt(m[0][0])
            for i in range(1,8):
                done=jnp.where(sub==i,R[i]*lax.rsqrt(m[i][i]),done)
            t[J]=jnp.where(lane<=lo+sub,done,0.0)
            for v in range(J+1,n//8):
                new=jnp.where(in_block,0.0,t[v])
                for k in range(8):
                    new=new-over_lanes(t[v],lo+k)*P[k]
                t[v]=new
        for _ in range(min(share,len(tasks))): tasks.pop(0)()
    return [jnp.concatenate(t,axis=0) for t in tables]

def at(k,size):
    return pl.ds(pl.multiple_of(k*size,size),size)

def split(x):
    hi=x.astype(BF)
    return hi,(x-hi.astype(F32)).astype(BF)

def bdot(a,b,ca,cb):
    return lax.dot_general(a,b,(((ca,),(cb,)),((),())),preferred_element_type=F32)

def dot3(a,b,ca,cb):
    (ah,al),(bh,bl)=split(a),split(b)
    return bdot(ah,bh,ca,cb)+(bdot(ah,bl,ca,cb)+bdot(al,bh,ca,cb))

def dot2(a,b,ca,cb):
    ah,al=split(a)
    return bdot(ah,b,ca,cb)+bdot(al,b,ca,cb)

def factor_both(a_l, g_l, a_r, g_r):
    tasks=[]
    def renew(a,lo,inv,r,rows):
        def task():
            q=dot3(a[rows,lo:lo+BLK],inv,1,1)
            a[rows,lo:lo+BLK]=q
            if r is not None: a[rows,lo+BLK:]=a[rows,lo+BLK:]-dot3(q,r,1,0)
        return task
    def lower(g,r,start,b):
        def task():
            g[b:b+BLK,b:]=g[b:b+BLK,b:]-tn(r[:,b-start:b-start+BLK],r[:,b-start:])
        return task
    for p in range(g_l.shape[0]//BLK):
        lo,hi=p*BLK,(p+1)*BLK
        live=[(a,g) for a,g in ((a_l,g_l),(a_r,g_r)) if g.shape[0]>lo]
        invs=inverse_factors([g[lo:hi,lo:hi] for _,g in live],tasks)
        tasks=[]
        for (a,g),inv in zip(live,invs):
            n=g.shape[0]
            r=None
            if hi<n:
                r=nn(inv,g[lo:hi,hi:])
                lower(g,r,hi,hi)()
                tasks+=[lower(g,r,hi,b) for b in range(hi+BLK,n,BLK)]
            tasks+=[renew(a,lo,inv,r,slice(k,k+ROWS)) for k in range(0,n,ROWS)]
    for task in tasks: task()

def owned(inv_ref):
    held=inv_ref[lax.axis_index("wide")*lax.axis_size("narrow")+lax.axis_index("narrow")]
    return jnp.where(held<0,0,jnp.where(held==MATS,2,1))

def fetch_grad(kind, q_ref, grad):
    big=grad.shape[0]
    @pl.when(kind==1)
    def _():
        grad[...]=jnp.zeros_like(grad)
        for i in range(big//32):
            grad[16*i:16*i+16]=q_ref[32*i:32*i+16]
    @pl.when(kind==2)
    def _():
        grad[...]=q_ref[...]

def copies(srcs,dsts,sems):
    return [pltpu.make_async_copy(a,b,sems.at[i]) for i,(a,b) in enumerate(zip(srcs,dsts))]

def update_body(inv_ref, q_ref, *refs):
    ins_hbm=refs[0:4]; outs_hbm=refs[4:6]; send_o=refs[6]
    ins=refs[7:11]; outs=refs[11:13]
    grad,update,in_sem,out_sem=refs[13:]
    first,second,left,right=ins
    kind=owned(inv_ref)
    c=right.shape[1]; big=left.shape[1]
    ndev=send_o.shape[0]
    copies_in=copies([h.at[0] for h in ins_hbm],ins,in_sem)
    copies_out=copies(outs,[h.at[0] for h in outs_hbm],out_sem)
    for cp in copies_in: cp.start()
    fetch_grad(kind,q_ref,grad)
    for cp in copies_in: cp.wait()
    @pl.when(kind==0)
    def _():
        for o in outs: o[...]=jnp.zeros_like(o)
        send_o[...]=jnp.zeros_like(send_o)
    @pl.when(kind>0)
    def _():
        L=left[...]; Rb=right[...]
        corr=1.0-0.5**STEP
        turned=dot3(dot2(L,grad[...],0,0),Rb,1,0)
        inside=lax.broadcasted_iota(jnp.int32,(big,c),0)<kind*c
        moment=jnp.where(inside,0.5*first[...]+0.5*turned,0.0)
        sec=jnp.where(inside,0.5*second[...]+0.5*turned*turned,0.0)
        outs[0][...]=moment; outs[1][...]=sec
        direction=moment/corr/(jnp.sqrt(sec/corr)+adam_eps)
        update[...]=dot3(dot3(L,direction,1,0),Rb,1,1)
    for cp in copies_out: cp.start()
    for size,number in ((c,1),(big,2)):
        @pl.when(kind==number)
        def _():
            r=size//ndev
            for d in range(ndev):
                u=update[r*d:r*d+r]
                if r<16: u=jnp.concatenate([u,jnp.zeros((16-r,c),F32)],axis=0)
                send_o[d]=u.astype(BF)
    for cp in copies_out: cp.wait()

def basis_body(inv_ref, q_ref, *refs):
    ins_hbm=refs[0:4]; outs_hbm=refs[4:8]
    ins=refs[8:12]; outs=refs[12:16]
    grad,g_l,g_r,in_sem,out_sem=refs[16:]
    left,right,lstat,rstat=ins
    left_o,right_o,lstat_o,rstat_o=outs
    kind=owned(inv_ref)
    c=right.shape[1]; big=left.shape[1]
    copies_in=copies([h.at[0] for h in ins_hbm],ins,in_sem)
    copies_out=copies(outs,[h.at[0] for h in outs_hbm],out_sem)
    for cp in copies_in: cp.start()
    fetch_grad(kind,q_ref,grad)
    for cp in copies_in: cp.wait()
    @pl.when(kind==0)
    def _():
        for o in outs: o[...]=jnp.zeros_like(o)
        for cp in copies_out: cp.start()
    @pl.when(kind>0)
    def _():
        g=grad[...]
        ls=0.95*lstat[...]+0.05*bdot(g,g,1,1)
        rs=0.95*rstat[...]+0.05*bdot(g,g,0,0)
        lstat_o[...]=ls; rstat_o[...]=rs
        for cp in copies_out[2:]: cp.start()
        ar=dot3(rs,right[...],1,0)
        right_o[...]=ar
        for k in range(0,c,BLK): g_r[k:k+BLK,k:]=tn(ar[:,k:k+BLK],ar[:,k:])
        al=dot3(ls,left[...],1,0)
        left_o[...]=al
        row=lax.broadcasted_iota(jnp.int32,(big,big),0)
        unit=jnp.where((row==lax.broadcasted_iota(jnp.int32,(big,big),1))&(row>=kind*c),1.0,0.0)
        for k in range(0,big,BLK): g_l[k:k+BLK,k:]=tn(al[:,k:k+BLK],al[:,k:])+unit[k:k+BLK,k:]
        factor_both(left_o,g_l,right_o,g_r)
        for cp in copies_out[:2]: cp.start()
    for cp in copies_out: cp.wait()

def owner_call(body,name,inv,q,ins,outs,extra_out,scratch,cost):
    sd=lambda a: jax.ShapeDtypeStruct(a.shape,F32)
    buf=lambda a: pltpu.VMEM(a.shape[1:],F32)
    dma=pltpu.SemaphoreType.DMA
    return pl.pallas_call(body,
        in_specs=[SMEM,VMEM]+[ANY]*len(ins),
        out_specs=[ANY]*len(outs)+[VMEM]*len(extra_out),
        out_shape=[sd(a) for a in outs]+extra_out,
        scratch_shapes=[buf(a) for a in ins]+[buf(a) for a in outs]+scratch+[dma((len(ins),)),dma((len(outs),))],
        compiler_params=pltpu.CompilerParams(vmem_limit_bytes=24<<20),
        cost_estimate=pl.CostEstimate(flops=cost,bytes_accessed=4<<20,transcendentals=0),
        name=name)(inv,q,*ins)

def owner_update(inv,q,first,second,left,right,ndev):
    c=right.shape[1]; big=left.shape[1]
    return owner_call(update_body,"owner_update",inv,q,(first,second,left,right),(first,second),
        [jax.ShapeDtypeStruct((ndev,16,c),BF)],[pltpu.VMEM((big,c),BF),pltpu.VMEM((big,c),F32)],4*10**9)

def owner_basis(inv,q,left,right,lstat,rstat):
    c=right.shape[1]; big=left.shape[1]
    slots=(left,right,lstat,rstat)
    return owner_call(basis_body,"owner_basis",inv,q,slots,slots,[],
        [pltpu.VMEM((big,c),BF),pltpu.VMEM((big,big),F32),pltpu.VMEM((c,c),F32)],3*10**10)

def place():
    w,n=lax.axis_index("wide"),lax.axis_index("narrow")
    return lax.div(w,2),lax.rem(w,2),lax.div(n,2),lax.rem(n,2)

def device(z,y,x,core):
    return (z*2+y,x*2+core)

def chip_of(z,y,x):
    return (z*2+y)*2+x

def greet(partners):
    barrier=pltpu.get_barrier_semaphore()
    count=0
    for dev,cond in partners:
        if cond is None:
            pl.semaphore_signal(barrier,inc=1,device_id=dev,device_id_type=MESH)
            count=count+1
        else:
            @pl.when(cond)
            def _():
                pl.semaphore_signal(barrier,inc=1,device_id=dev,device_id_type=MESH)
            count=count+jnp.where(cond,1,0)
    pl.semaphore_wait(barrier,count)

def remote(src,dst,send,recv,dev):
    return pltpu.make_async_remote_copy(src_ref=src,dst_ref=dst,send_sem=send,recv_sem=recv,device_id=dev,device_id_type=MESH)

GATHER=MATS+4
SHARE=GATHER//2
CUT=(SHARE+1)//2

def gather_body(depth, conv_ref, dense_ref, attn_ref, vec_ref, w_ref, part, vbuf,
                pair_s, pair_r, line_r, own_r, twin_r, up_s, down_s, x_s, y_s, twin_s):
    z,y,x,core=place()
    me=chip_of(z,y,x)
    rank=me*2+core
    c=w_ref.shape[-1]
    twin=device(z,y,x,1-core)
    side_x,side_y=device(z,y,1-x,core),device(z,1-y,x,core)
    above,below=device(z+1,y,x,core),device(z-1,y,x,core)
    greet([(twin,None),(side_x,None),(side_y,None),(below,z>0),(above,z<depth-1)])
    conv=conv_ref.shape[0]
    part[0,0:conv]=conv_ref[...]
    part[0,conv:MATS]=attn_ref[...]
    part[0,MATS]=dense_ref[0:8]
    part[0,MATS+1]=dense_ref[8:16]
    cols,rows_v=vec_ref.shape
    vbuf[...]=jnp.zeros_like(vbuf)
    vbuf[0:cols,0:rows_v]=vec_ref[...]
    turned=vbuf[0:8,0:128].T[0:16]
    vbuf[...]=jnp.zeros_like(vbuf)
    vbuf[:,0:8]=turned
    mine=pltpu.roll(vbuf[...],rank*cols,1)
    part[0,MATS+2]=mine[0:8]
    part[0,MATS+3]=mine[8:16]
    swap=remote(part.at[0],part.at[1],pair_s,pair_r,twin)
    swap.start()
    swap.wait()
    even,odd=core,1-core
    join=lambda a,b: jnp.concatenate([a,b],axis=0).astype(BF)
    def fill(m,value):
        @pl.when(core==m//SHARE)
        def _(): w_ref[m,z,y,x]=value()
    for k in range(2):
        @pl.when(core==k)
        def _():
            for m in range(k*SHARE,min((k+1)*SHARE,MATS)):
                w_ref[m,z,y,x]=join(part[even,m],part[odd,m])
    for h,src in ((0,even),(1,odd)):
        fill(MATS+h,lambda: join(part[src,MATS],part[src,MATS+1]))
    fill(MATS+2,lambda: join(part[0,MATS+2]+part[1,MATS+2],part[0,MATS+3]+part[1,MATS+3]))
    fill(MATS+3,lambda: jnp.zeros((16,c),BF))

    def mats(h,whose=core):
        return pl.ds(SHARE*whose+(0,CUT)[h],(CUT,SHARE-CUT)[h])
    every=pl.ds(SHARE*core,SHARE)
    def same(at,send,recv,dev):
        return remote(w_ref.at[at],w_ref.at[at],send,recv,dev)
    def to_up(zz): return same((every,zz,y,x),up_s.at[zz],line_r.at[zz],above)
    def to_down(zz): return same((every,zz,y,x),down_s.at[zz],line_r.at[zz],below)
    def first(h,zz):
        at=(mats(h),zz,y,x)
        return (same(at,x_s.at[0,zz],own_r.at[0,0,zz],side_x),same(at,y_s.at[0,zz],own_r.at[1,0,zz],side_y))[h]
    def second(h,zz):
        return (same((mats(0),zz,y),y_s.at[1,zz],own_r.at[0,1,zz],side_y),
                same((mats(1),zz,slice(None),x),x_s.at[1,zz],own_r.at[1,1,zz],side_x))[h]
    def line(zz,up,down):
        if up or down:
            same((every,zz,y,x),up_s.at[zz],line_r.at[zz],twin).wait_recv()
        if up is not False:
            @pl.when(z<depth-1)
            def _(): to_up(zz).start()
        if down is not False:
            @pl.when(z>0)
            def _(): to_down(zz).start()
        for h in range(2): first(h,zz).start()
    def sides(zz):
        same((mats(0),zz,y,1-x),x_s.at[0,zz],own_r.at[0,0,zz],side_x).wait_recv()
        second(0,zz).start()
        same((mats(1),zz,1-y,x),y_s.at[0,zz],own_r.at[1,0,zz],side_y).wait_recv()
        second(1,zz).start()
    def both(d,run):
        for zz,up in ((z-d,True),(z+d,False)):
            @pl.when((zz>=0)&(zz<depth))
            def _(): run(zz,up)
    line(z,None,None)
    for d in range(1,depth+1):
        if d<depth:
            both(d,lambda zz,up: line(zz,up,not up))
        if d==1: sides(z)
        else: both(d-1,lambda zz,up: sides(zz))
    for h in range(2):
        for zz in range(depth):
            at=((mats(0),zz,1-y),(mats(1),zz,slice(None),1-x))[h]
            same(at,twin_s.at[h],own_r.at[h,1,zz],twin).wait_recv()
        same((mats(h),),twin_s.at[h],twin_r.at[h],twin).start()
    for h in range(2):
        same((mats(h,1-core),),twin_s.at[h],twin_r.at[h],twin).wait_recv()
    for h in range(2):
        same((mats(h),),twin_s.at[h],twin_r.at[h],twin).wait_send()
        for zz in range(depth):
            first(h,zz).wait_send(); second(h,zz).wait_send()
    for zz in range(depth):
        @pl.when((z<depth-1)&(zz<=z))
        def _(): to_up(zz).wait_send()
        @pl.when((z>0)&(zz>=z))
        def _(): to_down(zz).wait_send()

def gather_weights(conv,dense,attn,vec,depth):
    c=conv.shape[2]
    dma=pltpu.SemaphoreType.DMA
    line=dma((depth,))
    return pl.pallas_call(functools.partial(gather_body,depth),
        out_shape=jax.ShapeDtypeStruct((GATHER,depth,2,2,16,c),BF),
        in_specs=[VMEM]*4,out_specs=VMEM,
        scratch_shapes=[pltpu.VMEM((2,GATHER,8,c),F32),pltpu.VMEM((16,c),F32),dma,dma,line,dma((2,2,depth)),dma((2,)),line,line,
          dma((2,depth)),dma((2,depth)),dma((2,))],
        compiler_params=pltpu.CompilerParams(collective_id=0,has_side_effects=True,vmem_limit_bytes=LIMIT),
        name="gather_weights")(conv,dense,attn,vec).reshape(GATHER,c,c)

REDUCE=MATS+2
HALF=REDUCE//2
PARTS=((0,3,"xyz"),(3,2,"yzx"),(5,1,"zxy"),(6,2,"xyz"),(8,2,"yzx"),(10,2,"zxy"))

def reduce_body(depth, inv_ref, g_ref, v_ref, q_ref, vec_o, acc, core_in, *rest):
    bufs=tuple(zip(*[iter(rest[:3*len(PARTS)])]*3))
    (final, pick, vsend, vrecv, core_s, core_r, ex_s, ex_r, z_s, z_r, twin_s, twin_r, out_s, out_r, v_s, v_r)=rest[3*len(PARTS):]
    z,y,x,core=place()
    me=chip_of(z,y,x)
    chips=depth*4
    twin=device(z,y,x,1-core)
    def of_chip(o):
        return device(lax.div(o,4),lax.rem(lax.div(o,2),2),lax.rem(o,2),core)
    others=[lax.rem(me+k,chips) for k in range(1,chips)]
    greet([(twin,None)]+[(of_chip(o),None) for o in others])
    c=g_ref.shape[2]
    pair=[]
    for i,(m0,n,_) in enumerate(PARTS):
        cp=remote(g_ref.at[pl.ds(HALF*(1-core)+m0,n)],core_in.at[m0:m0+n],core_s.at[i],core_r.at[i],twin)
        cp.start(); pair.append(cp)
    def vec_start(stage,dev):
        cp=remote(vsend.at[stage],vrecv.at[stage],v_s.at[stage],v_r.at[stage],dev)
        cp.start()
        return cp
    def vec_end(stage,cp):
        cp.wait()
        total=vsend[stage]+vrecv[stage]
        if stage<4: vsend[stage+1]=total
        else: vec_o[...]=total
    vsend[0]=v_ref[...]
    vcp=vec_start(0,twin)
    nbr_x,nbr_y=device(z,y,1-x,core),device(z,1-y,x,core)
    started={}
    def where(i,done):
        return ["z" in done and z, "y" in done and y, "x" in done and x]
    def index(m,place):
        return tuple([m]+[slice(None) if p is False else p for p in place])
    def swap_start(i,stage):
        m0,n,order=PARTS[i]
        axis=order[stage]
        at=where(i,order[:stage])
        at["zyx".index(axis)]=1-(x if axis=="x" else y)
        dst=bufs[i][0 if axis=="x" else 1]
        k=0 if axis=="x" else 1
        cp=remote(acc.at[index(slice(m0,m0+n),at)],dst,ex_s.at[i,k],ex_r.at[i,k],nbr_x if axis=="x" else nbr_y)
        cp.start()
        started[i,stage]=cp
    def swap_end(i,stage):
        m0,n,order=PARTS[i]
        axis=order[stage]
        started.pop((i,stage)).wait()
        at=where(i,order[:stage+1])
        src=bufs[i][0 if axis=="x" else 1]
        @pl.loop(0,n)
        def _(m):
            there=index(m0+m,at)
            acc[there]=(acc[there].astype(F32)+src[m].astype(F32)).astype(BF)
    def z_copy(i,stage,k):
        m0,n,order=PARTS[i]
        zz=lax.rem(z+k,depth)
        at=where(i,order[:stage])
        at[0]=zz
        return remote(acc.at[index(slice(m0,m0+n),at)],bufs[i][2].at[z],z_s.at[i,k],z_r.at[i,z],device(zz,y,x,core))
    def z_start(i,stage):
        for k in range(1,depth):
            z_copy(i,stage,k).start()
    def z_end(i,stage):
        m0,n,order=PARTS[i]
        src=bufs[i][2]
        at=where(i,order[:stage+1])
        for k in range(1,depth):
            zz=lax.rem(z+k,depth)
            remote(src.at[zz],src.at[zz],z_s.at[i,k],z_r.at[i,zz],twin).wait_recv()
        @pl.loop(0,n)
        def _(m):
            there=index(m0+m,at)
            total=acc[there].astype(F32)
            for k in range(1,depth):
                total=total+src[lax.rem(z+k,depth),m].astype(F32)
            acc[there]=total.astype(BF)
        for k in range(1,depth):
            z_copy(i,stage,k).wait_send()

    def add_pair(i):
        m0,n,_=PARTS[i]
        pair[i].wait()
        @pl.loop(0,n)
        def _(m):
            s=(g_ref[HALF*core+m0+m].astype(F32)+core_in[m0+m].astype(F32)).astype(BF)
            acc[m0+m]=s.reshape(acc.shape[1:])
    groups=range(0,len(PARTS),3)
    for i in groups:
        add_pair(i+2); z_start(i+2,0)
        add_pair(i); swap_start(i,0)
        add_pair(i+1); swap_start(i+1,0)
    vec_end(0,vcp); vcp=vec_start(1,nbr_x)
    for i in groups:
        swap_end(i,0); swap_start(i,1)
        swap_end(i+1,0); z_start(i+1,1)
        z_end(i+2,0); swap_start(i+2,1)
    vec_end(1,vcp); vcp=vec_start(2,nbr_y)
    for i in groups:
        swap_end(i,1); z_start(i,2)
        swap_end(i+2,1); swap_start(i+2,2)
        z_end(i+1,1); swap_start(i+1,2)
    vec_end(2,vcp); vcp=vec_start(3,device(lax.div(z,2)*2+(1-lax.rem(z,2)),y,x,core))
    for i in groups:
        swap_end(i+2,2)
        swap_end(i+1,2)
        z_end(i,2)
    vec_end(3,vcp); vcp=vec_start(4,device(lax.rem(z+2,4),y,x,core))
    there=pl.ds(HALF*core,HALF)
    for m in range(HALF):
        final[HALF*core+m]=acc[m,z,y,x]
    cp=remote(final.at[there],final.at[there],twin_s,twin_r,twin)
    cp.start(); cp.wait()
    for k in range(chips):
        o=me if k==0 else others[k-1]
        m=jnp.maximum(inv_ref[o*2+core],0)
        pick[k,0]=final[m]
        pick[k,1]=final[REDUCE-1]
        if k:
            remote(pick.at[k],q_ref.at[me],out_s.at[k],out_r.at[me],of_chip(o)).start()
    q_ref[me]=pick[0]
    vec_end(4,vcp)
    for k in range(1,chips):
        o=others[k-1]
        remote(pick.at[k],q_ref.at[o],out_s.at[k],out_r.at[o],of_chip(o)).wait()

def reduce_grads(inv,grads,vec,depth):
    c=grads.shape[2]
    chips=depth*4
    dma=pltpu.SemaphoreType.DMA
    vm=lambda *s: pltpu.VMEM(s,BF)
    bufs=[]
    for _,n,order in PARTS:
        left={"z":depth,"y":2,"x":2}
        shapes={}
        for axis in order:
            del left[axis]
            shapes[axis]=tuple(left[k] for k in "zyx" if k in left)
        bufs+=[vm(n,*shapes["x"],16,c),vm(n,*shapes["y"],16,c),vm(depth,n,*shapes["z"],16,c)]
    return pl.pallas_call(functools.partial(reduce_body,depth),
        out_shape=[jax.ShapeDtypeStruct((chips,2,16,c),BF),jax.ShapeDtypeStruct(vec.shape,F32)],
        in_specs=[SMEM,VMEM,VMEM],out_specs=[VMEM,VMEM],
        scratch_shapes=[vm(HALF,depth,2,2,16,c),vm(HALF,c,c)]+bufs+[vm(REDUCE,16,c),vm(chips,2,16,c),
          pltpu.VMEM((5,)+vec.shape,F32),pltpu.VMEM((5,)+vec.shape,F32),
          dma((len(PARTS),)),dma((len(PARTS),)),dma((len(PARTS),2)),dma((len(PARTS),2)),dma((len(PARTS),depth)),dma((len(PARTS),depth)),dma,dma,
          dma((chips,)),dma((chips,)),dma((5,)),dma((5,))],
        compiler_params=pltpu.CompilerParams(collective_id=1,has_side_effects=True,vmem_limit_bytes=18<<20),
        name="reduce_grads")(inv,grads,vec)

def deal_body(ndev, send_ref, out_ref, s_sem, r_sem):
    w,n=lax.axis_index("wide"),lax.axis_index("narrow")
    width=lax.axis_size("narrow")
    me=w*width+n
    dev=lambda d: (lax.div(d,width),lax.rem(d,width))
    others=[lax.rem(me+k,ndev) for k in range(1,ndev)]
    greet([(dev(d),None) for d in others])
    def copy(k):
        d=others[k]
        return remote(send_ref.at[d],out_ref.at[me],s_sem.at[k],r_sem.at[me],dev(d))
    for k in range(ndev-1): copy(k).start()
    out_ref[me]=send_ref[me]
    for k in range(ndev-1):
        d=others[k]
        remote(send_ref.at[d],out_ref.at[d],s_sem.at[k],r_sem.at[d],dev(d)).wait()

def deal_updates(send):
    ndev=send.shape[0]
    dma=pltpu.SemaphoreType.DMA
    return pl.pallas_call(functools.partial(deal_body,ndev),
        out_shape=jax.ShapeDtypeStruct(send.shape,send.dtype),
        in_specs=[VMEM],out_specs=VMEM,
        scratch_shapes=[dma((ndev,)),dma((ndev,))],
        compiler_params=pltpu.CompilerParams(collective_id=2,has_side_effects=True,vmem_limit_bytes=4<<20),
        name="deal_updates")(send)

def weights_body(owners_ref, upd_ref, conv_ref, dense_ref, attn_ref, vm_ref, v1_ref, v2_ref, gv_ref,
                 conv_o, dense_o, attn_o, vec_o, convc_o, densec_o, attnc_o, vecc_o, v1_o, v2_o):
    me=lax.axis_index("wide")*lax.axis_size("narrow")+lax.axis_index("narrow")
    c=dense_ref.shape[1]
    def new(master,number,fan):
        u=upd_ref[owners_ref[number]].astype(F32)[0:master.shape[0]]
        return master-fan**-0.5*(u+0.01*master)
    for k in range(conv_ref.shape[0]):
        v=new(conv_ref[k],k+(k>=9),9*c)
        conv_o[k]=v; convc_o[k]=v.astype(BF)
    v=new(dense_ref[...],9,dense_ref.shape[0]*lax.axis_size("wide")*lax.axis_size("narrow"))
    dense_o[...]=v; densec_o[...]=v.astype(BF)
    for k in range(4):
        v=new(attn_ref[k],19+k,c)
        attn_o[k]=v; attnc_o[k]=v.astype(BF)
    cols,rows=vm_ref.shape
    g=pltpu.roll(gv_ref[...],lax.rem(c-me*cols,c),1)[:,0:128].T[0:cols,0:rows]
    corr=1.0-0.5**STEP
    f=0.5*v1_ref[...]+0.5*g
    s=0.5*v2_ref[...]+0.5*g*g
    v=vm_ref[...]-0.2*(f/corr)/(jnp.sqrt(s/corr)+adam_eps)
    vec_o[...]=v; vecc_o[...]=v.astype(BF)
    v1_o[...]=f; v2_o[...]=s

def new_weights(owners,upd,conv,dense,attn,vm,v1,v2,gvec):
    sd=jax.ShapeDtypeStruct
    mains=(conv,dense,attn,vm)
    return pl.pallas_call(weights_body,
        out_shape=[sd(a.shape,F32) for a in mains]+[sd(a.shape,BF) for a in mains]+[sd(v1.shape,F32)]*2,
        in_specs=[SMEM]+[VMEM]*8,out_specs=[VMEM]*10,
        compiler_params=pltpu.CompilerParams(vmem_limit_bytes=4<<20),
        name="new_weights")(owners,upd,conv,dense,attn,vm,v1,v2,gvec)

def step(depth, images, time_embed, out_cotangent, conv_master, dense_master, attn_master, vector_master, vector_first, vector_second,
         owners, slot_first, slot_second, slot_left_basis, slot_right_basis, slot_left_stat, slot_right_stat):
    batch,side,_,c=images.shape
    ndev=lax.axis_size("wide")*lax.axis_size("narrow")
    flat=lambda a: a.reshape(batch,side*side,c)
    conv=conv_master.reshape((-1,)+conv_master.shape[2:])
    vector,vector_first,vector_second=vector_master.T,vector_first.T,vector_second.T
    if depth:
        w=gather_weights(conv,dense_master,attn_master,vector,depth)
    else:
        gather=lambda a,axis: lax.all_gather(a.astype(BF),AXES,axis=axis,tiled=True)
        dense=jnp.swapaxes(gather(dense_master,0).reshape(c//16,2,16,c),0,1).reshape(2,c,c)
        vec=jnp.pad(gather(vector_master,1),((0,c-vector_master.shape[0]),(0,0)))
        w=jnp.concatenate([gather(conv,1),gather(attn_master,1),dense,vec[None],jnp.zeros((1,c,c),BF)])
    act,igrad,tgrad,grads,gvec,inv=train_images(owners,flat(images),flat(out_cotangent),time_embed,w,side,ndev)
    if depth:
        q,gvec=reduce_grads(inv,grads,gvec,depth)
        q=q.reshape(-1,c)
    else:
        total=lax.optimization_barrier(lax.psum(grads.astype(F32),AXES)).astype(BF)
        gvec=lax.psum(gvec,AXES)
        held=inv[lax.axis_index(AXES)]
        q=jnp.stack([total[jnp.maximum(held,0)].reshape(c//16,16,c),total[MATS+1].reshape(c//16,16,c)],axis=1).reshape(-1,c)
    first_slot,second_slot,send=owner_update(inv,q,slot_first,slot_second,slot_left_basis,slot_right_basis,ndev)
    upd=deal_updates(send) if depth and DEAL else lax.all_to_all(send,AXES,0,0,tiled=True)
    slots=[first_slot,second_slot]+list(owner_basis(inv,q,slot_left_basis,slot_right_basis,slot_left_stat,slot_right_stat))
    new=new_weights(owners,upd,conv,dense_master,attn_master,vector,vector_first,vector_second,gvec)
    conv_new,dense_new,attn_new,vec_new,conv_copy,dense_copy,attn_copy,vec_copy,first_new,second_new=new
    return (act.reshape(images.shape),igrad.reshape(images.shape),tgrad,conv_new.reshape(conv_master.shape),dense_new,attn_new,vec_new.T,
            conv_copy.reshape(conv_master.shape),dense_copy,attn_copy,vec_copy.T,first_new.T,second_new.T,*slots)

def solution(mesh):
    rows,both=P(AXES),P(None,AXES)
    taps=P(None,None,AXES)
    depth=4 if (mesh.shape["wide"],mesh.shape["narrow"])==(8,4) else 0
    return jax.shard_map(functools.partial(step,depth),mesh=mesh,
        in_specs=(rows,rows,rows,taps,rows,both,both,both,both,P())+(rows,)*6,
        out_specs=(rows,rows,rows,taps,rows,both,both,taps,rows,both,both,both,both)+(rows,)*6,
        check_vma=False)
```

```python
import functools

import jax
import jax.numpy as jnp
from jax import lax
from jax.experimental import pallas as pl
from jax.experimental.pallas import tpu as pltpu
from jax.sharding import PartitionSpec as P

BF = jnp.bfloat16
F32 = jnp.float32
STEP = 10
GROUP = 8
BLK = 128
ROWS = 256
half_root = 0.5**0.5
norm_eps = 1e-6
adam_eps = 1e-8
HI = lax.Precision.HIGHEST
MESH = pl.DeviceIdType.MESH
AXES = ("wide", "narrow")
MATS = 22
VMEM = pl.BlockSpec(memory_space=pltpu.VMEM)
SMEM = pl.BlockSpec(memory_space=pltpu.SMEM)
ANY = pl.BlockSpec(memory_space=pl.ANY)
LIMIT = 56 << 20
TOGETHER = 6
DEAL = False

def mm(a,b):
    return lax.dot_general(a,b,(((1,),(0,)),((),())),preferred_element_type=F32)
def mm_nt(a,b):
    return lax.dot_general(a,b,(((1,),(1,)),((),())),preferred_element_type=F32)
def mm_tn(a,b):
    return lax.dot_general(a,b,(((0,),(0,)),((),())),preferred_element_type=F32)

def group_sum(v):
    lane=lax.broadcasted_iota(jnp.int32, v.shape, 1)
    n=v.shape[1]
    for s in (1,2,4):
        v=v+jnp.where((lane & s)==0, pltpu.roll(v,n-s,1), pltpu.roll(v,s,1))
    return v

def col_sum(v):
    return jnp.sum(v,axis=0,keepdims=True)

def pad8(v):
    return jnp.broadcast_to(v,(8,v.shape[1]))

def group_mean(colsum, count):
    return group_sum(pad8(colsum))[0:1]*(1.0/count)

def normal_form(v):
    count=v.shape[0]*GROUP
    m=group_mean(col_sum(v),count)
    yield
    c=v-m
    var=group_mean(col_sum(c*c),count)
    yield
    r=lax.rsqrt(var+norm_eps)
    return c*r, r

def norm_back(grad, xhat, r, gain):
    count=grad.shape[0]*GROUP
    shift_grad=col_sum(grad)
    gain_grad=col_sum(grad*xhat)
    m1=group_mean(shift_grad*gain,count)
    m2=group_mean(gain_grad*gain,count)
    yield
    return (grad*(gain*r)-(m1*r)-xhat*(m2*r)), gain_grad, shift_grad

def sigmoid(y):
    return pl.reciprocal(1.0+jnp.exp(-y),approx=True)

def spread(ref, i, v, side):
    tokens, c = v.shape
    parts=v.reshape(tokens//16,2,8,c)
    low,high=parts[:,0],parts[:,1]
    at=lax.broadcasted_iota(jnp.int32,low.shape,1)
    whole=lambda a,b: jnp.stack([a,b],axis=1).reshape(tokens,c).astype(BF)
    l,h=pltpu.roll(low,1,1),pltpu.roll(high,1,1)
    ref[i,side:side+tokens,0:c]=whole(jnp.where(at==0,0.0,l),jnp.where(at==0,l,h))
    ref[i,side:side+tokens,c:2*c]=v.astype(BF)
    l,h=pltpu.roll(low,7,1),pltpu.roll(high,7,1)
    ref[i,side:side+tokens,2*c:3*c]=whole(jnp.where(at==7,h,l),jnp.where(at==7,0.0,h))

def taps(ref, count, dy, tokens, side):
    return jnp.concatenate([ref[i,side*dy:side*dy+tokens,:] for i in range(count)],axis=0)

def train_body(side, owners_ref, img_ref, cot_ref, emb_ref, w_ref,
         act_ref, igrad_ref, tgrad_ref, gw_ref, gvec_ref, inv_ref,
         dense_ref, vec_ref, acc, gvec, proj, pgrad, p1, p2, s2, s1):
    step=pl.program_id(0); steps=pl.num_programs(0)
    ib,tokens,c=img_ref.shape
    batch=emb_ref.shape[0]
    scale=c**-0.5

    @pl.when(step==0)
    def _():
        acc[...]=jnp.zeros_like(acc)
        gvec[...]=jnp.zeros_like(gvec)
        pgrad[...]=jnp.zeros_like(pgrad)
        for ref in (p1,p2,s2,s1):
            for i in range(ib):
                z=jnp.zeros((side,3*c),BF)
                ref[i,0:side,:]=z
                ref[i,side+tokens:2*side+tokens,:]=z
        chips=c//16
        total=jnp.zeros((16,c),F32)
        for o in range(chips):
            total=total+w_ref[24,16*o:16*o+16].astype(F32)
            for h in range(2):
                dense_ref[32*o+16*h:32*o+16*h+16]=w_ref[22+h,16*o:16*o+16]
        vec_ref[...]=total
        for d in range(inv_ref.shape[0]):
            inv_ref[d]=-1
        for m in range(owners_ref.shape[0]):
            inv_ref[owners_ref[m]]=m if m<9 else MATS if m==9 else m-1
        e=emb_ref[...].astype(F32)
        proj[0:batch]=mm((e*sigmoid(e)).astype(BF),dense_ref[...])+total[7:8]

    vec=vec_ref[...]
    row=lambda k: vec[k:k+1]

    up=lambda t: t.astype(F32)
    sums={}
    def add(kk,val):
        sums[kk]=val if kk not in sums else sums[kk]+val
    def three(ref,k,dy):
        return jnp.concatenate([ref[k+3*dy+dx] for dx in range(3)],axis=0)
    def conv(ref,i,weight):
        out=mm(jnp.concatenate([ref[i,side*dy:side*dy+tokens,:] for dy in range(3)],axis=1),jnp.concatenate([weight(dy) for dy in range(3)],axis=0))
        yield
        return out
    def back(ref,i,base):
        out=mm_nt(jnp.concatenate([ref[i,side*dy:side*dy+tokens,:] for dy in range(3)],axis=1),jnp.concatenate([w_ref[base+8-t] for t in range(9)],axis=1))
        yield
        return out
    def wgrad(base,aref,gref,i):
        at=aref[i,side:side+tokens,c:2*c].T
        for dy in range(3):
            g=mm(at,gref[i,side*dy:side*dy+tokens,:])
            for dx in range(3):
                acc[base+8-(3*dy+dx)]+=g[:,dx*c:(dx+1)*c]
            yield
    def swish_back(grad,h,gain,shift):
        y=h*gain+shift
        s=sigmoid(y)
        return grad*(s*(1.0+y*(1.0-s)))

    def image(i):
        x=img_ref[i].astype(F32)
        h0,r0=yield from normal_form(x)
        y=h0*row(0)+row(3)
        spread(p1,i,y*sigmoid(y),side)
        yield
        t=yield from conv(p1,i,lambda dy: three(w_ref,0,dy))
        t=t+(row(6)+proj[pl.ds(step*ib+i,1),:])
        h1,r1=yield from normal_form(t)
        y=h1*row(1)+row(4)
        spread(p2,i,y*sigmoid(y),side)
        yield
        t=yield from conv(p2,i,lambda dy: three(w_ref,9,dy))
        mid=(x+(t+row(8)))*half_root
        h2,r2=yield from normal_form(mid)
        normed=(h2*row(2)+row(5)).astype(BF)
        yield
        q=(mm(normed,w_ref[18])+row(9)).astype(BF)
        k=mm(normed,w_ref[19]).astype(BF)
        yield
        v=(mm(normed,w_ref[20])+row(10)).astype(BF)
        sc=mm_nt(q,k)*scale
        yield
        e=jnp.exp(sc-jnp.max(sc,axis=1,keepdims=True))
        a=e*pl.reciprocal(jnp.sum(e,axis=1,keepdims=True),approx=True)
        low=a.astype(BF)
        yield
        mixed=mm(low,v).astype(BF)
        cot=cot_ref[i].astype(F32)*half_root
        bg=cot.astype(BF)
        mg=mm_nt(bg,w_ref[21]).astype(BF)
        add(11,col_sum(up(bg)))
        yield
        branch=mm(mixed,w_ref[21])+row(11)
        pg=mm_nt(mg,v)
        act_ref[i]=((mid+branch)*half_root).astype(BF)
        yield
        sg=(a*(pg-jnp.sum(a*pg,axis=1,keepdims=True))).astype(BF)
        acc[21]+=mm_tn(mixed,bg)
        vg=mm_tn(low,mg).astype(BF)
        yield
        qg=(mm(sg,k)*scale).astype(BF)
        kg=(mm_tn(sg,q)*scale).astype(BF)
        yield
        ng=mm_nt(qg,w_ref[18])+mm_nt(kg,w_ref[19])+mm_nt(vg,w_ref[20])
        yield
        normed_t=normed.T
        acc[18]+=mm(normed_t,qg)
        acc[19]+=mm(normed_t,kg)
        acc[20]+=mm(normed_t,vg)
        add(9,col_sum(up(qg)));add(10,col_sum(up(vg)))
        yield
        d,gg,gs=yield from norm_back(ng,h2,r2,row(2))
        add(2,gg);add(5,gs)
        midg=cot+d
        g=up((midg*half_root).astype(BF))
        add(8,col_sum(g))
        spread(s2,i,g,side)
        yield
        ag=yield from back(s2,i,9)
        d=swish_back(ag,h1,row(1),row(4))
        yield
        yield from wgrad(9,p2,s2,i)
        d,gg,gs=yield from norm_back(d,h1,r1,row(1))
        add(1,gg);add(4,gs)
        g=up(d.astype(BF))
        s=col_sum(g)
        add(6,s)
        pgr=up(s.astype(BF))
        pgrad[pl.ds(step*ib+i,1),:]=pgr
        add(7,pgr)
        spread(s1,i,g,side)
        yield
        ag=yield from back(s1,i,0)
        d=swish_back(ag,h0,row(0),row(3))
        yield
        yield from wgrad(0,p1,s1,i)
        d,gg,gs=yield from norm_back(d,h0,r0,row(0))
        add(0,gg);add(3,gs)
        igrad_ref[i]=midg*half_root+d

    def run(count):
        sums.clear()
        live=[image(i) for i in range(count)]
        while live:
            for g in list(live):
                try: next(g)
                except StopIteration: live.remove(g)
        gvec[0:12]+=jnp.concatenate([sums[j] for j in range(12)],axis=0)
    rest=batch-ib*(-(-batch//ib)-1)
    if rest==ib: run(ib)
    else:
        @pl.when(step<steps-1)
        def _(): run(ib)
        @pl.when(step==steps-1)
        def _(): run(rest)

    @pl.when(step==steps-1)
    def _():
        for m in range(acc.shape[0]):
            gw_ref[m]=acc[m].astype(BF)
        gvec_ref[...]=gvec[...]
        e=emb_ref[...].astype(F32)
        s=sigmoid(e)
        ea=(e*s).astype(BF)
        pg=pgrad[0:batch].astype(BF)
        tgrad_ref[...]=mm_nt(pg,dense_ref[...])*(s*(1.0+e*(1.0-s)))
        gd=mm_tn(ea,pg).astype(BF)
        for o in range(c//16):
            for h in range(2):
                gw_ref[22+h,16*o:16*o+16]=gd[32*o+16*h:32*o+16*h+16]

def train_images(owners,images,cot,embed,w,side,ndev):
    batch,tokens,c=images.shape
    emb=embed.shape[1]
    ib=min(TOGETHER,batch)
    rows=-(-batch//8)*8
    whole=lambda a: pl.BlockSpec(a.shape,lambda s: (0,)*len(a.shape))
    blk=pl.BlockSpec((ib,tokens,c),lambda s:(s,0,0))
    sd=jax.ShapeDtypeStruct
    outs=[sd((batch,tokens,c),BF),sd((batch,tokens,c),F32),sd((batch,emb),F32),sd((MATS+2,c,c),BF),sd((16,c),F32)]
    return pl.pallas_call(functools.partial(train_body,side),grid=(-(-batch//ib),),
        in_specs=[SMEM,blk,blk,whole(embed),whole(w)],
        out_specs=[blk,blk]+[whole(o) for o in outs[2:]]+[SMEM],
        out_shape=outs+[sd((ndev,),jnp.int32)],
        scratch_shapes=[pltpu.VMEM((emb,c),BF),pltpu.VMEM((16,c),F32),pltpu.VMEM((MATS,c,c),F32),pltpu.VMEM((16,c),F32),pltpu.VMEM((rows,c),F32),pltpu.VMEM((rows,c),F32)]
          +[pltpu.VMEM((ib,tokens+2*side,3*c),BF)]*4,
        compiler_params=pltpu.CompilerParams(vmem_limit_bytes=LIMIT),
        name="train_images")(owners,images,cot,embed,w)

def fdot(a,b,ca,cb):
    return lax.dot_general(a,b,(((ca,),(cb,)),((),())),precision=HI,preferred_element_type=F32)
nn=lambda a,b: fdot(a,b,1,0)
nt=lambda a,b: fdot(a,b,1,1)
tn=lambda a,b: fdot(a,b,0,0)

def inverse_factors(blocks, tasks):
    tasks=list(tasks)
    share=-(-len(tasks)//14)
    n=BLK
    lane=lax.broadcasted_iota(jnp.int32,(8,n),1)
    sub=lax.broadcasted_iota(jnp.int32,(8,n),0)
    tables=[[b[8*v:8*v+8] for v in range(n//8)] for b in blocks]
    over_lanes=lambda t,j: jnp.broadcast_to(t[:,j:j+1],(8,n))
    over_rows=lambda t,i: jnp.broadcast_to(t[i:i+1],(8,n))
    for J in range(n//8):
        lo=8*J
        in_block=(lane>=lo)&(lane<lo+8)
        for t in tables:
            cur=t[J]
            cols=[over_lanes(cur,lo+j) for j in range(8)]
            m=[[over_rows(cols[j],i) for j in range(i+1)] for i in range(8)]
            R=[jnp.where(in_block,jnp.where(lane==lo+i,1.0,0.0),over_rows(cur,i)) for i in range(8)]
            r=[None]*8
            l=[[None]*8 for _ in range(8)]
            for k in range(8):
                d=m[k][k]
                r[k]=pl.reciprocal(d,approx=True)
                for i in range(k+1,8):
                    l[i][k]=m[i][k]*r[k]
                for i in range(k+1,8):
                    for j in range(k+1,i+1):
                        m[i][j]=m[i][j]-l[i][k]*m[j][k]
                    R[i]=R[i]-l[i][k]*R[k]
            P=[None]*8
            for k in range(7,-1,-1):
                P[k]=R[k]*r[k]
                for i in range(7,k,-1):
                    P[k]=P[k]-l[i][k]*P[i]
            done=R[0]*lax.rsqrt(m[0][0])
            for i in range(1,8):
                done=jnp.where(sub==i,R[i]*lax.rsqrt(m[i][i]),done)
            t[J]=jnp.where(lane<=lo+sub,done,0.0)
            for v in range(J+1,n//8):
                new=jnp.where(in_block,0.0,t[v])
                for k in range(8):
                    new=new-over_lanes(t[v],lo+k)*P[k]
                t[v]=new
        for _ in range(min(share,len(tasks))): tasks.pop(0)()
    return [jnp.concatenate(t,axis=0) for t in tables]

def at(k,size):
    return pl.ds(pl.multiple_of(k*size,size),size)

def split(x):
    hi=x.astype(BF)
    return hi,(x-hi.astype(F32)).astype(BF)

def bdot(a,b,ca,cb):
    return lax.dot_general(a,b,(((ca,),(cb,)),((),())),preferred_element_type=F32)

def dot3(a,b,ca,cb):
    (ah,al),(bh,bl)=split(a),split(b)
    return bdot(ah,bh,ca,cb)+(bdot(ah,bl,ca,cb)+bdot(al,bh,ca,cb))

def dot2(a,b,ca,cb):
    ah,al=split(a)
    return bdot(ah,b,ca,cb)+bdot(al,b,ca,cb)

def factor_both(a_l, g_l, a_r, g_r):
    tasks=[]
    def renew(a,lo,inv,r,rows):
        def task():
            q=dot3(a[rows,lo:lo+BLK],inv,1,1)
            a[rows,lo:lo+BLK]=q
            if r is not None: a[rows,lo+BLK:]=a[rows,lo+BLK:]-dot3(q,r,1,0)
        return task
    def lower(g,r,start,b):
        def task():
            g[b:b+BLK,b:]=g[b:b+BLK,b:]-tn(r[:,b-start:b-start+BLK],r[:,b-start:])
        return task
    for p in range(g_l.shape[0]//BLK):
        lo,hi=p*BLK,(p+1)*BLK
        live=[(a,g) for a,g in ((a_l,g_l),(a_r,g_r)) if g.shape[0]>lo]
        invs=inverse_factors([g[lo:hi,lo:hi] for _,g in live],tasks)
        tasks=[]
        for (a,g),inv in zip(live,invs):
            n=g.shape[0]
            r=None
            if hi<n:
                r=nn(inv,g[lo:hi,hi:])
                lower(g,r,hi,hi)()
                tasks+=[lower(g,r,hi,b) for b in range(hi+BLK,n,BLK)]
            tasks+=[renew(a,lo,inv,r,slice(k,k+ROWS)) for k in range(0,n,ROWS)]
    for task in tasks: task()

def owned(inv_ref):
    held=inv_ref[lax.axis_index("wide")*lax.axis_size("narrow")+lax.axis_index("narrow")]
    return jnp.where(held<0,0,jnp.where(held==MATS,2,1))

def fetch_grad(kind, q_ref, grad):
    big=grad.shape[0]
    @pl.when(kind==1)
    def _():
        grad[...]=jnp.zeros_like(grad)
        for i in range(big//32):
            grad[16*i:16*i+16]=q_ref[32*i:32*i+16]
    @pl.when(kind==2)
    def _():
        grad[...]=q_ref[...]

def copies(srcs,dsts,sems):
    return [pltpu.make_async_copy(a,b,sems.at[i]) for i,(a,b) in enumerate(zip(srcs,dsts))]

def update_body(inv_ref, q_ref, *refs):
    ins_hbm=refs[0:4]; outs_hbm=refs[4:6]; send_o=refs[6]
    ins=refs[7:11]; outs=refs[11:13]
    grad,update,in_sem,out_sem=refs[13:]
    first,second,left,right=ins
    kind=owned(inv_ref)
    c=right.shape[1]; big=left.shape[1]
    ndev=send_o.shape[0]
    copies_in=copies([h.at[0] for h in ins_hbm],ins,in_sem)
    copies_out=copies(outs,[h.at[0] for h in outs_hbm],out_sem)
    for cp in copies_in: cp.start()
    fetch_grad(kind,q_ref,grad)
    for cp in copies_in: cp.wait()
    @pl.when(kind==0)
    def _():
        for o in outs: o[...]=jnp.zeros_like(o)
        send_o[...]=jnp.zeros_like(send_o)
    @pl.when(kind>0)
    def _():
        L=left[...]; Rb=right[...]
        corr=1.0-0.5**STEP
        turned=dot3(dot2(L,grad[...],0,0),Rb,1,0)
        inside=lax.broadcasted_iota(jnp.int32,(big,c),0)<kind*c
        moment=jnp.where(inside,0.5*first[...]+0.5*turned,0.0)
        sec=jnp.where(inside,0.5*second[...]+0.5*turned*turned,0.0)
        outs[0][...]=moment; outs[1][...]=sec
        direction=moment/corr/(jnp.sqrt(sec/corr)+adam_eps)
        update[...]=dot3(dot3(L,direction,1,0),Rb,1,1)
    for cp in copies_out: cp.start()
    for size,number in ((c,1),(big,2)):
        @pl.when(kind==number)
        def _():
            r=size//ndev
            for d in range(ndev):
                u=update[r*d:r*d+r]
                if r<16: u=jnp.concatenate([u,jnp.zeros((16-r,c),F32)],axis=0)
                send_o[d]=u.astype(BF)
    for cp in copies_out: cp.wait()

def basis_body(inv_ref, q_ref, *refs):
    ins_hbm=refs[0:4]; outs_hbm=refs[4:8]
    ins=refs[8:12]; outs=refs[12:16]
    grad,g_l,g_r,in_sem,out_sem=refs[16:]
    left,right,lstat,rstat=ins
    left_o,right_o,lstat_o,rstat_o=outs
    kind=owned(inv_ref)
    c=right.shape[1]; big=left.shape[1]
    copies_in=copies([h.at[0] for h in ins_hbm],ins,in_sem)
    copies_out=copies(outs,[h.at[0] for h in outs_hbm],out_sem)
    for cp in copies_in: cp.start()
    fetch_grad(kind,q_ref,grad)
    for cp in copies_in: cp.wait()
    @pl.when(kind==0)
    def _():
        for o in outs: o[...]=jnp.zeros_like(o)
        for cp in copies_out: cp.start()
    @pl.when(kind>0)
    def _():
        g=grad[...]
        ls=0.95*lstat[...]+0.05*bdot(g,g,1,1)
        rs=0.95*rstat[...]+0.05*bdot(g,g,0,0)
        lstat_o[...]=ls; rstat_o[...]=rs
        for cp in copies_out[2:]: cp.start()
        ar=dot3(rs,right[...],1,0)
        right_o[...]=ar
        for k in range(0,c,BLK): g_r[k:k+BLK,k:]=tn(ar[:,k:k+BLK],ar[:,k:])
        al=dot3(ls,left[...],1,0)
        left_o[...]=al
        row=lax.broadcasted_iota(jnp.int32,(big,big),0)
        unit=jnp.where((row==lax.broadcasted_iota(jnp.int32,(big,big),1))&(row>=kind*c),1.0,0.0)
        for k in range(0,big,BLK): g_l[k:k+BLK,k:]=tn(al[:,k:k+BLK],al[:,k:])+unit[k:k+BLK,k:]
        factor_both(left_o,g_l,right_o,g_r)
        for cp in copies_out[:2]: cp.start()
    for cp in copies_out: cp.wait()

def owner_call(body,name,inv,q,ins,outs,extra_out,scratch,cost):
    sd=lambda a: jax.ShapeDtypeStruct(a.shape,F32)
    buf=lambda a: pltpu.VMEM(a.shape[1:],F32)
    dma=pltpu.SemaphoreType.DMA
    return pl.pallas_call(body,
        in_specs=[SMEM,VMEM]+[ANY]*len(ins),
        out_specs=[ANY]*len(outs)+[VMEM]*len(extra_out),
        out_shape=[sd(a) for a in outs]+extra_out,
        scratch_shapes=[buf(a) for a in ins]+[buf(a) for a in outs]+scratch+[dma((len(ins),)),dma((len(outs),))],
        compiler_params=pltpu.CompilerParams(vmem_limit_bytes=24<<20),
        cost_estimate=pl.CostEstimate(flops=cost,bytes_accessed=4<<20,transcendentals=0),
        name=name)(inv,q,*ins)

def owner_update(inv,q,first,second,left,right,ndev):
    c=right.shape[1]; big=left.shape[1]
    return owner_call(update_body,"owner_update",inv,q,(first,second,left,right),(first,second),
        [jax.ShapeDtypeStruct((ndev,16,c),BF)],[pltpu.VMEM((big,c),BF),pltpu.VMEM((big,c),F32)],4*10**9)

def owner_basis(inv,q,left,right,lstat,rstat):
    c=right.shape[1]; big=left.shape[1]
    slots=(left,right,lstat,rstat)
    return owner_call(basis_body,"owner_basis",inv,q,slots,slots,[],
        [pltpu.VMEM((big,c),BF),pltpu.VMEM((big,big),F32),pltpu.VMEM((c,c),F32)],3*10**10)

def place():
    w,n=lax.axis_index("wide"),lax.axis_index("narrow")
    return lax.div(w,2),lax.rem(w,2),lax.div(n,2),lax.rem(n,2)

def device(z,y,x,core):
    return (z*2+y,x*2+core)

def chip_of(z,y,x):
    return (z*2+y)*2+x

def greet(partners):
    barrier=pltpu.get_barrier_semaphore()
    count=0
    for dev,cond in partners:
        if cond is None:
            pl.semaphore_signal(barrier,inc=1,device_id=dev,device_id_type=MESH)
            count=count+1
        else:
            @pl.when(cond)
            def _():
                pl.semaphore_signal(barrier,inc=1,device_id=dev,device_id_type=MESH)
            count=count+jnp.where(cond,1,0)
    pl.semaphore_wait(barrier,count)

def remote(src,dst,send,recv,dev):
    return pltpu.make_async_remote_copy(src_ref=src,dst_ref=dst,send_sem=send,recv_sem=recv,device_id=dev,device_id_type=MESH)

GATHER=MATS+4
SHARE=GATHER//2
CUT=(SHARE+1)//2

def gather_body(depth, conv_ref, dense_ref, attn_ref, vec_ref, w_ref, part, vbuf,
                pair_s, pair_r, line_r, own_r, twin_r, up_s, down_s, x_s, y_s, twin_s):
    z,y,x,core=place()
    me=chip_of(z,y,x)
    rank=me*2+core
    c=w_ref.shape[-1]
    twin=device(z,y,x,1-core)
    side_x,side_y=device(z,y,1-x,core),device(z,1-y,x,core)
    above,below=device(z+1,y,x,core),device(z-1,y,x,core)
    greet([(twin,None),(side_x,None),(side_y,None),(below,z>0),(above,z<depth-1)])
    conv=conv_ref.shape[0]
    part[0,0:conv]=conv_ref[...]
    part[0,conv:MATS]=attn_ref[...]
    part[0,MATS]=dense_ref[0:8]
    part[0,MATS+1]=dense_ref[8:16]
    cols,rows_v=vec_ref.shape
    vbuf[...]=jnp.zeros_like(vbuf)
    vbuf[0:cols,0:rows_v]=vec_ref[...]
    turned=vbuf[0:8,0:128].T[0:16]
    vbuf[...]=jnp.zeros_like(vbuf)
    vbuf[:,0:8]=turned
    mine=pltpu.roll(vbuf[...],rank*cols,1)
    part[0,MATS+2]=mine[0:8]
    part[0,MATS+3]=mine[8:16]
    swap=remote(part.at[0],part.at[1],pair_s,pair_r,twin)
    swap.start()
    swap.wait()
    even,odd=core,1-core
    join=lambda a,b: jnp.concatenate([a,b],axis=0).astype(BF)
    def fill(m,value):
        @pl.when(core==m//SHARE)
        def _(): w_ref[m,z,y,x]=value()
    for k in range(2):
        @pl.when(core==k)
        def _():
            for m in range(k*SHARE,min((k+1)*SHARE,MATS)):
                w_ref[m,z,y,x]=join(part[even,m],part[odd,m])
    for h,src in ((0,even),(1,odd)):
        fill(MATS+h,lambda: join(part[src,MATS],part[src,MATS+1]))
    fill(MATS+2,lambda: join(part[0,MATS+2]+part[1,MATS+2],part[0,MATS+3]+part[1,MATS+3]))
    fill(MATS+3,lambda: jnp.zeros((16,c),BF))

    def mats(h,whose=core):
        return pl.ds(SHARE*whose+(0,CUT)[h],(CUT,SHARE-CUT)[h])
    every=pl.ds(SHARE*core,SHARE)
    def same(at,send,recv,dev):
        return remote(w_ref.at[at],w_ref.at[at],send,recv,dev)
    def to_up(zz): return same((every,zz,y,x),up_s.at[zz],line_r.at[zz],above)
    def to_down(zz): return same((every,zz,y,x),down_s.at[zz],line_r.at[zz],below)
    def first(h,zz):
        at=(mats(h),zz,y,x)
        return (same(at,x_s.at[0,zz],own_r.at[0,0,zz],side_x),same(at,y_s.at[0,zz],own_r.at[1,0,zz],side_y))[h]
    def second(h,zz):
        return (same((mats(0),zz,y),y_s.at[1,zz],own_r.at[0,1,zz],side_y),
                same((mats(1),zz,slice(None),x),x_s.at[1,zz],own_r.at[1,1,zz],side_x))[h]
    def line(zz,up,down):
        if up or down:
            same((every,zz,y,x),up_s.at[zz],line_r.at[zz],twin).wait_recv()
        if up is not False:
            @pl.when(z<depth-1)
            def _(): to_up(zz).start()
        if down is not False:
            @pl.when(z>0)
            def _(): to_down(zz).start()
        for h in range(2): first(h,zz).start()
    def sides(zz):
        same((mats(0),zz,y,1-x),x_s.at[0,zz],own_r.at[0,0,zz],side_x).wait_recv()
        second(0,zz).start()
        same((mats(1),zz,1-y,x),y_s.at[0,zz],own_r.at[1,0,zz],side_y).wait_recv()
        second(1,zz).start()
    def both(d,run):
        for zz,up in ((z-d,True),(z+d,False)):
            @pl.when((zz>=0)&(zz<depth))
            def _(): run(zz,up)
    line(z,None,None)
    for d in range(1,depth+1):
        if d<depth:
            both(d,lambda zz,up: line(zz,up,not up))
        if d==1: sides(z)
        else: both(d-1,lambda zz,up: sides(zz))
    for h in range(2):
        for zz in range(depth):
            at=((mats(0),zz,1-y),(mats(1),zz,slice(None),1-x))[h]
            same(at,twin_s.at[h],own_r.at[h,1,zz],twin).wait_recv()
        same((mats(h),),twin_s.at[h],twin_r.at[h],twin).start()
    for h in range(2):
        same((mats(h,1-core),),twin_s.at[h],twin_r.at[h],twin).wait_recv()
    for h in range(2):
        same((mats(h),),twin_s.at[h],twin_r.at[h],twin).wait_send()
        for zz in range(depth):
            first(h,zz).wait_send(); second(h,zz).wait_send()
    for zz in range(depth):
        @pl.when((z<depth-1)&(zz<=z))
        def _(): to_up(zz).wait_send()
        @pl.when((z>0)&(zz>=z))
        def _(): to_down(zz).wait_send()

def gather_weights(conv,dense,attn,vec,depth):
    c=conv.shape[2]
    dma=pltpu.SemaphoreType.DMA
    line=dma((depth,))
    return pl.pallas_call(functools.partial(gather_body,depth),
        out_shape=jax.ShapeDtypeStruct((GATHER,depth,2,2,16,c),BF),
        in_specs=[VMEM]*4,out_specs=VMEM,
        scratch_shapes=[pltpu.VMEM((2,GATHER,8,c),F32),pltpu.VMEM((16,c),F32),dma,dma,line,dma((2,2,depth)),dma((2,)),line,line,
          dma((2,depth)),dma((2,depth)),dma((2,))],
        compiler_params=pltpu.CompilerParams(collective_id=0,has_side_effects=True,vmem_limit_bytes=LIMIT),
        name="gather_weights")(conv,dense,attn,vec).reshape(GATHER,c,c)

REDUCE=MATS+2
HALF=REDUCE//2
PARTS=((0,3,"xyz"),(3,2,"yzx"),(5,1,"zxy"),(6,2,"xyz"),(8,2,"yzx"),(10,2,"zxy"))

def reduce_body(depth, inv_ref, g_ref, v_ref, q_ref, vec_o, acc, core_in, *rest):
    bufs=tuple(zip(*[iter(rest[:3*len(PARTS)])]*3))
    (final, pick, vsend, vrecv, core_s, core_r, ex_s, ex_r, z_s, z_r, twin_s, twin_r, out_s, out_r, v_s, v_r)=rest[3*len(PARTS):]
    z,y,x,core=place()
    me=chip_of(z,y,x)
    chips=depth*4
    twin=device(z,y,x,1-core)
    def of_chip(o):
        return device(lax.div(o,4),lax.rem(lax.div(o,2),2),lax.rem(o,2),core)
    others=[lax.rem(me+k,chips) for k in range(1,chips)]
    greet([(twin,None)]+[(of_chip(o),None) for o in others])
    c=g_ref.shape[2]
    pair=[]
    for i,(m0,n,_) in enumerate(PARTS):
        cp=remote(g_ref.at[pl.ds(HALF*(1-core)+m0,n)],core_in.at[m0:m0+n],core_s.at[i],core_r.at[i],twin)
        cp.start(); pair.append(cp)
    def vec_start(stage,dev):
        cp=remote(vsend.at[stage],vrecv.at[stage],v_s.at[stage],v_r.at[stage],dev)
        cp.start()
        return cp
    def vec_end(stage,cp):
        cp.wait()
        total=vsend[stage]+vrecv[stage]
        if stage<4: vsend[stage+1]=total
        else: vec_o[...]=total
    vsend[0]=v_ref[...]
    vcp=vec_start(0,twin)
    nbr_x,nbr_y=device(z,y,1-x,core),device(z,1-y,x,core)
    started={}
    def where(i,done):
        return ["z" in done and z, "y" in done and y, "x" in done and x]
    def index(m,place):
        return tuple([m]+[slice(None) if p is False else p for p in place])
    def swap_start(i,stage):
        m0,n,order=PARTS[i]
        axis=order[stage]
        at=where(i,order[:stage])
        at["zyx".index(axis)]=1-(x if axis=="x" else y)
        dst=bufs[i][0 if axis=="x" else 1]
        k=0 if axis=="x" else 1
        cp=remote(acc.at[index(slice(m0,m0+n),at)],dst,ex_s.at[i,k],ex_r.at[i,k],nbr_x if axis=="x" else nbr_y)
        cp.start()
        started[i,stage]=cp
    def swap_end(i,stage):
        m0,n,order=PARTS[i]
        axis=order[stage]
        started.pop((i,stage)).wait()
        at=where(i,order[:stage+1])
        src=bufs[i][0 if axis=="x" else 1]
        @pl.loop(0,n)
        def _(m):
            there=index(m0+m,at)
            acc[there]=(acc[there].astype(F32)+src[m].astype(F32)).astype(BF)
    def z_copy(i,stage,k):
        m0,n,order=PARTS[i]
        zz=lax.rem(z+k,depth)
        at=where(i,order[:stage])
        at[0]=zz
        return remote(acc.at[index(slice(m0,m0+n),at)],bufs[i][2].at[z],z_s.at[i,k],z_r.at[i,z],device(zz,y,x,core))
    def z_start(i,stage):
        for k in range(1,depth):
            z_copy(i,stage,k).start()
    def z_end(i,stage):
        m0,n,order=PARTS[i]
        src=bufs[i][2]
        at=where(i,order[:stage+1])
        for k in range(1,depth):
            zz=lax.rem(z+k,depth)
            remote(src.at[zz],src.at[zz],z_s.at[i,k],z_r.at[i,zz],twin).wait_recv()
        @pl.loop(0,n)
        def _(m):
            there=index(m0+m,at)
            total=acc[there].astype(F32)
            for k in range(1,depth):
                total=total+src[lax.rem(z+k,depth),m].astype(F32)
            acc[there]=total.astype(BF)
        for k in range(1,depth):
            z_copy(i,stage,k).wait_send()

    def add_pair(i):
        m0,n,_=PARTS[i]
        pair[i].wait()
        @pl.loop(0,n)
        def _(m):
            s=(g_ref[HALF*core+m0+m].astype(F32)+core_in[m0+m].astype(F32)).astype(BF)
            acc[m0+m]=s.reshape(acc.shape[1:])
    groups=range(0,len(PARTS),3)
    for i in groups:
        add_pair(i+2); z_start(i+2,0)
        add_pair(i); swap_start(i,0)
        add_pair(i+1); swap_start(i+1,0)
    vec_end(0,vcp); vcp=vec_start(1,nbr_x)
    for i in groups:
        swap_end(i,0); swap_start(i,1)
        swap_end(i+1,0); z_start(i+1,1)
        z_end(i+2,0); swap_start(i+2,1)
    vec_end(1,vcp); vcp=vec_start(2,nbr_y)
    for i in groups:
        swap_end(i,1); z_start(i,2)
        swap_end(i+2,1); swap_start(i+2,2)
        z_end(i+1,1); swap_start(i+1,2)
    vec_end(2,vcp); vcp=vec_start(3,device(lax.div(z,2)*2+(1-lax.rem(z,2)),y,x,core))
    for i in groups:
        swap_end(i+2,2)
        swap_end(i+1,2)
        z_end(i,2)
    vec_end(3,vcp); vcp=vec_start(4,device(lax.rem(z+2,4),y,x,core))
    there=pl.ds(HALF*core,HALF)
    for m in range(HALF):
        final[HALF*core+m]=acc[m,z,y,x]
    cp=remote(final.at[there],final.at[there],twin_s,twin_r,twin)
    cp.start(); cp.wait()
    for k in range(chips):
        o=me if k==0 else others[k-1]
        m=jnp.maximum(inv_ref[o*2+core],0)
        pick[k,0]=final[m]
        pick[k,1]=final[REDUCE-1]
        if k:
            remote(pick.at[k],q_ref.at[me],out_s.at[k],out_r.at[me],of_chip(o)).start()
    q_ref[me]=pick[0]
    vec_end(4,vcp)
    for k in range(1,chips):
        o=others[k-1]
        remote(pick.at[k],q_ref.at[o],out_s.at[k],out_r.at[o],of_chip(o)).wait()

def reduce_grads(inv,grads,vec,depth):
    c=grads.shape[2]
    chips=depth*4
    dma=pltpu.SemaphoreType.DMA
    vm=lambda *s: pltpu.VMEM(s,BF)
    bufs=[]
    for _,n,order in PARTS:
        left={"z":depth,"y":2,"x":2}
        shapes={}
        for axis in order:
            del left[axis]
            shapes[axis]=tuple(left[k] for k in "zyx" if k in left)
        bufs+=[vm(n,*shapes["x"],16,c),vm(n,*shapes["y"],16,c),vm(depth,n,*shapes["z"],16,c)]
    return pl.pallas_call(functools.partial(reduce_body,depth),
        out_shape=[jax.ShapeDtypeStruct((chips,2,16,c),BF),jax.ShapeDtypeStruct(vec.shape,F32)],
        in_specs=[SMEM,VMEM,VMEM],out_specs=[VMEM,VMEM],
        scratch_shapes=[vm(HALF,depth,2,2,16,c),vm(HALF,c,c)]+bufs+[vm(REDUCE,16,c),vm(chips,2,16,c),
          pltpu.VMEM((5,)+vec.shape,F32),pltpu.VMEM((5,)+vec.shape,F32),
          dma((len(PARTS),)),dma((len(PARTS),)),dma((len(PARTS),2)),dma((len(PARTS),2)),dma((len(PARTS),depth)),dma((len(PARTS),depth)),dma,dma,
          dma((chips,)),dma((chips,)),dma((5,)),dma((5,))],
        compiler_params=pltpu.CompilerParams(collective_id=1,has_side_effects=True,vmem_limit_bytes=18<<20),
        name="reduce_grads")(inv,grads,vec)

def deal_body(ndev, send_ref, out_ref, s_sem, r_sem):
    w,n=lax.axis_index("wide"),lax.axis_index("narrow")
    width=lax.axis_size("narrow")
    me=w*width+n
    dev=lambda d: (lax.div(d,width),lax.rem(d,width))
    others=[lax.rem(me+k,ndev) for k in range(1,ndev)]
    greet([(dev(d),None) for d in others])
    def copy(k):
        d=others[k]
        return remote(send_ref.at[d],out_ref.at[me],s_sem.at[k],r_sem.at[me],dev(d))
    for k in range(ndev-1): copy(k).start()
    out_ref[me]=send_ref[me]
    for k in range(ndev-1):
        d=others[k]
        remote(send_ref.at[d],out_ref.at[d],s_sem.at[k],r_sem.at[d],dev(d)).wait()

def deal_updates(send):
    ndev=send.shape[0]
    dma=pltpu.SemaphoreType.DMA
    return pl.pallas_call(functools.partial(deal_body,ndev),
        out_shape=jax.ShapeDtypeStruct(send.shape,send.dtype),
        in_specs=[VMEM],out_specs=VMEM,
        scratch_shapes=[dma((ndev,)),dma((ndev,))],
        compiler_params=pltpu.CompilerParams(collective_id=2,has_side_effects=True,vmem_limit_bytes=4<<20),
        name="deal_updates")(send)

def weights_body(owners_ref, upd_ref, conv_ref, dense_ref, attn_ref, vm_ref, v1_ref, v2_ref, gv_ref,
                 conv_o, dense_o, attn_o, vec_o, convc_o, densec_o, attnc_o, vecc_o, v1_o, v2_o):
    me=lax.axis_index("wide")*lax.axis_size("narrow")+lax.axis_index("narrow")
    c=dense_ref.shape[1]
    def new(master,number,fan):
        u=upd_ref[owners_ref[number]].astype(F32)[0:master.shape[0]]
        return master-fan**-0.5*(u+0.01*master)
    for k in range(conv_ref.shape[0]):
        v=new(conv_ref[k],k+(k>=9),9*c)
        conv_o[k]=v; convc_o[k]=v.astype(BF)
    v=new(dense_ref[...],9,dense_ref.shape[0]*lax.axis_size("wide")*lax.axis_size("narrow"))
    dense_o[...]=v; densec_o[...]=v.astype(BF)
    for k in range(4):
        v=new(attn_ref[k],19+k,c)
        attn_o[k]=v; attnc_o[k]=v.astype(BF)
    cols,rows=vm_ref.shape
    g=pltpu.roll(gv_ref[...],lax.rem(c-me*cols,c),1)[:,0:128].T[0:cols,0:rows]
    corr=1.0-0.5**STEP
    f=0.5*v1_ref[...]+0.5*g
    s=0.5*v2_ref[...]+0.5*g*g
    v=vm_ref[...]-0.2*(f/corr)/(jnp.sqrt(s/corr)+adam_eps)
    vec_o[...]=v; vecc_o[...]=v.astype(BF)
    v1_o[...]=f; v2_o[...]=s

def new_weights(owners,upd,conv,dense,attn,vm,v1,v2,gvec):
    sd=jax.ShapeDtypeStruct
    mains=(conv,dense,attn,vm)
    return pl.pallas_call(weights_body,
        out_shape=[sd(a.shape,F32) for a in mains]+[sd(a.shape,BF) for a in mains]+[sd(v1.shape,F32)]*2,
        in_specs=[SMEM]+[VMEM]*8,out_specs=[VMEM]*10,
        compiler_params=pltpu.CompilerParams(vmem_limit_bytes=4<<20),
        name="new_weights")(owners,upd,conv,dense,attn,vm,v1,v2,gvec)

def step(depth, images, time_embed, out_cotangent, conv_master, dense_master, attn_master, vector_master, vector_first, vector_second,
         owners, slot_first, slot_second, slot_left_basis, slot_right_basis, slot_left_stat, slot_right_stat):
    batch,side,_,c=images.shape
    ndev=lax.axis_size("wide")*lax.axis_size("narrow")
    flat=lambda a: a.reshape(batch,side*side,c)
    conv=conv_master.reshape((-1,)+conv_master.shape[2:])
    vector,vector_first,vector_second=vector_master.T,vector_first.T,vector_second.T
    if depth:
        w=gather_weights(conv,dense_master,attn_master,vector,depth)
    else:
        gather=lambda a,axis: lax.all_gather(a.astype(BF),AXES,axis=axis,tiled=True)
        dense=jnp.swapaxes(gather(dense_master,0).reshape(c//16,2,16,c),0,1).reshape(2,c,c)
        vec=jnp.pad(gather(vector_master,1),((0,c-vector_master.shape[0]),(0,0)))
        w=jnp.concatenate([gather(conv,1),gather(attn_master,1),dense,vec[None],jnp.zeros((1,c,c),BF)])
    act,igrad,tgrad,grads,gvec,inv=train_images(owners,flat(images),flat(out_cotangent),time_embed,w,side,ndev)
    if depth:
        q,gvec=reduce_grads(inv,grads,gvec,depth)
        q=q.reshape(-1,c)
    else:
        total=lax.optimization_barrier(lax.psum(grads.astype(F32),AXES)).astype(BF)
        gvec=lax.psum(gvec,AXES)
        held=inv[lax.axis_index(AXES)]
        q=jnp.stack([total[jnp.maximum(held,0)].reshape(c//16,16,c),total[MATS+1].reshape(c//16,16,c)],axis=1).reshape(-1,c)
    first_slot,second_slot,send=owner_update(inv,q,slot_first,slot_second,slot_left_basis,slot_right_basis,ndev)
    upd=deal_updates(send) if depth and DEAL else lax.all_to_all(send,AXES,0,0,tiled=True)
    slots=[first_slot,second_slot]+list(owner_basis(inv,q,slot_left_basis,slot_right_basis,slot_left_stat,slot_right_stat))
    new=new_weights(owners,upd,conv,dense_master,attn_master,vector,vector_first,vector_second,gvec)
    conv_new,dense_new,attn_new,vec_new,conv_copy,dense_copy,attn_copy,vec_copy,first_new,second_new=new
    return (act.reshape(images.shape),igrad.reshape(images.shape),tgrad,conv_new.reshape(conv_master.shape),dense_new,attn_new,vec_new.T,
            conv_copy.reshape(conv_master.shape),dense_copy,attn_copy,vec_copy.T,first_new.T,second_new.T,*slots)

def solution(mesh):
    rows,both=P(AXES),P(None,AXES)
    taps=P(None,None,AXES)
    depth=4 if (mesh.shape["wide"],mesh.shape["narrow"])==(8,4) else 0
    return jax.shard_map(functools.partial(step,depth),mesh=mesh,
        in_specs=(rows,rows,rows,taps,rows,both,both,both,both,P())+(rows,)*6,
        out_specs=(rows,rows,rows,taps,rows,both,both,taps,rows,both,both,both,both)+(rows,)*6,
        check_vma=False)
```
